32 devices in a mesh: dp: 16 (over z, y, x), mp: 2 (over core).
Axes of the slice: x: 2, y: 2, z: 4, core: 2. Of those that a mesh axis runs over, the one named last changes fastest.
Arguments:
- tokens: bfloat16 [256, 128, 768], P(('dp', 'mp')), may hold values from -6 to 6
- cotangent: bfloat16 [256, 128, 768], P(('dp', 'mp')), may hold values from -6 to 6
- lengths: int32 [256], P(('dp', 'mp')), may hold values from 2 to 128, as said below
- token_types: int32 [256, 128], P(('dp', 'mp')), may hold values from 0 to 1, as said below
- node_pairs: int32 [256, 128, 2], P(('dp', 'mp')), may hold values from 0 to 63, as said below
- laplacian: float32 [256, 64, 16], P(('dp', 'mp')), may hold values from -4 to 4
- qkv_weight: bfloat16 [768, 3, 768], P(None, None, 'mp'), may hold values from -0.21875 to 0.21875
- out_weight: bfloat16 [768, 768], P('mp'), may hold values from -1.75 to 1.75
- up_weight: bfloat16 [768, 768], P(None, 'mp'), may hold values from -0.21875 to 0.21875
- down_weight: bfloat16 [768, 768], P('mp'), may hold values from -0.21875 to 0.21875
- qkv_master: float32 [768, 3, 768], P('dp', None, 'mp'), may hold values from -0.21875 to 0.21875
- qkv_mean: float32 [768, 3, 768], P('dp', None, 'mp'), may hold values from -0.0008544922 to 0.0008544922
- qkv_square: float32 [768, 3, 768], P('dp', None, 'mp'), may hold values from 7.2867343e-09 to 1.1770878e-07
- out_master: float32 [768, 768], P(('mp', 'dp')), may hold values from -0.21875 to 0.21875
- out_mean: float32 [768, 768], P(('mp', 'dp')), may hold values from -0.00036621094 to 0.00036621094
- out_square: float32 [768, 768], P(('mp', 'dp')), may hold values from 7.286734e-10 to 1.17708785e-08
- up_master: float32 [768, 768], P('dp', 'mp'), may hold values from -0.21875 to 0.21875
- up_mean: float32 [768, 768], P('dp', 'mp'), may hold values from -0.0008544922 to 0.0008544922
- up_square: float32 [768, 768], P('dp', 'mp'), may hold values from 7.2867343e-09 to 1.1770878e-07
- down_master: float32 [768, 768], P(('mp', 'dp')), may hold values from -0.21875 to 0.21875
- down_mean: float32 [768, 768], P(('mp', 'dp')), may hold values from -0.00036621094 to 0.00036621094
- down_square: float32 [768, 768], P(('mp', 'dp')), may hold values from 7.286734e-10 to 1.17708785e-08
- norm_params: float32 [4, 768], replicated, may hold values from -1.2 to 3.3, as said below
- norm_mean: float32 [4, 768], P(None, ('dp', 'mp')), may hold values from -0.0034179688 to 0.0034179688
- norm_square: float32 [4, 768], P(None, ('dp', 'mp')), may hold values from 1.1770878e-07 to 1.8777354e-06
- embed_weight: float32 [34, 768], replicated, may hold values from -1 to 1
- embed_mean: float32 [34, 768], P(None, ('dp', 'mp')), may hold values from -0.0034179688 to 0.0034179688
- embed_square: float32 [34, 768], P(None, ('dp', 'mp')), may hold values from 1.1770878e-07 to 1.8777354e-06
Outputs:
- output: bfloat16 [256, 128, 768], P(('dp', 'mp'))
- input_grad: float32 [256, 128, 768], P(('dp', 'mp'))
- clip_norm: float32 [], replicated
- qkv_updated: float32 [768, 3, 768], P('dp', None, 'mp')
- qkv_newmean: float32 [768, 3, 768], P('dp', None, 'mp')
- qkv_newsquare: float32 [768, 3, 768], P('dp', None, 'mp')
- out_updated: float32 [768, 768], P(('mp', 'dp'))
- out_newmean: float32 [768, 768], P(('mp', 'dp'))
- out_newsquare: float32 [768, 768], P(('mp', 'dp'))
- up_updated: float32 [768, 768], P('dp', 'mp')
- up_newmean: float32 [768, 768], P('dp', 'mp')
- up_newsquare: float32 [768, 768], P('dp', 'mp')
- down_updated: float32 [768, 768], P(('mp', 'dp'))
- down_newmean: float32 [768, 768], P(('mp', 'dp'))
- down_newsquare: float32 [768, 768], P(('mp', 'dp'))
- norm_updated: float32 [4, 768], P(None, ('dp', 'mp'))
- norm_newmean: float32 [4, 768], P(None, ('dp', 'mp'))
- norm_newsquare: float32 [4, 768], P(None, ('dp', 'mp'))
- embed_updated: float32 [34, 768], P(None, ('dp', 'mp'))
- embed_newmean: float32 [34, 768], P(None, ('dp', 'mp'))
- embed_newsquare: float32 [34, 768], P(None, ('dp', 'mp'))
The draws below stay inside these ranges and needn't reach their ends.
Inputs may be any that keep to these rules, and one draw needn't show every extreme that they name: A molecule's tokens fill its first lengths[m] slots; some molecule has exactly 128. `token_types`: 0 for a node token, 1 for an edge token; within a molecule's length the node tokens come first; slots beyond the length hold 0. `node_pairs`: A node token's pair is its own slot twice; an edge token's entries are below its molecule's number of node tokens, which is at most 64; slots beyond the length hold 0. `norm_params`: rows 0 and 2 hold the two norms' gains, rows 1 and 3 their shifts.
All inputs are finite; a program needn't handle non-finite values.
Results may differ from the reference program's by a relative error of at most 0.014.
The reference program's roundings to bfloat16 on the way count: a program that leaves them out, or rounds other values in their place, can miss the bound.
Values may be sent and summed in bfloat16 or wider, within the bound.
No kernel may reach another device: no remote copies, remote signals or barrier semaphores. Data moves between devices by JAX's collectives and lax.ppermute only.
A program may use at most 192 MiB of HBM per device.

```python
import math
import jax
import jax.numpy as jnp
from jax import lax

D = 768
HEADS = 32
HEAD_DIM = 24
FF = 768
LAP = 16
SEQ = 128
STEP = 10
NMAX = 64
ID = 34
MOLECULES = 256


def molecule_layout(key):
    length_key, node_key, pair_key = jax.random.split(jax.random.fold_in(key, 7), 3)
    molecule_index = jnp.arange(MOLECULES, dtype=jnp.int32)
    ceiling = SEQ // 3 + (SEQ - SEQ // 3) * molecule_index // max(MOLECULES - 1, 1)
    floor_len = jnp.maximum(ceiling // 2, 2)
    lengths = jax.random.randint(length_key, (MOLECULES,), floor_len, ceiling + 1)
    lengths = jnp.where(molecule_index == MOLECULES - 1, SEQ, lengths)
    node_top = jnp.minimum(lengths, NMAX)
    node_low = jnp.maximum(lengths // 3, 1)
    node_count = jax.random.randint(node_key, (MOLECULES,), node_low, node_top + 1)
    node_count = jnp.where(molecule_index == MOLECULES - 1, NMAX, node_count)
    position = jnp.arange(SEQ, dtype=jnp.int32)[None, :]
    is_edge = (position >= node_count[:, None]) & (position < lengths[:, None])
    token_types = is_edge.astype(jnp.int32)
    edge_ends = jax.random.randint(pair_key, (MOLECULES, SEQ, 2), 0, node_count[:, None, None])
    self_pair = jnp.where(position < node_count[:, None], position, 0)
    pair_rows = jnp.where(is_edge[:, :, None], edge_ends, self_pair[:, :, None])
    return (lengths, token_types, pair_rows.astype(jnp.int32))


def draw_lengths(key, part):
    return molecule_layout(key)[0]


def draw_token_types(key, part):
    return molecule_layout(key)[1]


def draw_node_pairs(key, part):
    return molecule_layout(key)[2]


def draw_norm_params(key, part):
    gain_key, shift_key = jax.random.split(jax.random.fold_in(key, 11))
    ramp = jnp.arange(D, dtype=jnp.float32) / D
    gains = (0.6 + 1.2 * ramp) * jax.random.uniform(gain_key, (2, D), jnp.float32, 0.8, 1.2)
    shifts = 0.3 * jnp.clip(jax.random.normal(shift_key, (2, D), jnp.float32), -4.0, 4.0)
    return jnp.stack([gains[0], shifts[0], gains[1], shifts[1]])


def steps_of(own_key, dims, pieces, smallest, top_value):
    def one(dim, blocks):
        draws = jax.random.uniform(jax.random.fold_in(jax.random.fold_in(own_key, 6), dim), (blocks,), jnp.float32, smallest / len(pieces), top_value / len(pieces))
        return jnp.repeat(jnp.exp(draws), dims[dim] // blocks).reshape((-1,) + (1,) * (len(dims) - dim - 1))

    loudness = one(*pieces[0])
    for cut in pieces[1:]:
        loudness = loudness * one(*cut)
    return loudness


def noise(rng, dims, deviation, limit, shards=(), held_as=jnp.bfloat16):
    loudness = steps_of(rng, dims, shards, -0.22, 0.18) if shards else 1.0
    entries = jax.random.normal(rng, dims, jnp.float32) * deviation * loudness
    return jnp.minimum(jnp.maximum(entries, -limit), limit).astype(held_as)


def setup_inputs(seed: int = 0) -> dict:
    key_list = jax.random.split(jax.random.key(seed), 29)
    return {
        "tokens": noise(key_list[0], (MOLECULES, SEQ, D), 1.0, 6.0, ((0, 32),)),
        "cotangent": noise(key_list[1], (MOLECULES, SEQ, D), 1.0, 6.0, ((0, 32),)),
        "lengths": draw_lengths(jax.random.fold_in(key_list[28], 71), 0),
        "token_types": draw_token_types(jax.random.fold_in(key_list[28], 71), 0),
        "node_pairs": draw_node_pairs(jax.random.fold_in(key_list[28], 71), 0),
        "laplacian": noise(key_list[5], (MOLECULES, NMAX, LAP), 1.0, 4.0, ((0, 32),), jnp.float32),
        "qkv_weight": noise(key_list[6], (D, 3, D), D ** -0.5, 0.21875, ((2, 2),)),
        "out_weight": noise(key_list[7], (D, D), (D // 64) ** -0.5, 1.75, ((0, 2),)),
        "up_weight": noise(key_list[8], (D, FF), D ** -0.5, 0.21875, ((1, 2),)),
        "down_weight": noise(key_list[9], (FF, D), FF ** -0.5, 0.21875, ((0, 2),)),
        "qkv_master": noise(key_list[10], (D, 3, D), D ** -0.5, 0.21875, ((0, 16), (2, 2)), jnp.float32),
        "qkv_mean": noise(key_list[11], (D, 3, D), (0.11 / (4 * D * D + 2 * D * FF + (4 + ID) * D) ** 0.5), 0.0008544922, ((0, 16), (2, 2)), jnp.float32),
        "qkv_square": jnp.clip(jnp.exp(math.log(1.1770877961225779e-07) - 2.7821581 * jax.random.uniform(key_list[12], (D, 3, D), jnp.float32) ** steps_of(key_list[12], (D, 3, D), ((0, 16), (2, 2)), -0.2, 0.2)), 7.286734327038857e-09, 1.1770877961225779e-07),
        "out_master": noise(key_list[13], (D, D), D ** -0.5, 0.21875, ((0, 32),), jnp.float32),
        "out_mean": noise(key_list[14], (D, D), (0.045 / (4 * D * D + 2 * D * FF + (4 + ID) * D) ** 0.5), 0.00036621094, ((0, 32),), jnp.float32),
        "out_square": jnp.clip(jnp.exp(math.log(1.177087849413283e-08) - 2.7821582 * jax.random.uniform(key_list[15], (D, D), jnp.float32) ** steps_of(key_list[15], (D, D), ((0, 32),), -0.2, 0.2)), 7.28673399397195e-10, 1.177087849413283e-08),
        "up_master": noise(key_list[16], (D, FF), D ** -0.5, 0.21875, ((0, 16), (1, 2)), jnp.float32),
        "up_mean": noise(key_list[17], (D, FF), (0.11 / (4 * D * D + 2 * D * FF + (4 + ID) * D) ** 0.5), 0.0008544922, ((0, 16), (1, 2)), jnp.float32),
        "up_square": jnp.clip(jnp.exp(math.log(1.1770877961225779e-07) - 2.7821581 * jax.random.uniform(key_list[18], (D, FF), jnp.float32) ** steps_of(key_list[18], (D, FF), ((0, 16), (1, 2)), -0.2, 0.2)), 7.286734327038857e-09, 1.1770877961225779e-07),
        "down_master": noise(key_list[19], (FF, D), FF ** -0.5, 0.21875, ((0, 32),), jnp.float32),
        "down_mean": noise(key_list[20], (FF, D), (0.045 / (4 * D * D + 2 * D * FF + (4 + ID) * D) ** 0.5), 0.00036621094, ((0, 32),), jnp.float32),
        "down_square": jnp.clip(jnp.exp(math.log(1.177087849413283e-08) - 2.7821582 * jax.random.uniform(key_list[21], (FF, D), jnp.float32) ** steps_of(key_list[21], (FF, D), ((0, 32),), -0.2, 0.2)), 7.28673399397195e-10, 1.177087849413283e-08),
        "norm_params": draw_norm_params(jax.random.fold_in(key_list[28], 71), 0),
        "norm_mean": noise(key_list[23], (4, D), (0.44 / (4 * D * D + 2 * D * FF + (4 + ID) * D) ** 0.5), 0.0034179688, ((1, 32),), jnp.float32),
        "norm_square": jnp.clip(jnp.exp(math.log(1.8777353716359357e-06) - 2.769608 * jax.random.uniform(key_list[24], (4, D), jnp.float32) ** steps_of(key_list[24], (4, D), ((1, 32),), -0.2, 0.2)), 1.1770877961225779e-07, 1.8777353716359357e-06),
        "embed_weight": noise(key_list[25], (ID, D), ID ** -0.5, 1.0, (), jnp.float32),
        "embed_mean": noise(key_list[26], (ID, D), (0.44 / (4 * D * D + 2 * D * FF + (4 + ID) * D) ** 0.5), 0.0034179688, ((1, 32),), jnp.float32),
        "embed_square": jnp.clip(jnp.exp(math.log(1.8777353716359357e-06) - 2.769608 * jax.random.uniform(key_list[27], (ID, D), jnp.float32) ** steps_of(key_list[27], (ID, D), ((1, 32),), -0.2, 0.2)), 1.1770877961225779e-07, 1.8777353716359357e-06),
    }


NORM_EPS = 1e-05
BETA_FIRST = 0.9
BETA_SECOND = 0.95
ADAM_EPS = 1e-08
MATRIX_RATE = 0.03
NORM_RATE = 0.5
EMBED_RATE = 0.05
MATRIX_DECAY = 0.1
CLIP_LIMIT = 1.0
MASK_VALUE = -1e+30
PRECISE = lax.Precision.HIGHEST

@jax.custom_vjp
def low(v):
    return lax.optimization_barrier(v.astype(jnp.bfloat16)).astype(jnp.float32)

@jax.custom_vjp
def low_back(v):
    return v

def low_keep(v):
    return (low(v), None)

def low_pass(kept, grad):
    return (grad,)

def back_keep(v):
    return (v, None)

def back_low(kept, grad):
    return (low(grad),)
low.defvjp(low_keep, low_pass)
low_back.defvjp(back_keep, back_low)

def layer_norm(values, gain_row, shift_row):
    centred = values - lax.optimization_barrier(jnp.mean(values, axis=-1, keepdims=True))
    spread = lax.optimization_barrier(jnp.mean(centred * centred, axis=-1, keepdims=True))
    return centred * lax.rsqrt(spread + NORM_EPS) * gain_row + shift_row

def token_features(token_types, node_pairs, laplacian):
    node_iota = jnp.arange(laplacian.shape[1], dtype=jnp.int32)
    left_pick = (node_pairs[:, :, 0:1] == node_iota).astype(jnp.float32)
    right_pick = (node_pairs[:, :, 1:2] == node_iota).astype(jnp.float32)
    left_ident = jnp.einsum('msn,mnl->msl', left_pick, laplacian, precision=PRECISE)
    right_ident = jnp.einsum('msn,mnl->msl', right_pick, laplacian, precision=PRECISE)
    type_pick = (token_types[:, :, None] == jnp.arange(2, dtype=jnp.int32)).astype(jnp.float32)
    return jnp.concatenate([left_ident, right_ident, type_pick], axis=-1)

def block_forward(tokens_f, qkv_w, out_w, up_w, down_w, norm_p, embed_w, features, key_mask):
    mol_count, slot_count, width = tokens_f.shape
    score_scale = 1.0 / math.sqrt(HEAD_DIM)
    hidden0 = tokens_f + jnp.einsum('msi,id->msd', features, embed_w, precision=PRECISE)
    normed_a = low(layer_norm(hidden0, norm_p[0], norm_p[1]))
    projected = jnp.einsum('msd,dce->cmse', normed_a, qkv_w, precision=PRECISE)
    projected = low_back(low(projected))
    head_view = projected.reshape(3, mol_count, slot_count, HEADS, HEAD_DIM)
    raw_scores = low_back(jnp.einsum('mqhe,mkhe->mhqk', head_view[0], head_view[1], precision=PRECISE))
    scaled = jnp.where(key_mask[:, None, None, :], raw_scores * score_scale, MASK_VALUE)
    top_score = lax.optimization_barrier(jnp.max(scaled, axis=-1, keepdims=True))
    expd = jnp.exp(scaled - top_score)
    probs = expd / lax.optimization_barrier(jnp.sum(expd, axis=-1, keepdims=True))
    probs_low = low(probs)
    mixed = jnp.einsum('mhqk,mkhe->mqhe', probs_low, head_view[2], precision=PRECISE)
    mixed = low_back(low(mixed)).reshape(mol_count, slot_count, width)
    attn = low_back(jnp.einsum('msf,fd->msd', mixed, out_w, precision=PRECISE))
    hidden1 = hidden0 + attn
    normed_b = low(layer_norm(hidden1, norm_p[2], norm_p[3]))
    pre_act = low_back(jnp.einsum('msd,df->msf', normed_b, up_w, precision=PRECISE))
    activ = low(jax.nn.gelu(pre_act, approximate=False))
    ffn = low_back(jnp.einsum('msf,fd->msd', activ, down_w, precision=PRECISE))
    return hidden1 + ffn

def adam_step(master, mean_old, square_old, gradient, rate, decay, clip_scale):
    clipped = gradient * clip_scale
    mean_new = BETA_FIRST * mean_old + (1.0 - BETA_FIRST) * clipped
    square_new = BETA_SECOND * square_old + (1.0 - BETA_SECOND) * clipped * clipped
    mean_hat = mean_new / (1.0 - BETA_FIRST ** STEP)
    square_hat = square_new / (1.0 - BETA_SECOND ** STEP)
    updated = master - rate * (mean_hat / (jnp.sqrt(square_hat) + ADAM_EPS) + decay * master)
    return (updated, mean_new, square_new)

def reference(tokens, cotangent, lengths, token_types, node_pairs, laplacian, qkv_weight, out_weight, up_weight, down_weight, qkv_master, qkv_mean, qkv_square, out_master, out_mean, out_square, up_master, up_mean, up_square, down_master, down_mean, down_square, norm_params, norm_mean, norm_square, embed_weight, embed_mean, embed_square):
    group_size = math.gcd(MOLECULES, max(1, 4096 // SEQ))
    group_count = MOLECULES // group_size

    def regroup(array):
        return array.reshape((group_count, group_size) + array.shape[1:])
    qkv_f = qkv_weight.astype(jnp.float32)
    out_f = out_weight.astype(jnp.float32)
    up_f = up_weight.astype(jnp.float32)
    down_f = down_weight.astype(jnp.float32)

    def one_group(carry, group_args):
        tok_group, cot_group, len_group, type_group, pair_group, lap_group = group_args
        features = token_features(type_group, pair_group, lap_group)
        key_mask = jnp.arange(SEQ, dtype=jnp.int32)[None, :] < len_group[:, None]

        def closed(tok_f, qkv_w, out_w, up_w, down_w, norm_p, embed_w):
            return block_forward(tok_f, qkv_w, out_w, up_w, down_w, norm_p, embed_w, features, key_mask)
        result, pullback = jax.vjp(closed, tok_group.astype(jnp.float32), qkv_f, out_f, up_f, down_f, norm_params, embed_weight)
        grads = pullback(cot_group.astype(jnp.float32))
        new_carry = tuple((total + piece for total, piece in zip(carry, grads[1:])))
        return (new_carry, (result.astype(jnp.bfloat16), grads[0]))
    start_carry = (jnp.zeros(qkv_f.shape, jnp.float32), jnp.zeros(out_f.shape, jnp.float32), jnp.zeros(up_f.shape, jnp.float32), jnp.zeros(down_f.shape, jnp.float32), jnp.zeros(norm_params.shape, jnp.float32), jnp.zeros(embed_weight.shape, jnp.float32))
    carry, (outputs, input_grads) = lax.scan(one_group, start_carry, (regroup(tokens), regroup(cotangent), regroup(lengths), regroup(token_types), regroup(node_pairs), regroup(laplacian)))
    output = outputs.reshape(MOLECULES, SEQ, D)
    input_grad = input_grads.reshape(MOLECULES, SEQ, D)
    grad_qkv, grad_out, grad_up, grad_down, grad_norm, grad_embed = carry
    total_square = sum((jnp.sum(piece * piece) for piece in carry))
    clip_norm = jnp.sqrt(total_square)
    clip_scale = jnp.minimum(1.0, CLIP_LIMIT / (clip_norm + 1e-06))
    qkv_new = adam_step(qkv_master, qkv_mean, qkv_square, grad_qkv, MATRIX_RATE, MATRIX_DECAY, clip_scale)
    out_new = adam_step(out_master, out_mean, out_square, grad_out, MATRIX_RATE, MATRIX_DECAY, clip_scale)
    up_new = adam_step(up_master, up_mean, up_square, grad_up, MATRIX_RATE, MATRIX_DECAY, clip_scale)
    down_new = adam_step(down_master, down_mean, down_square, grad_down, MATRIX_RATE, MATRIX_DECAY, clip_scale)
    norm_new = adam_step(norm_params, norm_mean, norm_square, grad_norm, NORM_RATE, 0.0, clip_scale)
    embed_new = adam_step(embed_weight, embed_mean, embed_square, grad_embed, EMBED_RATE, 0.0, clip_scale)
    return (output, input_grad, clip_norm, qkv_new[0], qkv_new[1], qkv_new[2], out_new[0], out_new[1], out_new[2], up_new[0], up_new[1], up_new[2], down_new[0], down_new[1], down_new[2], norm_new[0], norm_new[1], norm_new[2], embed_new[0], embed_new[1], embed_new[2])
```

```python
from functools import partial
import math

import jax
import jax.numpy as jnp
from jax import lax
from jax.experimental import pallas as pl
from jax.experimental.pallas import tpu as pltpu
from jax.sharding import PartitionSpec as P

HEAD_DIM = 24
PAD_DIM = 32
STEP = 10
NORM_EPS = 1e-05
BETA_FIRST = 0.9
BETA_SECOND = 0.95
ADAM_EPS = 1e-08
MATRIX_RATE = 0.03
NORM_RATE = 0.5
EMBED_RATE = 0.05
MATRIX_DECAY = 0.1
CLIP_LIMIT = 1.0
MASK_VALUE = -1e30
SCORE_SCALE = 1.0 / math.sqrt(HEAD_DIM)
LOG2E = 1.4426950408889634
LN2 = 0.6931471805599453
IDENT_ROWS = 40
PAIR = 2
VMEM_BYTES = 60 * 1024 * 1024

F32 = jnp.float32
BF16 = jnp.bfloat16


def dot_nn(lhs, rhs):
    return lax.dot_general(lhs, rhs, (((1,), (0,)), ((), ())), preferred_element_type=F32)


def dot_nt(lhs, rhs):
    return lax.dot_general(lhs, rhs, (((1,), (1,)), ((), ())), preferred_element_type=F32)


def norm_parts(values):
    scale = 1.0 / values.shape[0]
    centred = values - jnp.sum(values, axis=0, keepdims=True) * scale
    spread = jnp.sum(centred * centred, axis=0, keepdims=True) * scale
    return centred, lax.rsqrt(spread + NORM_EPS)


def gelu_parts(x):
    size = jnp.abs(x)
    bell = jnp.exp2((-0.5 * LOG2E) * (x * x))
    t = 1.0 / (1.0 + (0.3275911 / math.sqrt(2.0)) * size)
    poly = t * (
        0.5 * 0.254829592
        + t
        * (
            0.5 * -0.284496736
            + t * (0.5 * 1.421413741 + t * (0.5 * -1.453152027 + t * (0.5 * 1.061405429)))
        )
    )
    tail = poly * bell
    share = jnp.where(x < 0.0, tail, 1.0 - tail)
    return x * share, share + x * bell * (1.0 / math.sqrt(2.0 * math.pi))


def head_rows(values, tail):
    heads = values.shape[0] // HEAD_DIM
    cut = values.reshape(heads, HEAD_DIM, values.shape[1])
    tails = jnp.broadcast_to(tail[None], (heads,) + tail.shape)
    return jnp.concatenate([cut, tails], axis=1).reshape(heads * PAD_DIM, values.shape[1])


def block_columns(rows):
    zero = jnp.zeros((PAD_DIM, rows.shape[1]), rows.dtype)
    columns = []
    for head in range(4):
        pieces = [zero] * 4
        pieces[head] = rows[head * PAD_DIM : (head + 1) * PAD_DIM]
        columns.append(jnp.concatenate(pieces, axis=0))
    return jnp.concatenate(columns, axis=1)


def front_kernel(
    len_ref,
    tok_ref,
    cot_ref,
    typ_ref,
    pair_ref,
    lap_ref,
    est_ref,
    norm_ref,
    qkv_o,
    qkv_p,
    out_o,
    out_p,
    up_o,
    up_p,
    down_o,
    down_p,
    output_ref,
    h0_ref,
    gh1_ref,
    na_ref,
    fs_ref,
    q_ref,
    k_ref,
    v_ref,
    do_ref,
    e_ref,
    gown_ref,
    gpeer_ref,
    lnacc_ref,
    qkvt,
    outt,
    upt,
    downt,
    nb,
    act_s,
    cot_s,
    nbt_s,
    gp_s,
    mix_s,
    ga_s,
    mixf,
    h1_s,
    nrm_s,
    dgel_s,
    rec_s,
):
    step = pl.program_id(0)
    steps = pl.num_programs(0)
    slots = tok_ref.shape[1]
    width = tok_ref.shape[2]
    half = width // 2
    halves = ((qkv_o, out_o, up_o, down_o), (qkv_p, out_p, up_p, down_p))

    @pl.when(step == 0)
    def _():
        for h, (qkv, out, up, down) in enumerate(halves):
            for c in range(3):
                qkvt[h, c * half : (c + 1) * half, :] = qkv[c].T
            outt[h] = out[...].T
            upt[h] = up[...].T
            downt[h] = down[...].T
        for row in range(4):
            nb[row] = jnp.broadcast_to(norm_ref[:, row : row + 1], (width, slots))
        lnacc_ref[...] = jnp.zeros_like(lnacc_ref)

    base = pl.multiple_of(step * PAIR * slots, PAIR * slots)
    span = pl.ds(base, PAIR * slots)

    node_iota = lax.broadcasted_iota(jnp.int32, (lap_ref.shape[2], slots), 0)
    row_iota = lax.broadcasted_iota(jnp.int32, (8, slots), 0)
    lane_iota = lax.broadcasted_iota(jnp.int32, (1, slots), 1)

    for j in range(PAIR):
        lanes = slice(j * slots, (j + 1) * slots)
        lap = lap_ref[j]
        lap1 = lap.astype(BF16)
        rest = lap - lap1.astype(F32)
        lap2 = rest.astype(BF16)
        lap3 = (rest - lap2.astype(F32)).astype(BF16)
        laps = jnp.concatenate([lap1.astype(F32), lap2.astype(F32), lap3.astype(F32)], axis=0)
        laps = laps.astype(BF16)
        left = jnp.where(node_iota == pair_ref[j, 0:1, :], 1.0, 0.0).astype(BF16)
        right = jnp.where(node_iota == pair_ref[j, 1:2, :], 1.0, 0.0).astype(BF16)
        lf = dot_nn(laps, left)
        rf = dot_nn(laps, right)
        types = typ_ref[j]
        kinds = jnp.where((row_iota < 2) & (row_iota == types), 1.0, 0.0)
        none = jnp.zeros((8, slots), F32)
        ident = lap.shape[0]
        f1 = jnp.concatenate([lf[0:ident], rf[0:ident], kinds], axis=0)
        f2 = jnp.concatenate([lf[ident : 2 * ident], rf[ident : 2 * ident], none], axis=0)
        f3 = jnp.concatenate([lf[2 * ident :], rf[2 * ident :], none], axis=0)
        stack = jnp.concatenate([f1, f1, f1, f2, f2, f3, none, none], axis=0).astype(BF16)
        fs_ref[:, lanes] = stack
        h0 = tok_ref[j].T.astype(F32) + dot_nn(est_ref[...], stack)
        h0_ref[:, lanes] = h0
        centred, rec = norm_parts(h0)
        na_ref[:, lanes] = (centred * rec * nb[0] + nb[1]).astype(BF16)
        cot_s[:, pl.ds(pl.multiple_of(base + j * slots, slots), slots)] = cot_ref[j].T

    one_row = jnp.where(row_iota == 0, 1.0, 0.0)
    two_rows = jnp.where(row_iota < 2, 1.0, 0.0)
    for h in range(2):
        proj = dot_nn(qkvt[h], na_ref[...])
        rows = slice(h * (half // HEAD_DIM) * PAD_DIM, (h + 1) * (half // HEAD_DIM) * PAD_DIM)
        for j in range(PAIR):
            lanes = slice(j * slots, (j + 1) * slots)
            length = len_ref[step * PAIR + j]
            bias = jnp.where(lane_iota < length, 0.0, MASK_VALUE)
            bias_row = jnp.where(row_iota == 0, bias, 0.0)
            q = proj[0:half, lanes] * (SCORE_SCALE * LOG2E)
            q_ref[j, rows, :] = head_rows(q, one_row).astype(BF16)
            k_ref[j, rows, :] = head_rows(proj[half : 2 * half, lanes], bias_row).astype(BF16)
            v_ref[j, rows, :] = head_rows(proj[2 * half :, lanes], two_rows).astype(BF16)

    groups = width // (4 * HEAD_DIM)
    for j in range(PAIR):
        lanes = slice(j * slots, (j + 1) * slots)

        def attend(g, carry, j=j, lanes=lanes):
            rows = pl.ds(pl.multiple_of(g * 4 * PAD_DIM, 4 * PAD_DIM), 4 * PAD_DIM)
            keys = k_ref[j, rows, :].T
            vals = v_ref[j, rows, :]
            scores = dot_nn(keys, block_columns(q_ref[j, rows, :]))
            mixes, recs = [], []
            for a in range(4):
                own = scores[:, a * slots : (a + 1) * slots]
                top = jnp.max(own, axis=0, keepdims=True)
                ex = jnp.exp2(own - top).astype(BF16)
                e_ref[j, g * 4 + a] = ex
                got = dot_nn(vals[a * PAD_DIM : (a + 1) * PAD_DIM], ex)
                rec = 1.0 / got[HEAD_DIM : HEAD_DIM + 1]
                rec_s[j, g, a : a + 1, :] = rec
                mixes.append(got[0:HEAD_DIM] * rec)
            out_rows = pl.ds(pl.multiple_of(g * 4 * HEAD_DIM, 4 * HEAD_DIM), 4 * HEAD_DIM)
            mixf[out_rows, lanes] = jnp.concatenate(mixes, axis=0)
            return carry

        lax.fori_loop(0, groups, attend, 0)

    mix = mixf[...].astype(BF16)
    mix_s[:, span] = mix
    attn = dot_nn(outt[0], mix[0:half]) + dot_nn(outt[1], mix[half:])
    for j in range(PAIR):
        lanes = slice(j * slots, (j + 1) * slots)
        h1 = h0_ref[:, lanes] + attn[:, lanes]
        h1_s[:, lanes] = h1
        centred, rec = norm_parts(h1)
        unit = centred * rec
        nrm_s[:, lanes] = unit
        rec_s[j, groups, 0:1, :] = rec
        nbt_s[:, pl.ds(pl.multiple_of(base + j * slots, slots), slots)] = (
            unit * nb[2] + nb[3]
        ).astype(BF16)

    for h in range(2):
        rows = slice(h * half, (h + 1) * half)
        act, slope = gelu_parts(dot_nn(upt[h], nbt_s[:, span]))
        act_s[rows, span] = act.astype(BF16)
        dgel_s[rows, :] = slope
    ffn = dot_nn(downt[0], act_s[0:half, span]) + dot_nn(downt[1], act_s[half:, span])
    for j in range(PAIR):
        lanes = slice(j * slots, (j + 1) * slots)
        output_ref[j] = (h1_s[:, lanes] + ffn[:, lanes]).astype(BF16).T

    for h in range(2):
        rows = slice(h * half, (h + 1) * half)
        back = dot_nn(halves[h][3][...], cot_s[:, span])
        gp_s[rows, span] = (back * dgel_s[rows, :]).astype(BF16)
    grad_b = dot_nn(up_o[...], gp_s[0:half, span]) + dot_nn(up_p[...], gp_s[half:, span])
    inv = 1.0 / width
    for j in range(PAIR):
        lanes = slice(j * slots, (j + 1) * slots)
        cols = pl.ds(pl.multiple_of(base + j * slots, slots), slots)
        gb = grad_b[:, lanes]
        unit = nrm_s[:, lanes]
        lnacc_ref[0] += gb * unit
        lnacc_ref[1] += gb
        f = gb * nb[2]
        f_mean = jnp.sum(f, axis=0, keepdims=True) * inv
        fn_mean = jnp.sum(f * unit, axis=0, keepdims=True) * inv
        gh1 = cot_s[:, cols].astype(F32) + rec_s[j, groups, 0:1, :] * (
            f - f_mean - unit * fn_mean
        )
        gh1_ref[:, lanes] = gh1
        ga_s[:, cols] = gh1.astype(BF16)

    for h in range(2):
        gm = dot_nn(halves[h][1][...], ga_s[:, span])
        for j in range(PAIR):
            lanes = slice(j * slots, (j + 1) * slots)
            for g in range(groups // 2):
                at = h * (groups // 2) + g
                grad = gm[g * 96 : (g + 1) * 96, lanes].reshape(4, HEAD_DIM, slots)
                mixed = mixf[at * 96 : (at + 1) * 96, lanes].reshape(4, HEAD_DIM, slots)
                rec = rec_s[j, at].reshape(8, 1, slots)[0:4]
                inner = -(jnp.sum(grad * mixed, axis=1, keepdims=True) * rec)
                high = inner.astype(BF16).astype(F32)
                low = inner - high
                rows8 = lax.broadcasted_iota(jnp.int32, (4, 8, slots), 1)
                tail = jnp.where(rows8 == 0, high, jnp.where(rows8 == 1, low, 0.0))
                full = jnp.concatenate([grad * rec, tail], axis=1)
                do_ref[j, at * 128 : (at + 1) * 128, :] = (
                    full.reshape(4 * PAD_DIM, slots).astype(BF16)
                )

    @pl.when(step == steps - 1)
    def _():
        owners = gown_ref.shape[0]
        some = half // owners
        for h, g_ref in enumerate((gown_ref, gpeer_ref)):
            rows = slice(h * half, (h + 1) * half)
            gdown = dot_nt(act_s[rows, :], cot_s[...])
            gout = dot_nt(mix_s[rows, :], ga_s[...])
            for o in range(owners):
                both = jnp.concatenate(
                    [gdown[o * some : (o + 1) * some], gout[o * some : (o + 1) * some]], axis=0
                )
                g_ref[o, :, 0:width] = both.astype(g_ref.dtype)
            gup = dot_nt(nbt_s[...], gp_s[rows, :])
            g_ref[:, :, width:] = gup.reshape(owners, 2 * some, half).astype(g_ref.dtype)


def middle_kernel(na_ref, q_ref, k_ref, v_ref, do_ref, e_ref, dx_ref, g_ref):
    step = pl.program_id(0)
    steps = pl.num_programs(0)
    slots = q_ref.shape[2]
    half = dx_ref.shape[0] // 3
    base = pl.multiple_of(step * PAIR * slots, PAIR * slots)
    groups = half // (4 * HEAD_DIM)
    for j in range(PAIR):
        cols = pl.ds(pl.multiple_of(base + j * slots, slots), slots)

        def attend(g, carry, j=j, cols=cols):
            rows = pl.ds(pl.multiple_of(g * 4 * PAD_DIM, 4 * PAD_DIM), 4 * PAD_DIM)
            vals = v_ref[j, rows, :].T
            dos = do_ref[j, rows, :]
            qs = q_ref[j, rows, :]
            ks = k_ref[j, rows, :]
            back = dot_nn(vals, block_columns(dos))
            dq, dk, dv = [], [], []
            for a in range(4):
                cut = slice(a * PAD_DIM, (a + 1) * PAD_DIM)
                ex = e_ref[j, g * 4 + a]
                ds = (ex.astype(F32) * back[:, a * slots : (a + 1) * slots]).astype(BF16)
                dq.append(dot_nn(ks[cut], ds)[0:HEAD_DIM])
                dk.append(dot_nt(qs[cut], ds)[0:HEAD_DIM])
                dv.append(dot_nt(dos[cut], ex)[0:HEAD_DIM])
            for c, (parts, scale) in enumerate(((dq, SCORE_SCALE), (dk, LN2), (dv, None))):
                at = pl.ds(pl.multiple_of(c * half + g * 96, 32), 96)
                whole = jnp.concatenate(parts, axis=0)
                if scale is not None:
                    whole = whole * scale
                dx_ref[at, cols] = whole.astype(BF16)
            return carry

        lax.fori_loop(0, groups, attend, 0)

    @pl.when(step == steps - 1)
    def _():
        for c in range(3):
            grad = dot_nt(na_ref[...], dx_ref[c * half : (c + 1) * half, :])
            g_ref[:, :, c * half : (c + 1) * half] = grad.reshape(
                g_ref.shape[0], g_ref.shape[1], half
            ).astype(g_ref.dtype)


def back_kernel(
    dxo_ref, dxp_ref, qkv_o, qkv_p, h0_ref, gh1_ref, fs_ref, gain_ref, ig_ref, lnacc_ref, ge_ref, nb
):
    step = pl.program_id(0)
    slots = ig_ref.shape[1]
    width = ig_ref.shape[2]
    half = width // 2
    inv = 1.0 / width

    @pl.when(step == 0)
    def _():
        lnacc_ref[...] = jnp.zeros_like(lnacc_ref)
        ge_ref[...] = jnp.zeros_like(ge_ref)
        nb[...] = jnp.broadcast_to(gain_ref[:, 0:1], (width, slots))

    total = None
    for qkv, dx in ((qkv_o, dxo_ref), (qkv_p, dxp_ref)):
        for c in range(3):
            part = dot_nn(qkv[c], dx[c * half : (c + 1) * half, :])
            total = part if total is None else total + part
    for j in range(PAIR):
        lanes = slice(j * slots, (j + 1) * slots)
        ga = total[:, lanes]
        centred, rec = norm_parts(h0_ref[:, lanes])
        unit = centred * rec
        lnacc_ref[0] += ga * unit
        lnacc_ref[1] += ga
        f = ga * nb[...]
        f_mean = jnp.sum(f, axis=0, keepdims=True) * inv
        fn_mean = jnp.sum(f * unit, axis=0, keepdims=True) * inv
        ig = gh1_ref[:, lanes] + rec * (f - f_mean - unit * fn_mean)
        ig_ref[j] = ig.T
        high = ig.astype(BF16)
        rest = ig - high.astype(F32)
        low = rest.astype(BF16)
        least = (rest - low.astype(F32)).astype(BF16)
        fs = fs_ref[:, lanes]
        ge_ref[...] += dot_nt(high, fs) + dot_nt(low, fs) + dot_nt(least, fs)


def whole_spec(shape):
    zeros = (0,) * len(shape)
    return pl.BlockSpec(shape, lambda i: zeros, pipeline_mode=pl.Buffered(1))


def front(lengths, tokens, cotangent, token_types, pairs_t, lap_t, est, norm_t, own, peer):
    mols, slots, width = tokens.shape
    half = width // 2
    heads = width // HEAD_DIM
    toks = mols * slots
    steps = mols // PAIR
    owners = 16
    lead = lambda *rest: pl.BlockSpec((PAIR,) + rest, lambda i: (i,) + (0,) * len(rest))
    col = lambda rows: pl.BlockSpec((rows, PAIR * slots), lambda i: (0, i))
    weights = []
    for pair in zip(own, peer):
        weights += list(pair)
    gshape = (owners, 2 * half // owners, 3 * half)
    outs = [
        (jax.ShapeDtypeStruct((mols, slots, width), BF16), lead(slots, width)),
        (jax.ShapeDtypeStruct((width, toks), F32), col(width)),
        (jax.ShapeDtypeStruct((width, toks), F32), col(width)),
        (jax.ShapeDtypeStruct((width, toks), BF16), col(width)),
        (jax.ShapeDtypeStruct((256, toks), BF16), col(256)),
        (jax.ShapeDtypeStruct((mols, heads * PAD_DIM, slots), BF16), lead(heads * PAD_DIM, slots)),
        (jax.ShapeDtypeStruct((mols, heads * PAD_DIM, slots), BF16), lead(heads * PAD_DIM, slots)),
        (jax.ShapeDtypeStruct((mols, heads * PAD_DIM, slots), BF16), lead(heads * PAD_DIM, slots)),
        (jax.ShapeDtypeStruct((mols, heads * PAD_DIM, slots), BF16), lead(heads * PAD_DIM, slots)),
        (jax.ShapeDtypeStruct((mols, heads, slots, slots), BF16), lead(heads, slots, slots)),
        (jax.ShapeDtypeStruct(gshape, F32), whole_spec(gshape)),
        (jax.ShapeDtypeStruct(gshape, BF16), whole_spec(gshape)),
        (jax.ShapeDtypeStruct((2, width, slots), F32), whole_spec((2, width, slots))),
    ]
    return pl.pallas_call(
        front_kernel,
        grid=(steps,),
        out_shape=[o[0] for o in outs],
        out_specs=[o[1] for o in outs],
        in_specs=[
            pl.BlockSpec(memory_space=pltpu.SMEM),
            lead(slots, width),
            lead(slots, width),
            lead(1, slots),
            lead(2, slots),
            lead(lap_t.shape[1], lap_t.shape[2]),
            whole_spec(est.shape),
            whole_spec(norm_t.shape),
        ]
        + [whole_spec(w.shape) for w in weights],
        scratch_shapes=[
            pltpu.VMEM((2, 3 * half, width), BF16),
            pltpu.VMEM((2, width, half), BF16),
            pltpu.VMEM((2, half, width), BF16),
            pltpu.VMEM((2, width, half), BF16),
            pltpu.VMEM((4, width, slots), F32),
        ]
        + [pltpu.VMEM((width, toks), BF16)] * 6
        + [pltpu.VMEM((width, PAIR * slots), F32)] * 4
        + [pltpu.VMEM((PAIR, heads // 4 + 1, 8, slots), F32)],
        compiler_params=pltpu.CompilerParams(vmem_limit_bytes=VMEM_BYTES),
        cost_estimate=pl.CostEstimate(
            flops=2 * toks * width * width * 15, bytes_accessed=50_000_000, transcendentals=0
        ),
        name="front",
    )(
        lengths,
        tokens,
        cotangent,
        token_types.reshape(mols, 1, slots),
        pairs_t,
        lap_t,
        est,
        norm_t,
        *weights,
    )


def middle(which, dtype, na, q, k, v, do, e):
    mols, heads, slots, _ = e.shape
    width, toks = na.shape
    half = width // 2
    rows = heads // 2 * PAD_DIM
    part = pl.BlockSpec((PAIR, rows, slots), lambda i: (i, which, 0))
    gshape = (16, width // 16, 3 * half)
    return pl.pallas_call(
        middle_kernel,
        grid=(mols // PAIR,),
        out_shape=[
            jax.ShapeDtypeStruct((3 * half, toks), BF16),
            jax.ShapeDtypeStruct(gshape, dtype),
        ],
        in_specs=[
            whole_spec(na.shape),
            part,
            part,
            part,
            part,
            pl.BlockSpec((PAIR, heads // 2, slots, slots), lambda i: (i, which, 0, 0)),
        ],
        out_specs=[whole_spec((3 * half, toks)), whole_spec(gshape)],
        compiler_params=pltpu.CompilerParams(vmem_limit_bytes=VMEM_BYTES),
        cost_estimate=pl.CostEstimate(
            flops=2 * toks * width * width * 5, bytes_accessed=12_000_000, transcendentals=0
        ),
        name="middle",
    )(na, q, k, v, do, e)


def back(dxo, dxp, qkv_o, qkv_p, h0, gh1, fs, gain, mols):
    width, toks = h0.shape
    slots = toks // mols
    col = lambda rows: pl.BlockSpec((rows, PAIR * slots), lambda i: (0, i))
    return pl.pallas_call(
        back_kernel,
        grid=(mols // PAIR,),
        out_shape=[
            jax.ShapeDtypeStruct((mols, slots, width), F32),
            jax.ShapeDtypeStruct((2, width, slots), F32),
            jax.ShapeDtypeStruct((width, 256), F32),
        ],
        in_specs=[
            col(dxo.shape[0]),
            col(dxo.shape[0]),
            whole_spec(qkv_o.shape),
            whole_spec(qkv_p.shape),
            col(width),
            col(width),
            col(256),
            whole_spec(gain.shape),
        ],
        out_specs=[
            pl.BlockSpec((PAIR, slots, width), lambda i: (i, 0, 0)),
            whole_spec((2, width, slots)),
            whole_spec((width, 256)),
        ],
        scratch_shapes=[pltpu.VMEM((width, slots), F32)],
        compiler_params=pltpu.CompilerParams(vmem_limit_bytes=VMEM_BYTES),
        cost_estimate=pl.CostEstimate(
            flops=2 * toks * width * width * 4, bytes_accessed=15_000_000, transcendentals=0
        ),
        name="back",
    )(dxo, dxp, qkv_o, qkv_p, h0, gh1, fs, gain)


def swap(value):
    return lax.ppermute(value, "mp", [(0, 1), (1, 0)])


def hop(value, flip):
    size = lax.axis_size("dp")
    return lax.ppermute(value, "dp", [(i, i ^ flip) for i in range(size)])


def take(value, index, axis=0):
    return lax.dynamic_index_in_dim(value, index, axis, keepdims=False)


def exchange(value, mine, count, stride):
    total = take(value, mine).astype(F32)
    for k in range(1, count):
        total = total + hop(take(value, mine ^ k), k * stride).astype(F32)
    return total


def reduce_owned(value):
    index = lax.axis_index("dp")
    plane, line = index & 3, index >> 2
    rows, columns = value.shape[1:]
    cut = columns * 7 // 9 // 128 * 128
    first = value[:, :, :cut].reshape(4, 4, rows, cut).swapaxes(0, 1)
    first = exchange(first, plane, 4, 1).astype(BF16)
    first = exchange(first, line, 4, 4)
    second = value[:, :, cut:].reshape(4, 4, rows, columns - cut)
    second = exchange(second, line, 4, 4).astype(BF16)
    second = exchange(second, plane, 4, 1)
    return jnp.concatenate([first, second], axis=1)


def adam_step(master, mean_old, square_old, gradient, rate, decay, clip_scale):
    clipped = gradient * clip_scale
    mean_new = BETA_FIRST * mean_old + (1.0 - BETA_FIRST) * clipped
    square_new = BETA_SECOND * square_old + (1.0 - BETA_SECOND) * clipped * clipped
    mean_hat = mean_new / (1.0 - BETA_FIRST**STEP)
    square_hat = square_new / (1.0 - BETA_SECOND**STEP)
    updated = master - rate * (mean_hat / (jnp.sqrt(square_hat) + ADAM_EPS) + decay * master)
    return (updated, mean_new, square_new)


def on_device(
    tokens,
    cotangent,
    lengths,
    token_types,
    node_pairs,
    laplacian,
    qkv_weight,
    out_weight,
    up_weight,
    down_weight,
    qkv_master,
    qkv_mean,
    qkv_square,
    out_master,
    out_mean,
    out_square,
    up_master,
    up_mean,
    up_square,
    down_master,
    down_mean,
    down_square,
    norm_params,
    norm_mean,
    norm_square,
    embed_weight,
    embed_mean,
    embed_square,
):
    mols, slots, width = tokens.shape
    half = width // 2
    dp_size = lax.axis_size("dp")
    mp_size = lax.axis_size("mp")
    idents = embed_weight.shape[0]

    own = (qkv_weight.transpose(1, 0, 2), out_weight, up_weight, down_weight)
    peer = tuple(swap(w) for w in own)

    embed_rows = jnp.pad(embed_weight, ((0, IDENT_ROWS - idents), (0, 0)))
    e1 = lax.reduce_precision(embed_rows, 8, 7)
    e2 = lax.reduce_precision(embed_rows - e1, 8, 7)
    e3 = embed_rows - e1 - e2
    blank = jnp.zeros((256 - 6 * IDENT_ROWS, width), F32)
    est = jnp.concatenate([e1, e2, e3, e1, e2, e1, blank], axis=0).astype(BF16).T
    norm_t = norm_params.T

    (output, h0, gh1, na, fs, q, k, v, do, e, gown1, gpeer1, lnacc_b) = front(
        lengths,
        tokens,
        cotangent,
        token_types,
        node_pairs.transpose(0, 2, 1),
        laplacian.transpose(0, 2, 1),
        est,
        norm_t,
        own,
        peer,
    )
    sum1 = gown1 + swap(gpeer1).astype(F32)
    dxp, gpeer2 = middle(1, BF16, na, q, k, v, do, e)
    got2 = swap(gpeer2)
    dxo, gown2 = middle(0, F32, na, q, k, v, do, e)
    sum2 = gown2 + got2.astype(F32)
    input_grad, lnacc_a, gembed = back(
        dxo, dxp, own[0], peer[0], h0, gh1, fs, norm_t, mols
    )

    if dp_size == 16:
        red1 = reduce_owned(sum1.astype(BF16))
        red2 = reduce_owned(sum2.astype(BF16))
        some = half // dp_size
        reduced_down = red1[0:some, 0:width]
        reduced_out = red1[some:, 0:width]
        reduced_up = red1[:, width:]
        reduced_qkv = red2.reshape(2 * some, 3, half)
    else:
        some = half // 16
        scatter = partial(lax.psum_scatter, axis_name="dp", scatter_dimension=0, tiled=True)
        reduced_down = scatter(sum1[:, 0:some, 0:width].reshape(half, width))
        reduced_out = scatter(sum1[:, some:, 0:width].reshape(half, width))
        reduced_up = scatter(sum1[:, :, width:].reshape(width, half))
        reduced_qkv = scatter(sum2.reshape(width, 3, half))

    i1, i2, i3 = 0, 3 * IDENT_ROWS, 5 * IDENT_ROWS
    grad_embed = (
        gembed[:, i1 : i1 + idents] + gembed[:, i2 : i2 + idents] + gembed[:, i3 : i3 + idents]
    )
    small = jnp.concatenate(
        [jnp.sum(lnacc_a, axis=2).T, jnp.sum(lnacc_b, axis=2).T, grad_embed], axis=1
    )
    world = dp_size * mp_size
    shard_width = width // world
    small = small.reshape(world, shard_width, small.shape[1])
    got = lax.all_to_all(small, ("dp", "mp"), 0, 0, tiled=True)
    small_own = jnp.sum(got, axis=0).T
    reduced_norm = small_own[0:4]
    reduced_embed = small_own[4:]

    own_square = (
        jnp.sum(reduced_qkv * reduced_qkv)
        + jnp.sum(reduced_out * reduced_out)
        + jnp.sum(reduced_up * reduced_up)
        + jnp.sum(reduced_down * reduced_down)
        + jnp.sum(small_own * small_own)
    )
    squares = jnp.broadcast_to(own_square, (world, 1))
    total_square = jnp.sum(lax.all_to_all(squares, ("dp", "mp"), 0, 0, tiled=True))
    clip_norm = jnp.sqrt(total_square)
    clip_scale = jnp.minimum(1.0, CLIP_LIMIT / (clip_norm + 1e-06))
    shard_index = lax.axis_index("dp") * mp_size + lax.axis_index("mp")
    norm_own = lax.dynamic_slice_in_dim(norm_params, shard_index * shard_width, shard_width, 1)
    embed_own = lax.dynamic_slice_in_dim(embed_weight, shard_index * shard_width, shard_width, 1)
    qkv_new = adam_step(
        qkv_master, qkv_mean, qkv_square, reduced_qkv, MATRIX_RATE, MATRIX_DECAY, clip_scale
    )
    out_new = adam_step(
        out_master, out_mean, out_square, reduced_out, MATRIX_RATE, MATRIX_DECAY, clip_scale
    )
    up_new = adam_step(
        up_master, up_mean, up_square, reduced_up, MATRIX_RATE, MATRIX_DECAY, clip_scale
    )
    down_new = adam_step(
        down_master, down_mean, down_square, reduced_down, MATRIX_RATE, MATRIX_DECAY, clip_scale
    )
    norm_new = adam_step(norm_own, norm_mean, norm_square, reduced_norm, NORM_RATE, 0.0, clip_scale)
    embed_new = adam_step(
        embed_own, embed_mean, embed_square, reduced_embed, EMBED_RATE, 0.0, clip_scale
    )
    return (output, input_grad, clip_norm) + (
        qkv_new + out_new + up_new + down_new + norm_new + embed_new
    )


def solution(mesh):
    tokens = P(("dp", "mp"), None, None)
    qkv = P("dp", None, "mp")
    rows = P(("mp", "dp"), None)
    both = P("dp", "mp")
    small = P(None, ("dp", "mp"))
    return jax.shard_map(
        on_device,
        mesh=mesh,
        in_specs=(
            tokens,
            tokens,
            P(("dp", "mp")),
            P(("dp", "mp"), None),
            tokens,
            tokens,
            P(None, None, "mp"),
            P("mp", None),
            P(None, "mp"),
            P("mp", None),
        )
        + (qkv,) * 3
        + (rows,) * 3
        + (both,) * 3
        + (rows,) * 3
        + (P(), small, small) * 2,
        out_specs=(tokens, tokens, P())
        + (qkv,) * 3
        + (rows,) * 3
        + (both,) * 3
        + (rows,) * 3
        + (small,) * 6,
        check_vma=False,
    )
```

```python
from functools import partial
import math

import jax
import jax.numpy as jnp
from jax import lax
from jax.experimental import pallas as pl
from jax.experimental.pallas import tpu as pltpu
from jax.sharding import PartitionSpec as P

HEAD_DIM = 24
PAD_DIM = 32
STEP = 10
NORM_EPS = 1e-05
BETA_FIRST = 0.9
BETA_SECOND = 0.95
ADAM_EPS = 1e-08
MATRIX_RATE = 0.03
NORM_RATE = 0.5
EMBED_RATE = 0.05
MATRIX_DECAY = 0.1
CLIP_LIMIT = 1.0
MASK_VALUE = -1e30
SCORE_SCALE = 1.0 / math.sqrt(HEAD_DIM)
LOG2E = 1.4426950408889634
LN2 = 0.6931471805599453
IDENT_ROWS = 40
IDENT_USED = 34
PAIR = 2
VMEM_BYTES = 60 * 1024 * 1024

F32 = jnp.float32
BF16 = jnp.bfloat16


def dot_nn(lhs, rhs):
    return lax.dot_general(lhs, rhs, (((1,), (0,)), ((), ())), preferred_element_type=F32)


def dot_nt(lhs, rhs):
    return lax.dot_general(lhs, rhs, (((1,), (1,)), ((), ())), preferred_element_type=F32)


def norm_parts(values):
    scale = 1.0 / values.shape[0]
    centred = values - jnp.sum(values, axis=0, keepdims=True) * scale
    spread = jnp.sum(centred * centred, axis=0, keepdims=True) * scale
    return centred, lax.rsqrt(spread + NORM_EPS)


def gelu_parts(x):
    size = jnp.abs(x)
    bell = jnp.exp2((-0.5 * LOG2E) * (x * x))
    t = 1.0 / (1.0 + (0.3275911 / math.sqrt(2.0)) * size)
    poly = t * (
        0.5 * 0.254829592
        + t
        * (
            0.5 * -0.284496736
            + t * (0.5 * 1.421413741 + t * (0.5 * -1.453152027 + t * (0.5 * 1.061405429)))
        )
    )
    tail = poly * bell
    share = jnp.where(x < 0.0, tail, 1.0 - tail)
    return x * share, share + x * bell * (1.0 / math.sqrt(2.0 * math.pi))


def head_rows(values, tail):
    heads = values.shape[0] // HEAD_DIM
    cut = values.reshape(heads, HEAD_DIM, values.shape[1])
    tails = jnp.broadcast_to(tail[None], (heads,) + tail.shape)
    return jnp.concatenate([cut, tails], axis=1).reshape(heads * PAD_DIM, values.shape[1])


def block_columns(rows):
    zero = jnp.zeros((PAD_DIM, rows.shape[1]), rows.dtype)
    columns = []
    for head in range(4):
        pieces = [zero] * 4
        pieces[head] = rows[head * PAD_DIM : (head + 1) * PAD_DIM]
        columns.append(jnp.concatenate(pieces, axis=0))
    return jnp.concatenate(columns, axis=1)


def lane_columns(row, slots):
    return jnp.broadcast_to(row, (slots, row.shape[1])).T


def embed_kernel(
    tok_ref,
    cot_ref,
    typ_ref,
    pair_ref,
    lap_ref,
    embed_ref,
    norm_ref,
    h0_ref,
    na_ref,
    fs_ref,
    ct_ref,
    nb,
    rows,
    est,
):
    slots = tok_ref.shape[1]
    width = tok_ref.shape[2]

    @pl.when(pl.program_id(0) == 0)
    def _():
        for row in range(2):
            nb[row] = lane_columns(norm_ref[row : row + 1, :], slots)
        rows[...] = jnp.zeros_like(rows)
        rows[0 : embed_ref.shape[0], :] = embed_ref[...]
        whole = rows[...]
        e1 = whole.astype(BF16).astype(F32)
        e2 = (whole - e1).astype(BF16).astype(F32)
        e3 = whole - e1 - e2
        blank = jnp.zeros((8, width), F32)
        stacked = jnp.concatenate([e1, e2, e3, blank, e1, e2, e1, blank], axis=0)
        est[...] = stacked.T.astype(BF16)

    node_iota = lax.broadcasted_iota(jnp.int32, (lap_ref.shape[2], slots), 0)
    row_iota = lax.broadcasted_iota(jnp.int32, (8, slots), 0)
    for j in range(PAIR):
        lanes = slice(j * slots, (j + 1) * slots)
        lap = lap_ref[j]
        lap1 = lap.astype(BF16)
        rest = lap - lap1.astype(F32)
        lap2 = rest.astype(BF16)
        lap3 = (rest - lap2.astype(F32)).astype(BF16)
        laps = jnp.concatenate([lap1.astype(F32), lap2.astype(F32), lap3.astype(F32)], axis=0)
        laps = laps.astype(BF16)
        left = jnp.where(node_iota == pair_ref[j, 0:1, :], 1.0, 0.0).astype(BF16)
        right = jnp.where(node_iota == pair_ref[j, 1:2, :], 1.0, 0.0).astype(BF16)
        lf = dot_nn(laps, left)
        rf = dot_nn(laps, right)
        types = typ_ref[j]
        kinds = jnp.where((row_iota < 2) & (row_iota == types), 1.0, 0.0)
        none = jnp.zeros((8, slots), F32)
        ident = lap.shape[0]
        f1 = jnp.concatenate([lf[0:ident], rf[0:ident], kinds], axis=0)
        f2 = jnp.concatenate([lf[ident : 2 * ident], rf[ident : 2 * ident], none], axis=0)
        f3 = jnp.concatenate([lf[2 * ident :], rf[2 * ident :], none], axis=0)
        stack = jnp.concatenate([f1, f1, f1, none, f2, f2, f3, none], axis=0).astype(BF16)
        fs_ref[:, lanes] = stack
        h0 = tok_ref[j].T.astype(F32) + dot_nn(est[...], stack)
        h0_ref[:, lanes] = h0
        centred, rec = norm_parts(h0)
        na_ref[:, lanes] = (centred * rec * nb[0] + nb[1]).astype(BF16)
        ct_ref[:, lanes] = cot_ref[j].T


def front_kernel(
    len_ref,
    h0_ref,
    na_ref,
    cot_s,
    norm_ref,
    qkv_o,
    qkv_p,
    out_o,
    out_p,
    up_o,
    up_p,
    down_o,
    down_p,
    output_ref,
    gh1_ref,
    q_ref,
    k_ref,
    v_ref,
    do_ref,
    e_ref,
    gown_ref,
    gpeer_ref,
    lnacc_ref,
    qkvt,
    outt,
    upt,
    downt,
    nb,
    act_s,
    nbt_s,
    gp_s,
    mix_s,
    ga_s,
    mixf,
    h1_s,
    nrm_s,
    dgel_s,
    rec_s,
):
    step = pl.program_id(0)
    steps = pl.num_programs(0)
    slots = output_ref.shape[1]
    width = output_ref.shape[2]
    half = width // 2
    halves = ((qkv_o, out_o, up_o, down_o), (qkv_p, out_p, up_p, down_p))

    @pl.when(step == 0)
    def _():
        for h, (qkv, out, up, down) in enumerate(halves):
            for c in range(3):
                qkvt[h, c * half : (c + 1) * half, :] = qkv[c].T
            outt[h] = out[...].T
            upt[h] = up[...].T
            downt[h] = down[...].T
        for row in range(2):
            nb[row] = lane_columns(norm_ref[row + 2 : row + 3, :], slots)
        lnacc_ref[...] = jnp.zeros_like(lnacc_ref)

    base = pl.multiple_of(step * PAIR * slots, PAIR * slots)
    span = pl.ds(base, PAIR * slots)

    row_iota = lax.broadcasted_iota(jnp.int32, (8, slots), 0)
    lane_iota = lax.broadcasted_iota(jnp.int32, (1, slots), 1)

    one_row = jnp.where(row_iota == 0, 1.0, 0.0)
    two_rows = jnp.where(row_iota < 2, 1.0, 0.0)
    for h in range(2):
        proj = dot_nn(qkvt[h], na_ref[...])
        rows = slice(h * (half // HEAD_DIM) * PAD_DIM, (h + 1) * (half // HEAD_DIM) * PAD_DIM)
        for j in range(PAIR):
            lanes = slice(j * slots, (j + 1) * slots)
            length = len_ref[step * PAIR + j]
            bias = jnp.where(lane_iota < length, 0.0, MASK_VALUE)
            bias_row = jnp.where(row_iota == 0, bias, 0.0)
            q = proj[0:half, lanes] * (SCORE_SCALE * LOG2E)
            q_ref[j, rows, :] = head_rows(q, one_row).astype(BF16)
            k_ref[j, rows, :] = head_rows(proj[half : 2 * half, lanes], bias_row).astype(BF16)
            v_ref[j, rows, :] = head_rows(proj[2 * half :, lanes], two_rows).astype(BF16)

    groups = width // (4 * HEAD_DIM)
    for j in range(PAIR):
        lanes = slice(j * slots, (j + 1) * slots)

        def attend(g, carry, j=j, lanes=lanes):
            rows = pl.ds(pl.multiple_of(g * 4 * PAD_DIM, 4 * PAD_DIM), 4 * PAD_DIM)
            keys = k_ref[j, rows, :].T
            vals = v_ref[j, rows, :]
            scores = dot_nn(keys, block_columns(q_ref[j, rows, :]))
            mixes, recs = [], []
            for a in range(4):
                own = scores[:, a * slots : (a + 1) * slots]
                top = jnp.max(own, axis=0, keepdims=True)
                ex = jnp.exp2(own - top).astype(BF16)
                e_ref[j, g * 4 + a] = ex
                got = dot_nn(vals[a * PAD_DIM : (a + 1) * PAD_DIM], ex)
                rec = 1.0 / got[HEAD_DIM : HEAD_DIM + 1]
                rec_s[j, g, a : a + 1, :] = rec
                mixes.append(got[0:HEAD_DIM] * rec)
            out_rows = pl.ds(pl.multiple_of(g * 4 * HEAD_DIM, 4 * HEAD_DIM), 4 * HEAD_DIM)
            mixf[out_rows, lanes] = jnp.concatenate(mixes, axis=0)
            return carry

        lax.fori_loop(0, groups, attend, 0, unroll=4)

    mix = mixf[...].astype(BF16)
    mix_s[:, span] = mix
    attn = dot_nn(outt[0], mix[0:half]) + dot_nn(outt[1], mix[half:])
    for j in range(PAIR):
        lanes = slice(j * slots, (j + 1) * slots)
        h1 = h0_ref[:, lanes] + attn[:, lanes]
        h1_s[:, lanes] = h1
        centred, rec = norm_parts(h1)
        unit = centred * rec
        nrm_s[:, lanes] = unit
        rec_s[j, groups, 0:1, :] = rec
        nbt_s[:, pl.ds(pl.multiple_of(base + j * slots, slots), slots)] = (
            unit * nb[0] + nb[1]
        ).astype(BF16)

    for h in range(2):
        rows = slice(h * half, (h + 1) * half)
        act, slope = gelu_parts(dot_nn(upt[h], nbt_s[:, span]))
        act_s[rows, span] = act.astype(BF16)
        dgel_s[rows, :] = slope
    ffn = dot_nn(downt[0], act_s[0:half, span]) + dot_nn(downt[1], act_s[half:, span])
    for j in range(PAIR):
        lanes = slice(j * slots, (j + 1) * slots)
        output_ref[j] = (h1_s[:, lanes] + ffn[:, lanes]).astype(BF16).T

    for h in range(2):
        rows = slice(h * half, (h + 1) * half)
        back = dot_nn(halves[h][3][...], cot_s[:, span])
        gp_s[rows, span] = (back * dgel_s[rows, :]).astype(BF16)
    grad_b = dot_nn(up_o[...], gp_s[0:half, span]) + dot_nn(up_p[...], gp_s[half:, span])
    inv = 1.0 / width
    for j in range(PAIR):
        lanes = slice(j * slots, (j + 1) * slots)
        cols = pl.ds(pl.multiple_of(base + j * slots, slots), slots)
        gb = grad_b[:, lanes]
        unit = nrm_s[:, lanes]
        lnacc_ref[0] += gb * unit
        lnacc_ref[1] += gb
        f = gb * nb[0]
        f_mean = jnp.sum(f, axis=0, keepdims=True) * inv
        fn_mean = jnp.sum(f * unit, axis=0, keepdims=True) * inv
        gh1 = cot_s[:, cols].astype(F32) + rec_s[j, groups, 0:1, :] * (
            f - f_mean - unit * fn_mean
        )
        gh1_ref[:, lanes] = gh1
        ga_s[:, cols] = gh1.astype(BF16)

    for h in range(2):
        gm = dot_nn(halves[h][1][...], ga_s[:, span])
        for j in range(PAIR):
            lanes = slice(j * slots, (j + 1) * slots)
            for g in range(groups // 2):
                at = h * (groups // 2) + g
                grad = gm[g * 96 : (g + 1) * 96, lanes].reshape(4, HEAD_DIM, slots)
                mixed = mixf[at * 96 : (at + 1) * 96, lanes].reshape(4, HEAD_DIM, slots)
                rec = rec_s[j, at].reshape(8, 1, slots)[0:4]
                inner = -(jnp.sum(grad * mixed, axis=1, keepdims=True) * rec)
                high = inner.astype(BF16).astype(F32)
                low = inner - high
                rows8 = lax.broadcasted_iota(jnp.int32, (4, 8, slots), 1)
                tail = jnp.where(rows8 == 0, high, jnp.where(rows8 == 1, low, 0.0))
                full = jnp.concatenate([grad * rec, tail], axis=1)
                do_ref[j, at * 128 : (at + 1) * 128, :] = (
                    full.reshape(4 * PAD_DIM, slots).astype(BF16)
                )

    @pl.when(step == steps - 1)
    def _():
        owners = gown_ref.shape[0]
        some = half // owners
        for h, g_ref in enumerate((gown_ref, gpeer_ref)):
            rows = slice(h * half, (h + 1) * half)
            gdown = dot_nt(act_s[rows, :], cot_s[...])
            gout = dot_nt(mix_s[rows, :], ga_s[...])
            for o in range(owners):
                both = jnp.concatenate(
                    [gdown[o * some : (o + 1) * some], gout[o * some : (o + 1) * some]], axis=0
                )
                g_ref[o, :, 0:width] = both.astype(g_ref.dtype)
            gup = dot_nt(nbt_s[...], gp_s[rows, :])
            g_ref[:, :, width:] = gup.reshape(owners, 2 * some, half).astype(g_ref.dtype)


def middle_kernel(na_ref, q_ref, k_ref, v_ref, do_ref, e_ref, dx_ref, g_ref):
    step = pl.program_id(0)
    steps = pl.num_programs(0)
    slots = q_ref.shape[2]
    half = dx_ref.shape[0] // 3
    base = pl.multiple_of(step * PAIR * slots, PAIR * slots)
    groups = half // (4 * HEAD_DIM)
    for j in range(PAIR):
        cols = pl.ds(pl.multiple_of(base + j * slots, slots), slots)

        def attend(g, carry, j=j, cols=cols):
            rows = pl.ds(pl.multiple_of(g * 4 * PAD_DIM, 4 * PAD_DIM), 4 * PAD_DIM)
            vals = v_ref[j, rows, :].T
            dos = do_ref[j, rows, :]
            qs = q_ref[j, rows, :]
            ks = k_ref[j, rows, :]
            back = dot_nn(vals, block_columns(dos))
            dq, dk, dv = [], [], []
            for a in range(4):
                cut = slice(a * PAD_DIM, (a + 1) * PAD_DIM)
                ex = e_ref[j, g * 4 + a]
                ds = (ex.astype(F32) * back[:, a * slots : (a + 1) * slots]).astype(BF16)
                dq.append(dot_nn(ks[cut], ds)[0:HEAD_DIM])
                dk.append(dot_nt(qs[cut], ds)[0:HEAD_DIM])
                dv.append(dot_nt(dos[cut], ex)[0:HEAD_DIM])
            for c, (parts, scale) in enumerate(((dq, SCORE_SCALE), (dk, LN2), (dv, None))):
                at = pl.ds(pl.multiple_of(c * half + g * 96, 32), 96)
                whole = jnp.concatenate(parts, axis=0)
                if scale is not None:
                    whole = whole * scale
                dx_ref[at, cols] = whole.astype(BF16)
            return carry

        lax.fori_loop(0, groups, attend, 0, unroll=4)

    @pl.when(step == steps - 1)
    def _():
        for c in range(3):
            grad = dot_nt(na_ref[...], dx_ref[c * half : (c + 1) * half, :])
            g_ref[:, :, c * half : (c + 1) * half] = grad.reshape(
                g_ref.shape[0], g_ref.shape[1], half
            ).astype(g_ref.dtype)


def back_kernel(
    dxo_ref, dxp_ref, qkv_o, qkv_p, h0_ref, gh1_ref, fs_ref, gain_ref, lnb_ref, ig_ref, small_ref, nb, lnacc, ge
):
    step = pl.program_id(0)
    slots = ig_ref.shape[1]
    width = ig_ref.shape[2]
    half = width // 2
    inv = 1.0 / width

    @pl.when(step == 0)
    def _():
        lnacc[...] = jnp.zeros_like(lnacc)
        ge[...] = jnp.zeros_like(ge)
        nb[...] = lane_columns(gain_ref[0:1, :], slots)

    total = None
    for qkv, dx in ((qkv_o, dxo_ref), (qkv_p, dxp_ref)):
        for c in range(3):
            part = dot_nn(qkv[c], dx[c * half : (c + 1) * half, :])
            total = part if total is None else total + part
    highs, lows = [], []
    for j in range(PAIR):
        lanes = slice(j * slots, (j + 1) * slots)
        ga = total[:, lanes]
        centred, rec = norm_parts(h0_ref[:, lanes])
        unit = centred * rec
        lnacc[0] += ga * unit
        lnacc[1] += ga
        f = ga * nb[...]
        f_mean = jnp.sum(f, axis=0, keepdims=True) * inv
        fn_mean = jnp.sum(f * unit, axis=0, keepdims=True) * inv
        ig = gh1_ref[:, lanes] + rec * (f - f_mean - unit * fn_mean)
        ig_ref[j] = ig.T
        high = ig.astype(BF16)
        highs.append(high)
        lows.append((ig - high.astype(F32)).astype(BF16))
    fs = fs_ref[...]
    ge[...] += dot_nt(jnp.concatenate(highs, axis=1), fs) + dot_nt(
        jnp.concatenate(lows, axis=1), fs
    )

    @pl.when(step == pl.num_programs(0) - 1)
    def _():
        lane = lax.broadcasted_iota(jnp.int32, (width, slots), 1)
        rows = ge[:, 0:slots] + ge[:, slots:]
        sums = (lnacc[0], lnacc[1], lnb_ref[0], lnb_ref[1])
        for at, part in enumerate(sums):
            rows = jnp.where(lane == IDENT_USED + at, jnp.sum(part, axis=1, keepdims=True), rows)
        rows = jnp.where(lane < IDENT_ROWS, rows, 0.0)
        if small_ref.shape[0] == width:
            small_ref[...] = rows
        else:
            cut = rows.reshape(small_ref.shape[0], 3, 8, slots)
            flat = (small_ref.shape[0] * 8, slots)
            packed = cut[:, 0].reshape(flat)
            packed = packed + pltpu.roll(cut[:, 1].reshape(flat), IDENT_ROWS, 1)
            packed = packed + pltpu.roll(cut[:, 2].reshape(flat), 2 * IDENT_ROWS, 1)
            small_ref[...] = packed.reshape(small_ref.shape)


def gather_kernel(got1_ref, own_ref, a_ref, b_ref, c_ref, got_ref, red1_ref, red2_ref, small_ref, sq_ref):
    red1 = got1_ref[0].astype(F32)
    for o in range(1, got1_ref.shape[0]):
        red1 = red1 + got1_ref[o].astype(F32)
    red2 = own_ref[...].astype(F32) + a_ref[...].astype(F32)
    red2 = red2 + b_ref[...].astype(F32) + c_ref[...].astype(F32)
    small = got_ref[0]
    for o in range(1, got_ref.shape[0]):
        small = small + got_ref[o]
    red1_ref[...] = red1
    red2_ref[...] = red2
    small_ref[...] = small
    both = red1 * red1 + red2 * red2
    lanes = sq_ref.shape[1]
    folded = both[:, 0:lanes]
    for c in range(1, both.shape[1] // lanes):
        folded = folded + both[:, c * lanes : (c + 1) * lanes]
    total = jnp.sum(folded) + jnp.sum(small * small)
    sq_ref[...] = jnp.full(sq_ref.shape, total, F32)


def adam_kernel(*refs):
    sq_ref, red1_ref, red2_ref, small_ref = refs[0:4]
    ins, clip_ref, outs = refs[4:22], refs[22], refs[23:41]
    total = jnp.sum(sq_ref[...], axis=0, keepdims=True)
    clip = jnp.sqrt(total)
    clip_ref[...] = clip
    scale = jnp.max(jnp.minimum(1.0, CLIP_LIMIT / (clip + 1e-06)))
    half = red2_ref.shape[1] // 3
    some = red1_ref.shape[0] // 2
    lanes = small_ref.shape[1]
    small = small_ref[...]
    table = jnp.concatenate(
        [
            small,
            pltpu.roll(small, lanes - IDENT_ROWS, 1),
            pltpu.roll(small, lanes - 2 * IDENT_ROWS, 1),
        ],
        axis=0,
    )
    norm_grad = table.T[IDENT_USED : IDENT_USED + 4]
    matrix = (MATRIX_RATE, MATRIX_DECAY)
    for c in range(3):
        step = adam_step(
            ins[0][c], ins[1][c], ins[2][c], red2_ref[:, c * half : (c + 1) * half], *matrix, scale
        )
        for out, value in zip(outs[0:3], step):
            out[c] = value
    jobs = (
        (red1_ref[some:, 0 : 2 * half], matrix),
        (red1_ref[:, 2 * half :], matrix),
        (red1_ref[0:some, 0 : 2 * half], matrix),
        (norm_grad, (NORM_RATE, 0.0)),
        (table[:, 0:IDENT_USED], (EMBED_RATE, 0.0)),
    )
    for at, (grad, rates) in enumerate(jobs):
        i = 3 * (at + 1)
        step = adam_step(ins[i][...], ins[i + 1][...], ins[i + 2][...], grad, *rates, scale)
        for out, value in zip(outs[i : i + 3], step):
            out[...] = value


def whole_spec(shape):
    zeros = (0,) * len(shape)
    return pl.BlockSpec(shape, lambda i: zeros, pipeline_mode=pl.Buffered(1))


def lead_spec(*rest):
    return pl.BlockSpec((PAIR,) + rest, lambda i: (i,) + (0,) * len(rest))


def column_spec(rows, slots):
    return pl.BlockSpec((rows, PAIR * slots), lambda i: (0, i))


def costs(flops, moved):
    return pl.CostEstimate(flops=flops, bytes_accessed=moved, transcendentals=0)


def embed(tokens, cotangent, token_types, pairs_t, lap_t, embed_weight, norm_params):
    mols, slots, width = tokens.shape
    toks = mols * slots
    rows = (width, width, 256, width)
    types = (F32, BF16, BF16, BF16)
    return pl.pallas_call(
        embed_kernel,
        grid=(mols // PAIR,),
        out_shape=[jax.ShapeDtypeStruct((r, toks), t) for r, t in zip(rows, types)],
        out_specs=[column_spec(r, slots) for r in rows],
        in_specs=[
            lead_spec(slots, width),
            lead_spec(slots, width),
            lead_spec(1, slots),
            lead_spec(2, slots),
            lead_spec(lap_t.shape[1], lap_t.shape[2]),
            whole_spec(embed_weight.shape),
            whole_spec(norm_params.shape),
        ],
        scratch_shapes=[
            pltpu.VMEM((2, width, slots), F32),
            pltpu.VMEM((IDENT_ROWS, width), F32),
            pltpu.VMEM((width, 256), BF16),
        ],
        compiler_params=pltpu.CompilerParams(vmem_limit_bytes=VMEM_BYTES),
        cost_estimate=costs(8_000_000_000, 10_000_000),
        name="embed",
    )(tokens, cotangent, token_types.reshape(mols, 1, slots), pairs_t, lap_t, embed_weight, norm_params)


def front(lengths, h0, na, cot, norm_params, own, peer, mols):
    width, toks = h0.shape
    slots = toks // mols
    half = width // 2
    heads = width // HEAD_DIM
    owners = 16
    col = column_spec(width, slots)
    weights = []
    for pair in zip(own, peer):
        weights += list(pair)
    gshape = (owners, 2 * half // owners, 3 * half)
    padded = jax.ShapeDtypeStruct((mols, heads * PAD_DIM, slots), BF16)
    outs = [
        (jax.ShapeDtypeStruct((mols, slots, width), BF16), lead_spec(slots, width)),
        (jax.ShapeDtypeStruct((width, toks), F32), col),
        (padded, lead_spec(heads * PAD_DIM, slots)),
        (padded, lead_spec(heads * PAD_DIM, slots)),
        (padded, lead_spec(heads * PAD_DIM, slots)),
        (padded, lead_spec(heads * PAD_DIM, slots)),
        (jax.ShapeDtypeStruct((mols, heads, slots, slots), BF16), lead_spec(heads, slots, slots)),
        (jax.ShapeDtypeStruct(gshape, BF16), whole_spec(gshape)),
        (jax.ShapeDtypeStruct(gshape, BF16), whole_spec(gshape)),
        (jax.ShapeDtypeStruct((2, width, slots), F32), whole_spec((2, width, slots))),
    ]
    return pl.pallas_call(
        front_kernel,
        grid=(mols // PAIR,),
        out_shape=[o[0] for o in outs],
        out_specs=[o[1] for o in outs],
        in_specs=[
            pl.BlockSpec(memory_space=pltpu.SMEM),
            col,
            col,
            whole_spec(cot.shape),
            whole_spec(norm_params.shape),
        ]
        + [whole_spec(w.shape) for w in weights],
        scratch_shapes=[
            pltpu.VMEM((2, 3 * half, width), BF16),
            pltpu.VMEM((2, width, half), BF16),
            pltpu.VMEM((2, half, width), BF16),
            pltpu.VMEM((2, width, half), BF16),
            pltpu.VMEM((2, width, slots), F32),
        ]
        + [pltpu.VMEM((width, toks), BF16)] * 5
        + [pltpu.VMEM((width, PAIR * slots), F32)] * 4
        + [pltpu.VMEM((PAIR, heads // 4 + 1, 8, slots), F32)],
        compiler_params=pltpu.CompilerParams(vmem_limit_bytes=VMEM_BYTES),
        cost_estimate=costs(60_000_000_000, 50_000_000),
        name="front",
    )(lengths, h0, na, cot, norm_params, *weights)


def middle(which, na, q, k, v, do, e):
    mols, heads, slots, _ = e.shape
    width, toks = na.shape
    half = width // 2
    rows = heads // 2 * PAD_DIM
    part = pl.BlockSpec((PAIR, rows, slots), lambda i: (i, which, 0))
    gshape = (16, width // 16, 3 * half)
    return pl.pallas_call(
        middle_kernel,
        grid=(mols // PAIR,),
        out_shape=[
            jax.ShapeDtypeStruct((3 * half, toks), BF16),
            jax.ShapeDtypeStruct(gshape, BF16),
        ],
        in_specs=[
            whole_spec(na.shape),
            part,
            part,
            part,
            part,
            pl.BlockSpec((PAIR, heads // 2, slots, slots), lambda i: (i, which, 0, 0)),
        ],
        out_specs=[whole_spec((3 * half, toks)), whole_spec(gshape)],
        compiler_params=pltpu.CompilerParams(vmem_limit_bytes=VMEM_BYTES),
        cost_estimate=costs(20_000_000_000, 12_000_000),
        name="middle",
    )(na, q, k, v, do, e)


def back(dxo, dxp, qkv_o, qkv_p, h0, gh1, fs, gain, lnb, mols, packed):
    width, toks = h0.shape
    slots = toks // mols
    col = column_spec(width, slots)
    dxs = column_spec(dxo.shape[0], slots)
    small = (width // 24, 8, slots) if packed else (width, slots)
    return pl.pallas_call(
        back_kernel,
        grid=(mols // PAIR,),
        out_shape=[
            jax.ShapeDtypeStruct((mols, slots, width), F32),
            jax.ShapeDtypeStruct(small, F32),
        ],
        in_specs=[
            dxs,
            dxs,
            whole_spec(qkv_o.shape),
            whole_spec(qkv_p.shape),
            col,
            col,
            column_spec(fs.shape[0], slots),
            whole_spec(gain.shape),
            whole_spec(lnb.shape),
        ],
        out_specs=[lead_spec(slots, width), whole_spec(small)],
        scratch_shapes=[
            pltpu.VMEM((width, slots), F32),
            pltpu.VMEM((2, width, slots), F32),
            pltpu.VMEM((width, fs.shape[0]), F32),
        ],
        compiler_params=pltpu.CompilerParams(vmem_limit_bytes=VMEM_BYTES),
        cost_estimate=costs(18_000_000_000, 15_000_000),
        name="back",
    )(dxo, dxp, qkv_o, qkv_p, h0, gh1, fs, gain, lnb)


def gather(got1, own2, others2, got):
    rows, columns = got1.shape[1:]
    lanes = got.shape[2]
    return pl.pallas_call(
        gather_kernel,
        out_shape=[
            jax.ShapeDtypeStruct((rows, columns), F32),
            jax.ShapeDtypeStruct((rows, columns), F32),
            jax.ShapeDtypeStruct(got.shape[1:], F32),
            jax.ShapeDtypeStruct((got.shape[0], lanes), F32),
        ],
        compiler_params=pltpu.CompilerParams(vmem_limit_bytes=VMEM_BYTES),
        name="gather",
    )(got1, own2, *others2, got)


def adam_all(squares, red1, red2, small, state):
    return pl.pallas_call(
        adam_kernel,
        out_shape=[jax.ShapeDtypeStruct((1, squares.shape[1]), F32)]
        + [jax.ShapeDtypeStruct(a.shape, F32) for a in state],
        compiler_params=pltpu.CompilerParams(vmem_limit_bytes=VMEM_BYTES),
        name="adam",
    )(squares, red1, red2, small, *state)


def swap(value):
    return lax.ppermute(value, "mp", [(0, 1), (1, 0)])


def hop(value, flip):
    size = lax.axis_size("dp")
    return lax.ppermute(value, "dp", [(i, i ^ flip) for i in range(size)])


def take(value, index, axis=0):
    return lax.dynamic_index_in_dim(value, index, axis, keepdims=False)


def adam_step(master, mean_old, square_old, gradient, rate, decay, clip_scale):
    clipped = gradient * clip_scale
    mean_new = BETA_FIRST * mean_old + (1.0 - BETA_FIRST) * clipped
    square_new = BETA_SECOND * square_old + (1.0 - BETA_SECOND) * clipped * clipped
    mean_hat = mean_new / (1.0 - BETA_FIRST**STEP)
    square_hat = square_new / (1.0 - BETA_SECOND**STEP)
    updated = master - rate * (mean_hat / (jnp.sqrt(square_hat) + ADAM_EPS) + decay * master)
    return (updated, mean_new, square_new)


def on_device(
    tokens,
    cotangent,
    lengths,
    token_types,
    node_pairs,
    laplacian,
    qkv_weight,
    out_weight,
    up_weight,
    down_weight,
    qkv_master,
    qkv_mean,
    qkv_square,
    out_master,
    out_mean,
    out_square,
    up_master,
    up_mean,
    up_square,
    down_master,
    down_mean,
    down_square,
    norm_params,
    norm_mean,
    norm_square,
    embed_weight,
    embed_mean,
    embed_square,
):
    mols, slots, width = tokens.shape
    half = width // 2
    dp_size = lax.axis_size("dp")
    mp_size = lax.axis_size("mp")
    idents = embed_weight.shape[0]

    own = (qkv_weight.transpose(1, 0, 2), out_weight, up_weight, down_weight)
    peer = tuple(swap(w) for w in own)

    world = dp_size * mp_size
    shard_width = width // world
    fits = dp_size == 16 and shard_width == 24

    h0, na, fs, cot = embed(
        tokens,
        cotangent,
        token_types,
        node_pairs.transpose(0, 2, 1),
        laplacian.transpose(0, 2, 1),
        embed_weight,
        norm_params,
    )
    (output, gh1, q, k, v, do, e, gown1, gpeer1, lnb) = front(
        lengths, h0, na, cot, norm_params, own, peer, mols
    )
    sum1 = (gown1.astype(F32) + swap(gpeer1).astype(F32)).astype(BF16)
    sum1, do = lax.optimization_barrier((sum1, do))
    if fits:
        got1 = lax.all_to_all(sum1, "dp", 0, 0, tiled=True)
    dxp, gpeer2 = middle(1, na, q, k, v, do, e)
    got2 = swap(gpeer2)
    dxo, gown2 = middle(0, na, q, k, v, do, e)
    sum2 = (gown2.astype(F32) + got2.astype(F32)).astype(BF16)
    index = lax.axis_index("dp")
    if fits:
        plane, line = index & 3, index >> 2
        grid = sum2.reshape((4, 4) + sum2.shape[1:]).swapaxes(0, 1)
        own2 = take(grid, plane)
        sends = [take(grid, plane ^ k) for k in (1, 2, 3)]
        sends, dxo = lax.optimization_barrier((sends, dxo))
        near = [hop(piece, k) for piece, k in zip(sends, (1, 2, 3))]
    input_grad, small = back(dxo, dxp, own[0], peer[0], h0, gh1, fs, norm_params, lnb, mols, fits)

    shard_index = index * mp_size + lax.axis_index("mp")
    norm_own = lax.dynamic_slice_in_dim(norm_params, shard_index * shard_width, shard_width, 1)
    embed_own = lax.dynamic_slice_in_dim(embed_weight, shard_index * shard_width, shard_width, 1)
    flip = lambda a: a.transpose(1, 0, 2)
    if fits:
        plane_sum = own2.astype(F32)
        for piece in near:
            plane_sum = plane_sum + piece.astype(F32)
        plane_sum = plane_sum.astype(BF16)
        small, got1, plane_sum = lax.optimization_barrier((small, got1, plane_sum))
        got = lax.all_to_all(small, ("dp", "mp"), 0, 0, tiled=True)
        far = [hop(take(plane_sum, line ^ k), 4 * k) for k in (1, 2, 3)]
        red1, red2, small_own, squares = gather(got1, take(plane_sum, line), far, got)
        lanes = squares.shape[1]
        squares = lax.all_to_all(squares.reshape(world, 1, lanes), ("dp", "mp"), 0, 0, tiled=True)
        state = (
            (flip(qkv_master), flip(qkv_mean), flip(qkv_square))
            + (out_master, out_mean, out_square)
            + (up_master, up_mean, up_square)
            + (down_master, down_mean, down_square)
            + (norm_own, norm_mean, norm_square)
            + (embed_own.T, embed_mean.T, embed_square.T)
        )
        clip, *new = adam_all(squares.reshape(world, lanes), red1, red2, small_own, state)
        new = [flip(a) for a in new[0:3]] + list(new[3:15]) + [a.T for a in new[15:18]]
        return (output, input_grad, clip[0, 0]) + tuple(new)

    some = half // 16
    scatter = partial(lax.psum_scatter, axis_name="dp", scatter_dimension=0, tiled=True)
    sum1, sum2 = sum1.astype(F32), sum2.astype(F32)
    reduced_down = scatter(sum1[:, 0:some, 0:width].reshape(half, width))
    reduced_out = scatter(sum1[:, some:, 0:width].reshape(half, width))
    reduced_up = scatter(sum1[:, :, width:].reshape(width, half))
    reduced_qkv = scatter(sum2.reshape(width, 3, half))
    small = small[:, : idents + 4].reshape(world, shard_width, idents + 4)
    small_own = jnp.sum(lax.all_to_all(small, ("dp", "mp"), 0, 0, tiled=True), axis=0).T
    reduced = (reduced_qkv, reduced_out, reduced_up, reduced_down, small_own[idents:], small_own[:idents])
    own_square = sum(jnp.sum(piece * piece) for piece in reduced)
    clip_norm = jnp.sqrt(lax.psum(own_square, ("dp", "mp")))
    clip_scale = jnp.minimum(1.0, CLIP_LIMIT / (clip_norm + 1e-06))
    state = (
        (qkv_master, qkv_mean, qkv_square, MATRIX_RATE, MATRIX_DECAY),
        (out_master, out_mean, out_square, MATRIX_RATE, MATRIX_DECAY),
        (up_master, up_mean, up_square, MATRIX_RATE, MATRIX_DECAY),
        (down_master, down_mean, down_square, MATRIX_RATE, MATRIX_DECAY),
        (norm_own, norm_mean, norm_square, NORM_RATE, 0.0),
        (embed_own, embed_mean, embed_square, EMBED_RATE, 0.0),
    )
    new = ()
    for (master, mean, square, rate, decay), grad in zip(state, reduced):
        new += adam_step(master, mean, square, grad, rate, decay, clip_scale)
    return (output, input_grad, clip_norm) + new


def solution(mesh):
    tokens = P(("dp", "mp"), None, None)
    qkv = P("dp", None, "mp")
    rows = P(("mp", "dp"), None)
    both = P("dp", "mp")
    small = P(None, ("dp", "mp"))
    return jax.shard_map(
        on_device,
        mesh=mesh,
        in_specs=(
            tokens,
            tokens,
            P(("dp", "mp")),
            P(("dp", "mp"), None),
            tokens,
            tokens,
            P(None, None, "mp"),
            P("mp", None),
            P(None, "mp"),
            P("mp", None),
        )
        + (qkv,) * 3
        + (rows,) * 3
        + (both,) * 3
        + (rows,) * 3
        + (P(), small, small) * 2,
        out_specs=(tokens, tokens, P())
        + (qkv,) * 3
        + (rows,) * 3
        + (both,) * 3
        + (rows,) * 3
        + (small,) * 6,
        check_vma=False,
    )
```

```python
from functools import partial
import math

import jax
import jax.numpy as jnp
from jax import lax
from jax.experimental import pallas as pl
from jax.experimental.pallas import tpu as pltpu
from jax.sharding import PartitionSpec as P

HEAD_DIM = 24
PAD_DIM = 32
STEP = 10
NORM_EPS = 1e-05
BETA_FIRST = 0.9
BETA_SECOND = 0.95
ADAM_EPS = 1e-08
MATRIX_RATE = 0.03
NORM_RATE = 0.5
EMBED_RATE = 0.05
MATRIX_DECAY = 0.1
CLIP_LIMIT = 1.0
MASK_VALUE = -1e30
SCORE_SCALE = 1.0 / math.sqrt(HEAD_DIM)
LOG2E = 1.4426950408889634
LN2 = 0.6931471805599453
IDENT_ROWS = 40
IDENT_USED = 34
PAIR = 2
VMEM_BYTES = 60 * 1024 * 1024
FRONT_UNROLL = 8
MIDDLE_UNROLL = 8

F32 = jnp.float32
BF16 = jnp.bfloat16


def dot_nn(lhs, rhs):
    return lax.dot_general(lhs, rhs, (((1,), (0,)), ((), ())), preferred_element_type=F32)


def dot_nt(lhs, rhs):
    return lax.dot_general(lhs, rhs, (((1,), (1,)), ((), ())), preferred_element_type=F32)


def norm_parts(values):
    scale = 1.0 / values.shape[0]
    centred = values - jnp.sum(values, axis=0, keepdims=True) * scale
    spread = jnp.sum(centred * centred, axis=0, keepdims=True) * scale
    return centred, lax.rsqrt(spread + NORM_EPS)


def gelu_parts(x):
    size = jnp.abs(x)
    bell = jnp.exp2((-0.5 * LOG2E) * (x * x))
    t = 1.0 / (1.0 + (0.3275911 / math.sqrt(2.0)) * size)
    poly = t * (
        0.5 * 0.254829592
        + t
        * (
            0.5 * -0.284496736
            + t * (0.5 * 1.421413741 + t * (0.5 * -1.453152027 + t * (0.5 * 1.061405429)))
        )
    )
    tail = poly * bell
    share = jnp.where(x < 0.0, tail, 1.0 - tail)
    return x * share, share + x * bell * (1.0 / math.sqrt(2.0 * math.pi))


def head_rows(values, tail):
    heads = values.shape[0] // HEAD_DIM
    cut = values.reshape(heads, HEAD_DIM, values.shape[1])
    tails = jnp.broadcast_to(tail[None], (heads,) + tail.shape)
    return jnp.concatenate([cut, tails], axis=1).reshape(heads * PAD_DIM, values.shape[1])


def block_columns(rows):
    zero = jnp.zeros((PAD_DIM, rows.shape[1]), rows.dtype)
    columns = []
    for head in range(4):
        pieces = [zero] * 4
        pieces[head] = rows[head * PAD_DIM : (head + 1) * PAD_DIM]
        columns.append(jnp.concatenate(pieces, axis=0))
    return jnp.concatenate(columns, axis=1)


def lane_columns(row, slots):
    return jnp.broadcast_to(row, (slots, row.shape[1])).T


def embed_kernel(
    tok_ref,
    cot_ref,
    typ_ref,
    pair_ref,
    lap_ref,
    embed_ref,
    norm_ref,
    h0_ref,
    na_ref,
    fs_ref,
    ct_ref,
    nb,
    rows,
    est,
):
    slots = tok_ref.shape[1]
    width = tok_ref.shape[2]

    @pl.when(pl.program_id(0) == 0)
    def _():
        for row in range(2):
            nb[row] = lane_columns(norm_ref[row : row + 1, :], slots)
        rows[...] = jnp.zeros_like(rows)
        rows[0 : embed_ref.shape[0], :] = embed_ref[...]
        whole = rows[...]
        e1 = whole.astype(BF16).astype(F32)
        e2 = (whole - e1).astype(BF16).astype(F32)
        e3 = whole - e1 - e2
        blank = jnp.zeros((8, width), F32)
        stacked = jnp.concatenate([e1, e2, e3, blank, e1, e2, e1, blank], axis=0)
        est[...] = stacked.T.astype(BF16)

    node_iota = lax.broadcasted_iota(jnp.int32, (lap_ref.shape[2], slots), 0)
    row_iota = lax.broadcasted_iota(jnp.int32, (8, slots), 0)
    for j in range(PAIR):
        lanes = slice(j * slots, (j + 1) * slots)
        lap = lap_ref[j]
        lap1 = lap.astype(BF16)
        rest = lap - lap1.astype(F32)
        lap2 = rest.astype(BF16)
        lap3 = (rest - lap2.astype(F32)).astype(BF16)
        laps = jnp.concatenate([lap1.astype(F32), lap2.astype(F32), lap3.astype(F32)], axis=0)
        laps = laps.astype(BF16)
        left = jnp.where(node_iota == pair_ref[j, 0:1, :], 1.0, 0.0).astype(BF16)
        right = jnp.where(node_iota == pair_ref[j, 1:2, :], 1.0, 0.0).astype(BF16)
        lf = dot_nn(laps, left)
        rf = dot_nn(laps, right)
        types = typ_ref[j]
        kinds = jnp.where((row_iota < 2) & (row_iota == types), 1.0, 0.0)
        none = jnp.zeros((8, slots), F32)
        ident = lap.shape[0]
        f1 = jnp.concatenate([lf[0:ident], rf[0:ident], kinds], axis=0)
        f2 = jnp.concatenate([lf[ident : 2 * ident], rf[ident : 2 * ident], none], axis=0)
        f3 = jnp.concatenate([lf[2 * ident :], rf[2 * ident :], none], axis=0)
        stack = jnp.concatenate([f1, f1, f1, none, f2, f2, f3, none], axis=0).astype(BF16)
        fs_ref[:, lanes] = stack
        h0 = tok_ref[j].T.astype(F32) + dot_nn(est[...], stack)
        h0_ref[:, lanes] = h0
        centred, rec = norm_parts(h0)
        na_ref[:, lanes] = (centred * rec * nb[0] + nb[1]).astype(BF16)
        ct_ref[:, lanes] = cot_ref[j].T


def block_pair(rows):
    zero = jnp.zeros((PAD_DIM, rows.shape[1]), rows.dtype)
    left = jnp.concatenate([rows[0:PAD_DIM], zero], axis=0)
    right = jnp.concatenate([zero, rows[PAD_DIM:]], axis=0)
    return jnp.concatenate([left, right], axis=1)


def staged(at, first, second, third):
    one, two = {}, {}
    count = len(at)
    for n in range(count + 2):
        if n < count:
            one[n] = first(*at[n])
        if 0 <= n - 1 < count:
            two[n - 1] = second(*at[n - 1], one.pop(n - 1))
        if 0 <= n - 2 < count:
            third(*at[n - 2], two.pop(n - 2))


def front_kernel(
    len_ref,
    h0_ref,
    na_ref,
    cot_s,
    norm_ref,
    qkv_o,
    qkv_p,
    out_o,
    out_p,
    up_o,
    up_p,
    down_o,
    down_p,
    gh1_ref,
    h1_s,
    act_s,
    q_ref,
    k_ref,
    v_ref,
    do_ref,
    e_ref,
    gown_ref,
    gpeer_ref,
    lnacc_ref,
    qkvt,
    outt,
    upt,
    outw,
    upw,
    downw,
    nb,
    nbt_s,
    gp_s,
    mix_s,
    ga_s,
    mixf,
    nrm_s,
    rec_s,
):
    step = pl.program_id(0)
    steps = pl.num_programs(0)
    slots = e_ref.shape[2]
    width = h0_ref.shape[0]
    half = width // 2
    halves = ((qkv_o, out_o, up_o, down_o), (qkv_p, out_p, up_p, down_p))

    @pl.when(step == 0)
    def _():
        for h, (qkv, out, up, down) in enumerate(halves):
            part = slice(h * half, (h + 1) * half)
            for c in range(3):
                at = (3 * h + c) * half
                qkvt[at : at + half, :] = qkv[c].T
            outt[:, part] = out[...].T
            upt[part, :] = up[...].T
            outw[part, :] = out[...]
            upw[:, part] = up[...]
            downw[part, :] = down[...]
        for row in range(2):
            nb[row] = lane_columns(norm_ref[row + 2 : row + 3, :], slots)
        lnacc_ref[...] = jnp.zeros_like(lnacc_ref)

    base = pl.multiple_of(step * PAIR * slots, PAIR * slots)
    span = pl.ds(base, PAIR * slots)

    phase = pl.when(step >= 0)
    groups = width // (4 * HEAD_DIM)
    inv = 1.0 / width
    parts = tuple(slice(h * half, (h + 1) * half) for h in range(2))
    sides = tuple(slice(j * slots, (j + 1) * slots) for j in range(PAIR))
    columns = tuple(
        pl.ds(pl.multiple_of(base + j * slots, slots), slots) for j in range(PAIR)
    )

    @phase
    def _():
        row_iota = lax.broadcasted_iota(jnp.int32, (8, slots), 0)
        lane_iota = lax.broadcasted_iota(jnp.int32, (1, slots), 1)
        one_row = jnp.where(row_iota == 0, 1.0, 0.0)
        two_rows = jnp.where(row_iota < 2, 1.0, 0.0)
        padded = half // HEAD_DIM * PAD_DIM
        for h in range(2):
            rows = slice(h * padded, (h + 1) * padded)
            for c, ref in enumerate((q_ref, k_ref, v_ref)):
                at = (3 * h + c) * half
                proj = dot_nn(qkvt[at : at + half, :], na_ref[...])
                for j in range(PAIR):
                    own = proj[:, sides[j]]
                    if c == 0:
                        own, tail = own * (SCORE_SCALE * LOG2E), one_row
                    elif c == 1:
                        length = len_ref[step * PAIR + j]
                        bias = jnp.where(lane_iota < length, 0.0, MASK_VALUE)
                        tail = jnp.where(row_iota == 0, bias, 0.0)
                    else:
                        tail = two_rows
                    ref[j, rows, :] = head_rows(own, tail).astype(BF16)

    def score(j, g):
        rows = pl.ds(pl.multiple_of(g * 4 * PAD_DIM, 4 * PAD_DIM), 4 * PAD_DIM)
        return dot_nn(k_ref[j, rows, :].T, block_columns(q_ref[j, rows, :]))

    def weigh(j, g, scores):
        exps = []
        for a in range(4):
            own = scores[:, a * slots : (a + 1) * slots]
            ex = jnp.exp2(own - jnp.max(own, axis=0, keepdims=True)).astype(BF16)
            e_ref[j, g * 4 + a] = ex
            exps.append(ex)
        return exps

    def mix_values(j, g, exps):
        rows = pl.ds(pl.multiple_of(g * 4 * PAD_DIM, 4 * PAD_DIM), 4 * PAD_DIM)
        vals = v_ref[j, rows, :]
        mixes = []
        for a in range(0, 4, 2):
            two = dot_nn(
                vals[a * PAD_DIM : (a + 2) * PAD_DIM], jnp.concatenate(exps[a : a + 2], axis=1)
            )
            for b in range(2):
                got = two[b * PAD_DIM : (b + 1) * PAD_DIM, b * slots : (b + 1) * slots]
                rec = 1.0 / got[HEAD_DIM : HEAD_DIM + 1]
                rec_s[j, g, a + b : a + b + 1, :] = rec
                mixes.append(got[0:HEAD_DIM] * rec)
        out_rows = pl.ds(pl.multiple_of(g * 4 * HEAD_DIM, 4 * HEAD_DIM), 4 * HEAD_DIM)
        mixf[j, out_rows, :] = jnp.concatenate(mixes, axis=0)

    def attend(i, carry):
        at = [i * FRONT_UNROLL + u for u in range(FRONT_UNROLL)]
        at = [(lax.div(n, groups), lax.rem(n, groups)) for n in at]
        staged(at, score, weigh, mix_values)
        return carry

    lax.fori_loop(0, PAIR * groups // FRONT_UNROLL, attend, 0)

    @phase
    def _():
        for j in range(PAIR):
            mix_s[:, columns[j]] = mixf[j].astype(BF16)
        attn = jnp.concatenate([dot_nn(outt[part, :], mix_s[:, span]) for part in parts], axis=0)
        for j in range(PAIR):
            h1 = h0_ref[:, sides[j]] + attn[:, sides[j]]
            h1_s[:, sides[j]] = h1
            centred, rec = norm_parts(h1)
            unit = centred * rec
            nrm_s[:, sides[j]] = unit
            rec_s[j, groups, 0:1, :] = rec
            nbt_s[:, columns[j]] = (unit * nb[0] + nb[1]).astype(BF16)

    @phase
    def _():
        for part in parts:
            act, slope = gelu_parts(dot_nn(upt[part, :], nbt_s[:, span]))
            act_s[part, span] = act.astype(BF16)
            back = dot_nn(downw[part, :], cot_s[:, span])
            gp_s[part, span] = (back * slope).astype(BF16)

    @phase
    def _():
        grad_b = jnp.concatenate([dot_nn(upw[part, :], gp_s[:, span]) for part in parts], axis=0)
        for j in range(PAIR):
            gb = grad_b[:, sides[j]]
            unit = nrm_s[:, sides[j]]
            lnacc_ref[0] += gb * unit
            lnacc_ref[1] += gb
            f = gb * nb[0]
            f_mean = jnp.sum(f, axis=0, keepdims=True) * inv
            fn_mean = jnp.sum(f * unit, axis=0, keepdims=True) * inv
            gh1 = cot_s[:, columns[j]].astype(F32) + rec_s[j, groups, 0:1, :] * (
                f - f_mean - unit * fn_mean
            )
            gh1_ref[:, sides[j]] = gh1
            ga_s[:, columns[j]] = gh1.astype(BF16)

    @phase
    def _():
        rows8 = lax.broadcasted_iota(jnp.int32, (4, 8, slots), 1)
        for h, part in enumerate(parts):
            gm = dot_nn(outw[part, :], ga_s[:, span])
            for j in range(PAIR):
                for g in range(groups // 2):
                    at = h * (groups // 2) + g
                    grad = gm[g * 96 : (g + 1) * 96, sides[j]].reshape(4, HEAD_DIM, slots)
                    mixed = mixf[j, at * 96 : (at + 1) * 96, :].reshape(4, HEAD_DIM, slots)
                    rec = rec_s[j, at].reshape(8, 1, slots)[0:4]
                    inner = -(jnp.sum(grad * mixed, axis=1, keepdims=True) * rec)
                    high = inner.astype(BF16).astype(F32)
                    low = inner - high
                    tail = jnp.where(rows8 == 0, high, jnp.where(rows8 == 1, low, 0.0))
                    full = jnp.concatenate([grad * rec, tail], axis=1)
                    do_ref[j, at * 128 : (at + 1) * 128, :] = (
                        full.reshape(4 * PAD_DIM, slots).astype(BF16)
                    )

    @pl.when(step == steps - 1)
    def _():
        owners = gown_ref.shape[0]
        some = half // owners
        for h, g_ref in enumerate((gown_ref, gpeer_ref)):
            rows = slice(h * half, (h + 1) * half)
            gdown = dot_nt(act_s[rows, :], cot_s[...])
            gout = dot_nt(mix_s[rows, :], ga_s[...])
            for o in range(owners):
                both = jnp.concatenate(
                    [gdown[o * some : (o + 1) * some], gout[o * some : (o + 1) * some]], axis=0
                )
                g_ref[o, :, 0:width] = both.astype(g_ref.dtype)
            gup = dot_nt(nbt_s[...], gp_s[rows, :])
            g_ref[:, :, width:] = gup.reshape(owners, 2 * some, half).astype(g_ref.dtype)


def middle_kernel(na_ref, q_ref, k_ref, v_ref, do_ref, e_ref, dx_ref, g_ref):
    attention_back(q_ref, k_ref, v_ref, do_ref, e_ref, dx_ref)
    half = dx_ref.shape[0] // 3

    @pl.when(pl.program_id(0) == pl.num_programs(0) - 1)
    def _():
        for c in range(3):
            cut = slice(c * half, (c + 1) * half)
            grad = dot_nt(na_ref[...], dx_ref[cut, :])
            g_ref[:, :, cut] = grad.reshape(g_ref.shape[0:2] + (half,)).astype(BF16)


def middle_own_kernel(
    plane_ref, na_ref, q_ref, k_ref, v_ref, do_ref, e_ref, got_ref, dx_ref, g0, g1, g2, g3, total
):
    attention_back(q_ref, k_ref, v_ref, do_ref, e_ref, dx_ref)
    half = dx_ref.shape[0] // 3

    @pl.when(pl.program_id(0) == pl.num_programs(0) - 1)
    def _():
        for c in range(3):
            cut = slice(c * half, (c + 1) * half)
            grad = dot_nt(na_ref[...], dx_ref[cut, :]).reshape(total.shape[0:2] + (half,))
            total[:, :, cut] = (grad + got_ref[:, :, cut].astype(F32)).astype(BF16)
        plane = plane_ref[0]
        for k, g_ref in enumerate((g0, g1, g2, g3)):
            for line in range(4):
                g_ref[line] = total[line * 4 + (plane ^ k)]


def attention_back(q_ref, k_ref, v_ref, do_ref, e_ref, dx_ref):
    step = pl.program_id(0)
    slots = q_ref.shape[2]
    half = dx_ref.shape[0] // 3
    base = pl.multiple_of(step * PAIR * slots, PAIR * slots)
    groups = half // (4 * HEAD_DIM)

    def rows_of(g):
        return pl.ds(pl.multiple_of(g * 4 * PAD_DIM, 4 * PAD_DIM), 4 * PAD_DIM)

    def score(j, g):
        return dot_nn(v_ref[j, rows_of(g), :].T, block_columns(do_ref[j, rows_of(g), :]))

    def weigh(j, g, back):
        grads = []
        for a in range(4):
            ex = e_ref[j, g * 4 + a].astype(F32)
            grads.append((ex * back[:, a * slots : (a + 1) * slots]).astype(BF16))
        return grads

    def products(j, g, grads):
        dos = do_ref[j, rows_of(g), :]
        qs = q_ref[j, rows_of(g), :]
        ks = k_ref[j, rows_of(g), :]
        dq, dk, dv = [], [], []
        for a in range(0, 4, 2):
            cut = slice(a * PAD_DIM, (a + 2) * PAD_DIM)
            both = jnp.concatenate(grads[a : a + 2], axis=1)
            exps = jnp.concatenate([e_ref[j, g * 4 + a + b].T for b in range(2)], axis=1)
            two = dot_nn(ks[cut], both)
            dq.append(two[0:HEAD_DIM, 0:slots])
            dq.append(two[PAD_DIM : PAD_DIM + HEAD_DIM, slots:])
            two = dot_nt(block_pair(qs[cut]), both)
            dk.append(two[0:HEAD_DIM])
            dk.append(two[PAD_DIM : PAD_DIM + HEAD_DIM])
            two = dot_nn(dos[cut], exps)
            dv.append(two[0:HEAD_DIM, 0:slots])
            dv.append(two[PAD_DIM : PAD_DIM + HEAD_DIM, slots:])
        cols = pl.ds(pl.multiple_of(base + j * slots, slots), slots)
        for c, (parts, scale) in enumerate(((dq, SCORE_SCALE), (dk, LN2), (dv, None))):
            at = pl.ds(pl.multiple_of(c * half + g * 96, 32), 96)
            whole = jnp.concatenate(parts, axis=0)
            if scale is not None:
                whole = whole * scale
            dx_ref[at, cols] = whole.astype(BF16)

    def attend(i, carry):
        at = [i * MIDDLE_UNROLL + u for u in range(MIDDLE_UNROLL)]
        at = [(lax.div(n, groups), lax.rem(n, groups)) for n in at]
        staged(at, score, weigh, products)
        return carry

    lax.fori_loop(0, PAIR * groups // MIDDLE_UNROLL, attend, 0)


def back_kernel(
    dxo_ref,
    dxp_ref,
    qkv_o,
    qkv_p,
    h0_ref,
    gh1_ref,
    fs_ref,
    gain_ref,
    lnb_ref,
    h1_ref,
    act_ref,
    down_o,
    down_p,
    ig_ref,
    output_ref,
    small_ref,
    nb,
    lnacc,
    ge,
    qkvw,
    downt,
):
    step = pl.program_id(0)
    slots = ig_ref.shape[1]
    width = ig_ref.shape[2]
    half = width // 2
    inv = 1.0 / width

    @pl.when(step == 0)
    def _():
        lnacc[...] = jnp.zeros_like(lnacc)
        ge[...] = jnp.zeros_like(ge)
        nb[...] = lane_columns(gain_ref[0:1, :], slots)
        for h, (qkv, down) in enumerate(((qkv_o, down_o), (qkv_p, down_p))):
            for c in range(3):
                at = (3 * h + c) * half
                qkvw[:, at : at + half] = qkv[c]
            downt[:, h * half : (h + 1) * half] = down[...].T

    total = dot_nn(qkvw[...], jnp.concatenate([dxo_ref[...], dxp_ref[...]], axis=0))
    ffn = dot_nn(downt[...], act_ref[...])
    for j in range(PAIR):
        lanes = slice(j * slots, (j + 1) * slots)
        output_ref[j] = (h1_ref[:, lanes] + ffn[:, lanes]).astype(BF16).T
    highs, lows = [], []
    for j in range(PAIR):
        lanes = slice(j * slots, (j + 1) * slots)
        ga = total[:, lanes]
        centred, rec = norm_parts(h0_ref[:, lanes])
        unit = centred * rec
        lnacc[0] += ga * unit
        lnacc[1] += ga
        f = ga * nb[...]
        f_mean = jnp.sum(f, axis=0, keepdims=True) * inv
        fn_mean = jnp.sum(f * unit, axis=0, keepdims=True) * inv
        ig = gh1_ref[:, lanes] + rec * (f - f_mean - unit * fn_mean)
        ig_ref[j] = ig.T
        high = ig.astype(BF16)
        highs.append(high)
        lows.append((ig - high.astype(F32)).astype(BF16))
    fs = fs_ref[...]
    ge[...] += dot_nt(jnp.concatenate(highs, axis=1), fs) + dot_nt(
        jnp.concatenate(lows, axis=1), fs
    )

    @pl.when(step == pl.num_programs(0) - 1)
    def _():
        lane = lax.broadcasted_iota(jnp.int32, (width, slots), 1)
        rows = ge[:, 0:slots] + ge[:, slots:]
        sums = (lnacc[0], lnacc[1], lnb_ref[0], lnb_ref[1])
        for at, part in enumerate(sums):
            rows = jnp.where(lane == IDENT_USED + at, jnp.sum(part, axis=1, keepdims=True), rows)
        rows = jnp.where(lane < IDENT_ROWS, rows, 0.0)
        if small_ref.shape[0] == width:
            small_ref[...] = rows
        else:
            cut = rows.reshape(small_ref.shape[0], 3, 8, slots)
            flat = (small_ref.shape[0] * 8, slots)
            packed = cut[:, 0].reshape(flat)
            packed = packed + pltpu.roll(cut[:, 1].reshape(flat), IDENT_ROWS, 1)
            packed = packed + pltpu.roll(cut[:, 2].reshape(flat), 2 * IDENT_ROWS, 1)
            small_ref[...] = packed.reshape(small_ref.shape)


def square_sum(value, lanes):
    both = value * value
    folded = both[:, 0:lanes]
    for c in range(1, both.shape[1] // lanes):
        folded = folded + both[:, c * lanes : (c + 1) * lanes]
    return jnp.sum(folded, axis=0, keepdims=True)


def first_kernel(got_ref, red_ref, sq_ref):
    red = got_ref[0].astype(F32)
    for o in range(1, got_ref.shape[0]):
        red = red + got_ref[o].astype(F32)
    red_ref[...] = red
    sq_ref[...] = square_sum(red, sq_ref.shape[1])


def gather_kernel(own_ref, a_ref, b_ref, c_ref, got_ref, sq1_ref, red_ref, small_ref, sq_ref):
    red = own_ref[...].astype(F32) + a_ref[...].astype(F32)
    red = red + b_ref[...].astype(F32) + c_ref[...].astype(F32)
    small = got_ref[0]
    for o in range(1, got_ref.shape[0]):
        small = small + got_ref[o]
    red_ref[...] = red
    small_ref[...] = small
    lanes = sq_ref.shape[1]
    rows = sq1_ref[...] + square_sum(red, lanes) + square_sum(small, lanes)
    sq_ref[...] = jnp.full(sq_ref.shape, jnp.sum(rows), F32)


def adam_kernel(*refs):
    sq_ref, red1_ref, red2_ref, small_ref = refs[0:4]
    ins, clip_ref, outs = refs[4:22], refs[22], refs[23:41]
    total = jnp.sum(sq_ref[...], axis=0, keepdims=True)
    clip = jnp.sqrt(total)
    clip_ref[...] = clip
    scale = jnp.max(jnp.minimum(1.0, CLIP_LIMIT / (clip + 1e-06)))
    half = red2_ref.shape[1] // 3
    some = red1_ref.shape[0] // 2
    lanes = small_ref.shape[1]
    small = small_ref[...]
    table = jnp.concatenate(
        [
            small,
            pltpu.roll(small, lanes - IDENT_ROWS, 1),
            pltpu.roll(small, lanes - 2 * IDENT_ROWS, 1),
        ],
        axis=0,
    )
    norm_grad = table.T[IDENT_USED : IDENT_USED + 4]
    matrix = (MATRIX_RATE, MATRIX_DECAY)
    for c in range(3):
        step = adam_step(
            ins[0][c], ins[1][c], ins[2][c], red2_ref[:, c * half : (c + 1) * half], *matrix, scale
        )
        for out, value in zip(outs[0:3], step):
            out[c] = value
    jobs = (
        (red1_ref[some:, 0 : 2 * half], matrix),
        (red1_ref[:, 2 * half :], matrix),
        (red1_ref[0:some, 0 : 2 * half], matrix),
        (norm_grad, (NORM_RATE, 0.0)),
        (table[:, 0:IDENT_USED], (EMBED_RATE, 0.0)),
    )
    for at, (grad, rates) in enumerate(jobs):
        i = 3 * (at + 1)
        step = adam_step(ins[i][...], ins[i + 1][...], ins[i + 2][...], grad, *rates, scale)
        for out, value in zip(outs[i : i + 3], step):
            out[...] = value


def whole_spec(shape):
    zeros = (0,) * len(shape)
    return pl.BlockSpec(shape, lambda i: zeros, pipeline_mode=pl.Buffered(1))


def lead_spec(*rest):
    return pl.BlockSpec((PAIR,) + rest, lambda i: (i,) + (0,) * len(rest))


def column_spec(rows, slots):
    return pl.BlockSpec((rows, PAIR * slots), lambda i: (0, i))


def costs(flops, moved):
    return pl.CostEstimate(flops=flops, bytes_accessed=moved, transcendentals=0)


def embed(tokens, cotangent, token_types, pairs_t, lap_t, embed_weight, norm_params):
    mols, slots, width = tokens.shape
    toks = mols * slots
    rows = (width, width, 256, width)
    types = (F32, BF16, BF16, BF16)
    return pl.pallas_call(
        embed_kernel,
        grid=(mols // PAIR,),
        out_shape=[jax.ShapeDtypeStruct((r, toks), t) for r, t in zip(rows, types)],
        out_specs=[column_spec(r, slots) for r in rows],
        in_specs=[
            lead_spec(slots, width),
            lead_spec(slots, width),
            lead_spec(1, slots),
            lead_spec(2, slots),
            lead_spec(lap_t.shape[1], lap_t.shape[2]),
            whole_spec(embed_weight.shape),
            whole_spec(norm_params.shape),
        ],
        scratch_shapes=[
            pltpu.VMEM((2, width, slots), F32),
            pltpu.VMEM((IDENT_ROWS, width), F32),
            pltpu.VMEM((width, 256), BF16),
        ],
        compiler_params=pltpu.CompilerParams(vmem_limit_bytes=VMEM_BYTES),
        cost_estimate=costs(8_000_000_000, 10_000_000),
        name="embed",
    )(tokens, cotangent, token_types.reshape(mols, 1, slots), pairs_t, lap_t, embed_weight, norm_params)


def front(lengths, h0, na, cot, norm_params, own, peer, mols):
    width, toks = h0.shape
    slots = toks // mols
    half = width // 2
    heads = width // HEAD_DIM
    owners = 16
    col = column_spec(width, slots)
    weights = []
    for pair in zip(own, peer):
        weights += list(pair)
    gshape = (owners, 2 * half // owners, 3 * half)
    padded = jax.ShapeDtypeStruct((mols, heads * PAD_DIM, slots), BF16)
    outs = [
        (jax.ShapeDtypeStruct((width, toks), F32), col),
        (jax.ShapeDtypeStruct((width, toks), F32), col),
        (jax.ShapeDtypeStruct((width, toks), BF16), whole_spec((width, toks))),
        (padded, lead_spec(heads * PAD_DIM, slots)),
        (padded, lead_spec(heads * PAD_DIM, slots)),
        (padded, lead_spec(heads * PAD_DIM, slots)),
        (padded, lead_spec(heads * PAD_DIM, slots)),
        (jax.ShapeDtypeStruct((mols, heads, slots, slots), BF16), lead_spec(heads, slots, slots)),
        (jax.ShapeDtypeStruct(gshape, BF16), whole_spec(gshape)),
        (jax.ShapeDtypeStruct(gshape, BF16), whole_spec(gshape)),
        (jax.ShapeDtypeStruct((2, width, slots), F32), whole_spec((2, width, slots))),
    ]
    return pl.pallas_call(
        front_kernel,
        grid=(mols // PAIR,),
        out_shape=[o[0] for o in outs],
        out_specs=[o[1] for o in outs],
        in_specs=[
            pl.BlockSpec(memory_space=pltpu.SMEM),
            col,
            col,
            whole_spec(cot.shape),
            whole_spec(norm_params.shape),
        ]
        + [whole_spec(w.shape) for w in weights],
        scratch_shapes=[
            pltpu.VMEM((6 * half, width), BF16),
        ]
        + [pltpu.VMEM((width, width), BF16)] * 5
        + [pltpu.VMEM((2, width, slots), F32)]
        + [pltpu.VMEM((width, toks), BF16)] * 4
        + [pltpu.VMEM((PAIR, width, slots), F32), pltpu.VMEM((width, PAIR * slots), F32)]
        + [pltpu.VMEM((PAIR, heads // 4 + 1, 8, slots), F32)],
        compiler_params=pltpu.CompilerParams(vmem_limit_bytes=VMEM_BYTES),
        cost_estimate=costs(60_000_000_000, 50_000_000),
        name="front",
    )(lengths, h0, na, cot, norm_params, *weights)


def middle(which, na, q, k, v, do, e, got=None, plane=None):
    mols, heads, slots, _ = e.shape
    width, toks = na.shape
    half = width // 2
    rows = heads // 2 * PAD_DIM
    part = pl.BlockSpec((PAIR, rows, slots), lambda i: (i, which, 0))
    gshape = (16, width // 16, 3 * half)
    dx = jax.ShapeDtypeStruct((3 * half, toks), BF16)
    specs = [
        whole_spec(na.shape),
        part,
        part,
        part,
        part,
        pl.BlockSpec((PAIR, heads // 2, slots, slots), lambda i: (i, which, 0, 0)),
    ]
    common = dict(
        grid=(mols // PAIR,),
        compiler_params=pltpu.CompilerParams(vmem_limit_bytes=VMEM_BYTES),
        cost_estimate=costs(20_000_000_000, 12_000_000),
    )
    if got is None:
        return pl.pallas_call(
            middle_kernel,
            out_shape=[dx, jax.ShapeDtypeStruct(gshape, BF16)],
            in_specs=specs,
            out_specs=[whole_spec(dx.shape), whole_spec(gshape)],
            name="middle_peer",
            **common,
        )(na, q, k, v, do, e)
    piece = (4,) + gshape[1:]
    return pl.pallas_call(
        middle_own_kernel,
        out_shape=[dx] + [jax.ShapeDtypeStruct(piece, BF16)] * 4,
        in_specs=[pl.BlockSpec(memory_space=pltpu.SMEM)] + specs + [whole_spec(gshape)],
        out_specs=[whole_spec(dx.shape)] + [whole_spec(piece)] * 4,
        scratch_shapes=[pltpu.VMEM(gshape, BF16)],
        name="middle_own",
        **common,
    )(plane, na, q, k, v, do, e, got)


def back(dxo, dxp, qkv_o, qkv_p, h0, gh1, fs, gain, lnb, h1, act, down_o, down_p, mols, packed):
    width, toks = h0.shape
    slots = toks // mols
    col = column_spec(width, slots)
    dxs = column_spec(dxo.shape[0], slots)
    small = (width // 24, 8, slots) if packed else (width, slots)
    return pl.pallas_call(
        back_kernel,
        grid=(mols // PAIR,),
        out_shape=[
            jax.ShapeDtypeStruct((mols, slots, width), F32),
            jax.ShapeDtypeStruct((mols, slots, width), BF16),
            jax.ShapeDtypeStruct(small, F32),
        ],
        in_specs=[
            dxs,
            dxs,
            whole_spec(qkv_o.shape),
            whole_spec(qkv_p.shape),
            col,
            col,
            column_spec(fs.shape[0], slots),
            whole_spec(gain.shape),
            whole_spec(lnb.shape),
            col,
            col,
            whole_spec(down_o.shape),
            whole_spec(down_p.shape),
        ],
        out_specs=[lead_spec(slots, width), lead_spec(slots, width), whole_spec(small)],
        scratch_shapes=[
            pltpu.VMEM((width, slots), F32),
            pltpu.VMEM((2, width, slots), F32),
            pltpu.VMEM((width, fs.shape[0]), F32),
            pltpu.VMEM((width, 3 * width), BF16),
            pltpu.VMEM((width, width), BF16),
        ],
        compiler_params=pltpu.CompilerParams(vmem_limit_bytes=VMEM_BYTES),
        cost_estimate=costs(18_000_000_000, 15_000_000),
        name="back",
    )(dxo, dxp, qkv_o, qkv_p, h0, gh1, fs, gain, lnb, h1, act, down_o, down_p)


def first_sum(got):
    rows, columns = got.shape[1:]
    return pl.pallas_call(
        first_kernel,
        out_shape=[
            jax.ShapeDtypeStruct((rows, columns), F32),
            jax.ShapeDtypeStruct((1, 128), F32),
        ],
        compiler_params=pltpu.CompilerParams(vmem_limit_bytes=VMEM_BYTES),
        cost_estimate=costs(1_000_000, 2_000_000),
        name="first_sum",
    )(got)


def gather(own2, others2, got, squares):
    rows, columns = own2.shape
    lanes = got.shape[2]
    return pl.pallas_call(
        gather_kernel,
        out_shape=[
            jax.ShapeDtypeStruct((rows, columns), F32),
            jax.ShapeDtypeStruct(got.shape[1:], F32),
            jax.ShapeDtypeStruct((got.shape[0], lanes), F32),
        ],
        compiler_params=pltpu.CompilerParams(vmem_limit_bytes=VMEM_BYTES),
        name="gather",
    )(own2, *others2, got, squares)


def adam_all(squares, red1, red2, small, state):
    return pl.pallas_call(
        adam_kernel,
        out_shape=[jax.ShapeDtypeStruct((1, squares.shape[1]), F32)]
        + [jax.ShapeDtypeStruct(a.shape, F32) for a in state],
        compiler_params=pltpu.CompilerParams(vmem_limit_bytes=VMEM_BYTES),
        name="adam",
    )(squares, red1, red2, small, *state)


def swap(value):
    return lax.ppermute(value, "mp", [(0, 1), (1, 0)])


def hop(value, flip):
    size = lax.axis_size("dp")
    return lax.ppermute(value, "dp", [(i, i ^ flip) for i in range(size)])


def take(value, index, axis=0):
    return lax.dynamic_index_in_dim(value, index, axis, keepdims=False)


def adam_step(master, mean_old, square_old, gradient, rate, decay, clip_scale):
    clipped = gradient * clip_scale
    mean_new = BETA_FIRST * mean_old + (1.0 - BETA_FIRST) * clipped
    square_new = BETA_SECOND * square_old + (1.0 - BETA_SECOND) * clipped * clipped
    mean_hat = mean_new / (1.0 - BETA_FIRST**STEP)
    square_hat = square_new / (1.0 - BETA_SECOND**STEP)
    updated = master - rate * (mean_hat / (jnp.sqrt(square_hat) + ADAM_EPS) + decay * master)
    return (updated, mean_new, square_new)


def on_device(
    tokens,
    cotangent,
    lengths,
    token_types,
    node_pairs,
    laplacian,
    qkv_weight,
    out_weight,
    up_weight,
    down_weight,
    qkv_master,
    qkv_mean,
    qkv_square,
    out_master,
    out_mean,
    out_square,
    up_master,
    up_mean,
    up_square,
    down_master,
    down_mean,
    down_square,
    norm_params,
    norm_mean,
    norm_square,
    embed_weight,
    embed_mean,
    embed_square,
):
    mols, slots, width = tokens.shape
    half = width // 2
    dp_size = lax.axis_size("dp")
    mp_size = lax.axis_size("mp")
    idents = embed_weight.shape[0]

    own = (qkv_weight.transpose(1, 0, 2), out_weight, up_weight, down_weight)
    peer = tuple(swap(w) for w in own)

    world = dp_size * mp_size
    shard_width = width // world
    fits = dp_size == 16 and shard_width == 24

    h0, na, fs, cot = embed(
        tokens,
        cotangent,
        token_types,
        node_pairs.transpose(0, 2, 1),
        laplacian.transpose(0, 2, 1),
        embed_weight,
        norm_params,
    )
    (gh1, h1, act, q, k, v, do, e, gown1, gpeer1, lnb) = front(
        lengths, h0, na, cot, norm_params, own, peer, mols
    )
    got1 = swap(gpeer1)
    dxp, gpeer2 = middle(1, na, q, k, v, do, e)
    got1, dxp = lax.optimization_barrier((got1, dxp))
    sum1 = (gown1.astype(F32) + got1.astype(F32)).astype(BF16)
    got2 = swap(gpeer2)
    sum1, do = lax.optimization_barrier((sum1, do))
    if fits:
        got1 = lax.all_to_all(sum1, "dp", 0, 0, tiled=True)
    index = lax.axis_index("dp")
    plane, line = (index & 3, index >> 2) if fits else (jnp.int32(0), None)
    dxo, *pieces = middle(0, na, q, k, v, do, e, got2, plane.reshape(1))
    if fits:
        pieces, dxo = lax.optimization_barrier((pieces, dxo))
        near = [hop(piece, k) for piece, k in zip(pieces[1:], (1, 2, 3))]
    input_grad, output, small = back(
        dxo,
        dxp,
        own[0],
        peer[0],
        h0,
        gh1,
        fs,
        norm_params,
        lnb,
        h1,
        act,
        own[3],
        peer[3],
        mols,
        fits,
    )

    shard_index = index * mp_size + lax.axis_index("mp")
    norm_own = lax.dynamic_slice_in_dim(norm_params, shard_index * shard_width, shard_width, 1)
    embed_own = lax.dynamic_slice_in_dim(embed_weight, shard_index * shard_width, shard_width, 1)
    flip = lambda a: a.transpose(1, 0, 2)
    if fits:
        small, got1 = lax.optimization_barrier((small, got1))
        got = lax.all_to_all(small, ("dp", "mp"), 0, 0, tiled=True)
        red1, squares1 = first_sum(got1)
        plane_sum = pieces[0].astype(F32)
        for piece in near:
            plane_sum = plane_sum + piece.astype(F32)
        plane_sum = plane_sum.astype(BF16)
        far = [hop(take(plane_sum, line ^ k), 4 * k) for k in (1, 2, 3)]
        red2, small_own, squares = gather(take(plane_sum, line), far, got, squares1)
        lanes = squares.shape[1]
        squares = lax.all_to_all(squares.reshape(world, 1, lanes), ("dp", "mp"), 0, 0, tiled=True)
        state = (
            (flip(qkv_master), flip(qkv_mean), flip(qkv_square))
            + (out_master, out_mean, out_square)
            + (up_master, up_mean, up_square)
            + (down_master, down_mean, down_square)
            + (norm_own, norm_mean, norm_square)
            + (embed_own.T, embed_mean.T, embed_square.T)
        )
        clip, *new = adam_all(squares.reshape(world, lanes), red1, red2, small_own, state)
        new = [flip(a) for a in new[0:3]] + list(new[3:15]) + [a.T for a in new[15:18]]
        return (output, input_grad, clip[0, 0]) + tuple(new)

    some = half // 16
    scatter = partial(lax.psum_scatter, axis_name="dp", scatter_dimension=0, tiled=True)
    sum1 = sum1.astype(F32)
    sum2 = jnp.stack(pieces, axis=1).astype(F32)
    reduced_down = scatter(sum1[:, 0:some, 0:width].reshape(half, width))
    reduced_out = scatter(sum1[:, some:, 0:width].reshape(half, width))
    reduced_up = scatter(sum1[:, :, width:].reshape(width, half))
    reduced_qkv = scatter(sum2.reshape(width, 3, half))
    small = small[:, : idents + 4].reshape(world, shard_width, idents + 4)
    small_own = jnp.sum(lax.all_to_all(small, ("dp", "mp"), 0, 0, tiled=True), axis=0).T
    reduced = (reduced_qkv, reduced_out, reduced_up, reduced_down, small_own[idents:], small_own[:idents])
    own_square = sum(jnp.sum(piece * piece) for piece in reduced)
    clip_norm = jnp.sqrt(lax.psum(own_square, ("dp", "mp")))
    clip_scale = jnp.minimum(1.0, CLIP_LIMIT / (clip_norm + 1e-06))
    state = (
        (qkv_master, qkv_mean, qkv_square, MATRIX_RATE, MATRIX_DECAY),
        (out_master, out_mean, out_square, MATRIX_RATE, MATRIX_DECAY),
        (up_master, up_mean, up_square, MATRIX_RATE, MATRIX_DECAY),
        (down_master, down_mean, down_square, MATRIX_RATE, MATRIX_DECAY),
        (norm_own, norm_mean, norm_square, NORM_RATE, 0.0),
        (embed_own, embed_mean, embed_square, EMBED_RATE, 0.0),
    )
    new = ()
    for (master, mean, square, rate, decay), grad in zip(state, reduced):
        new += adam_step(master, mean, square, grad, rate, decay, clip_scale)
    return (output, input_grad, clip_norm) + new


def solution(mesh):
    tokens = P(("dp", "mp"), None, None)
    qkv = P("dp", None, "mp")
    rows = P(("mp", "dp"), None)
    both = P("dp", "mp")
    small = P(None, ("dp", "mp"))
    return jax.shard_map(
        on_device,
        mesh=mesh,
        in_specs=(
            tokens,
            tokens,
            P(("dp", "mp")),
            P(("dp", "mp"), None),
            tokens,
            tokens,
            P(None, None, "mp"),
            P("mp", None),
            P(None, "mp"),
            P("mp", None),
        )
        + (qkv,) * 3
        + (rows,) * 3
        + (both,) * 3
        + (rows,) * 3
        + (P(), small, small) * 2,
        out_specs=(tokens, tokens, P())
        + (qkv,) * 3
        + (rows,) * 3
        + (both,) * 3
        + (rows,) * 3
        + (small,) * 6,
        check_vma=False,
    )
```

```python
from functools import partial
import math

import jax
import jax.numpy as jnp
from jax import lax
from jax.experimental import pallas as pl
from jax.experimental.pallas import tpu as pltpu
from jax.sharding import PartitionSpec as P

HEAD_DIM = 24
PAD_DIM = 32
STEP = 10
NORM_EPS = 1e-05
BETA_FIRST = 0.9
BETA_SECOND = 0.95
ADAM_EPS = 1e-08
MATRIX_RATE = 0.03
NORM_RATE = 0.5
EMBED_RATE = 0.05
MATRIX_DECAY = 0.1
CLIP_LIMIT = 1.0
MASK_VALUE = -1e30
SCORE_SCALE = 1.0 / math.sqrt(HEAD_DIM)
LOG2E = 1.4426950408889634
LN2 = 0.6931471805599453
IDENT_ROWS = 40
IDENT_USED = 34
PAIR = 2
VMEM_BYTES = 60 * 1024 * 1024
FRONT_UNROLL = 8
MIDDLE_UNROLL = 8

F32 = jnp.float32
BF16 = jnp.bfloat16


def dot_nn(lhs, rhs):
    return lax.dot_general(lhs, rhs, (((1,), (0,)), ((), ())), preferred_element_type=F32)


def dot_nt(lhs, rhs):
    return lax.dot_general(lhs, rhs, (((1,), (1,)), ((), ())), preferred_element_type=F32)


def norm_parts(values):
    scale = 1.0 / values.shape[0]
    centred = values - jnp.sum(values, axis=0, keepdims=True) * scale
    spread = jnp.sum(centred * centred, axis=0, keepdims=True) * scale
    return centred, lax.rsqrt(spread + NORM_EPS)


def gelu_parts(x):
    size = jnp.abs(x)
    bell = jnp.exp2((-0.5 * LOG2E) * (x * x))
    t = 1.0 / (1.0 + (0.3275911 / math.sqrt(2.0)) * size)
    poly = t * (
        0.5 * 0.254829592
        + t
        * (
            0.5 * -0.284496736
            + t * (0.5 * 1.421413741 + t * (0.5 * -1.453152027 + t * (0.5 * 1.061405429)))
        )
    )
    tail = poly * bell
    share = jnp.where(x < 0.0, tail, 1.0 - tail)
    return x * share, share + x * bell * (1.0 / math.sqrt(2.0 * math.pi))


def head_rows(values, tail):
    heads = values.shape[0] // HEAD_DIM
    cut = values.reshape(heads, HEAD_DIM, values.shape[1])
    tails = jnp.broadcast_to(tail[None], (heads,) + tail.shape)
    return jnp.concatenate([cut, tails], axis=1).reshape(heads * PAD_DIM, values.shape[1])


def block_columns(rows):
    zero = jnp.zeros((PAD_DIM, rows.shape[1]), rows.dtype)
    columns = []
    for head in range(4):
        pieces = [zero] * 4
        pieces[head] = rows[head * PAD_DIM : (head + 1) * PAD_DIM]
        columns.append(jnp.concatenate(pieces, axis=0))
    return jnp.concatenate(columns, axis=1)


def lane_columns(row, slots):
    return jnp.broadcast_to(row, (slots, row.shape[1])).T


def embed_kernel(
    tok_ref,
    cot_ref,
    typ_ref,
    pair_ref,
    lap_ref,
    embed_ref,
    norm_ref,
    h0_ref,
    na_ref,
    fs_ref,
    ct_ref,
    nb,
    rows,
    est,
):
    slots = tok_ref.shape[1]
    width = tok_ref.shape[2]

    @pl.when(pl.program_id(0) == 0)
    def _():
        for row in range(2):
            nb[row] = lane_columns(norm_ref[row : row + 1, :], slots)
        rows[...] = jnp.zeros_like(rows)
        rows[0 : embed_ref.shape[0], :] = embed_ref[...]
        whole = rows[...]
        e1 = whole.astype(BF16).astype(F32)
        e2 = (whole - e1).astype(BF16).astype(F32)
        e3 = whole - e1 - e2
        blank = jnp.zeros((8, width), F32)
        stacked = jnp.concatenate([e1, e2, e3, blank, e1, e2, e1, blank], axis=0)
        est[...] = stacked.T.astype(BF16)

    node_iota = lax.broadcasted_iota(jnp.int32, (lap_ref.shape[2], slots), 0)
    row_iota = lax.broadcasted_iota(jnp.int32, (8, slots), 0)
    for j in range(PAIR):
        lanes = slice(j * slots, (j + 1) * slots)
        lap = lap_ref[j]
        lap1 = lap.astype(BF16)
        rest = lap - lap1.astype(F32)
        lap2 = rest.astype(BF16)
        lap3 = (rest - lap2.astype(F32)).astype(BF16)
        laps = jnp.concatenate([lap1.astype(F32), lap2.astype(F32), lap3.astype(F32)], axis=0)
        laps = laps.astype(BF16)
        left = jnp.where(node_iota == pair_ref[j, 0:1, :], 1.0, 0.0).astype(BF16)
        right = jnp.where(node_iota == pair_ref[j, 1:2, :], 1.0, 0.0).astype(BF16)
        lf = dot_nn(laps, left)
        rf = dot_nn(laps, right)
        types = typ_ref[j]
        kinds = jnp.where((row_iota < 2) & (row_iota == types), 1.0, 0.0)
        none = jnp.zeros((8, slots), F32)
        ident = lap.shape[0]
        f1 = jnp.concatenate([lf[0:ident], rf[0:ident], kinds], axis=0)
        f2 = jnp.concatenate([lf[ident : 2 * ident], rf[ident : 2 * ident], none], axis=0)
        f3 = jnp.concatenate([lf[2 * ident :], rf[2 * ident :], none], axis=0)
        stack = jnp.concatenate([f1, f1, f1, none, f2, f2, f3, none], axis=0).astype(BF16)
        fs_ref[:, lanes] = stack
        h0 = tok_ref[j].T.astype(F32) + dot_nn(est[...], stack)
        h0_ref[:, lanes] = h0
        centred, rec = norm_parts(h0)
        na_ref[:, lanes] = (centred * rec * nb[0] + nb[1]).astype(BF16)
        ct_ref[:, lanes] = cot_ref[j].T


def block_pair(rows):
    zero = jnp.zeros((PAD_DIM, rows.shape[1]), rows.dtype)
    left = jnp.concatenate([rows[0:PAD_DIM], zero], axis=0)
    right = jnp.concatenate([zero, rows[PAD_DIM:]], axis=0)
    return jnp.concatenate([left, right], axis=1)


def staged(at, first, second, third):
    one, two = {}, {}
    count = len(at)
    for n in range(count + 2):
        if n < count:
            one[n] = first(*at[n])
        if 0 <= n - 1 < count:
            two[n - 1] = second(*at[n - 1], one.pop(n - 1))
        if 0 <= n - 2 < count:
            third(*at[n - 2], two.pop(n - 2))


def front_kernel(
    len_ref,
    h0_ref,
    na_ref,
    cot_s,
    norm_ref,
    qkv_o,
    qkv_p,
    out_o,
    out_p,
    up_o,
    up_p,
    down_o,
    down_p,
    gh1_ref,
    h1_s,
    act_s,
    q_ref,
    k_ref,
    v_ref,
    do_ref,
    e_ref,
    gown_ref,
    gpeer_ref,
    lnacc_ref,
    qkvt,
    outt,
    upt,
    outw,
    upw,
    downw,
    nb,
    nbt_s,
    gp_s,
    mix_s,
    ga_s,
    mixf,
    nrm_s,
    rec_s,
):
    step = pl.program_id(0)
    steps = pl.num_programs(0)
    slots = e_ref.shape[2]
    width = h0_ref.shape[0]
    half = width // 2
    halves = ((qkv_o, out_o, up_o, down_o), (qkv_p, out_p, up_p, down_p))

    @pl.when(step == 0)
    def _():
        for h, (qkv, out, up, down) in enumerate(halves):
            part = slice(h * half, (h + 1) * half)
            for c in range(3):
                at = (3 * h + c) * half
                qkvt[at : at + half, :] = qkv[c].T
            outt[:, part] = out[...].T
            upt[part, :] = up[...].T
            outw[part, :] = out[...]
            upw[:, part] = up[...]
            downw[part, :] = down[...]
        for row in range(2):
            nb[row] = lane_columns(norm_ref[row + 2 : row + 3, :], slots)
        lnacc_ref[...] = jnp.zeros_like(lnacc_ref)

    base = pl.multiple_of(step * PAIR * slots, PAIR * slots)
    span = pl.ds(base, PAIR * slots)

    phase = pl.when(step >= 0)
    groups = width // (4 * HEAD_DIM)
    inv = 1.0 / width
    parts = tuple(slice(h * half, (h + 1) * half) for h in range(2))
    sides = tuple(slice(j * slots, (j + 1) * slots) for j in range(PAIR))
    columns = tuple(
        pl.ds(pl.multiple_of(base + j * slots, slots), slots) for j in range(PAIR)
    )

    @phase
    def _():
        row_iota = lax.broadcasted_iota(jnp.int32, (8, slots), 0)
        lane_iota = lax.broadcasted_iota(jnp.int32, (1, slots), 1)
        one_row = jnp.where(row_iota == 0, 1.0, 0.0)
        two_rows = jnp.where(row_iota < 2, 1.0, 0.0)
        padded = half // HEAD_DIM * PAD_DIM
        for h in range(2):
            rows = slice(h * padded, (h + 1) * padded)
            for c, ref in enumerate((q_ref, k_ref, v_ref)):
                at = (3 * h + c) * half
                proj = dot_nn(qkvt[at : at + half, :], na_ref[...])
                for j in range(PAIR):
                    own = proj[:, sides[j]]
                    if c == 0:
                        own, tail = own * (SCORE_SCALE * LOG2E), one_row
                    elif c == 1:
                        length = len_ref[step * PAIR + j]
                        bias = jnp.where(lane_iota < length, 0.0, MASK_VALUE)
                        tail = jnp.where(row_iota == 0, bias, 0.0)
                    else:
                        tail = two_rows
                    ref[j, rows, :] = head_rows(own, tail).astype(BF16)

    def score(j, g):
        rows = pl.ds(pl.multiple_of(g * 4 * PAD_DIM, 4 * PAD_DIM), 4 * PAD_DIM)
        return dot_nn(k_ref[j, rows, :].T, block_columns(q_ref[j, rows, :]))

    def weigh(j, g, scores):
        exps = []
        for a in range(4):
            own = scores[:, a * slots : (a + 1) * slots]
            ex = jnp.exp2(own - jnp.max(own, axis=0, keepdims=True)).astype(BF16)
            e_ref[j, g * 4 + a] = ex
            exps.append(ex)
        return exps

    def mix_values(j, g, exps):
        rows = pl.ds(pl.multiple_of(g * 4 * PAD_DIM, 4 * PAD_DIM), 4 * PAD_DIM)
        vals = v_ref[j, rows, :]
        mixes = []
        for a in range(0, 4, 2):
            two = dot_nn(
                vals[a * PAD_DIM : (a + 2) * PAD_DIM], jnp.concatenate(exps[a : a + 2], axis=1)
            )
            for b in range(2):
                got = two[b * PAD_DIM : (b + 1) * PAD_DIM, b * slots : (b + 1) * slots]
                rec = 1.0 / got[HEAD_DIM : HEAD_DIM + 1]
                rec_s[j, g, a + b : a + b + 1, :] = rec
                mixes.append(got[0:HEAD_DIM] * rec)
        out_rows = pl.ds(pl.multiple_of(g * 4 * HEAD_DIM, 4 * HEAD_DIM), 4 * HEAD_DIM)
        mixf[j, out_rows, :] = jnp.concatenate(mixes, axis=0)

    def attend(i, carry):
        at = [i * FRONT_UNROLL + u for u in range(FRONT_UNROLL)]
        at = [(lax.div(n, groups), lax.rem(n, groups)) for n in at]
        staged(at, score, weigh, mix_values)
        return carry

    lax.fori_loop(0, PAIR * groups // FRONT_UNROLL, attend, 0)

    @phase
    def _():
        for j in range(PAIR):
            mix_s[:, columns[j]] = mixf[j].astype(BF16)
        attn = jnp.concatenate([dot_nn(outt[part, :], mix_s[:, span]) for part in parts], axis=0)
        for j in range(PAIR):
            h1 = h0_ref[:, sides[j]] + attn[:, sides[j]]
            h1_s[:, sides[j]] = h1
            centred, rec = norm_parts(h1)
            unit = centred * rec
            nrm_s[:, sides[j]] = unit
            rec_s[j, groups, 0:1, :] = rec
            nbt_s[:, columns[j]] = (unit * nb[0] + nb[1]).astype(BF16)

    @phase
    def _():
        for part in parts:
            act, slope = gelu_parts(dot_nn(upt[part, :], nbt_s[:, span]))
            act_s[part, span] = act.astype(BF16)
            back = dot_nn(downw[part, :], cot_s[:, span])
            gp_s[part, span] = (back * slope).astype(BF16)

    @phase
    def _():
        grad_b = jnp.concatenate([dot_nn(upw[part, :], gp_s[:, span]) for part in parts], axis=0)
        for j in range(PAIR):
            gb = grad_b[:, sides[j]]
            unit = nrm_s[:, sides[j]]
            lnacc_ref[0] += gb * unit
            lnacc_ref[1] += gb
            f = gb * nb[0]
            f_mean = jnp.sum(f, axis=0, keepdims=True) * inv
            fn_mean = jnp.sum(f * unit, axis=0, keepdims=True) * inv
            gh1 = cot_s[:, columns[j]].astype(F32) + rec_s[j, groups, 0:1, :] * (
                f - f_mean - unit * fn_mean
            )
            gh1_ref[:, sides[j]] = gh1
            ga_s[:, columns[j]] = gh1.astype(BF16)

    @phase
    def _():
        rows8 = lax.broadcasted_iota(jnp.int32, (4, 8, slots), 1)
        for h, part in enumerate(parts):
            gm = dot_nn(outw[part, :], ga_s[:, span])
            for j in range(PAIR):
                for g in range(groups // 2):
                    at = h * (groups // 2) + g
                    grad = gm[g * 96 : (g + 1) * 96, sides[j]].reshape(4, HEAD_DIM, slots)
                    mixed = mixf[j, at * 96 : (at + 1) * 96, :].reshape(4, HEAD_DIM, slots)
                    rec = rec_s[j, at].reshape(8, 1, slots)[0:4]
                    inner = -(jnp.sum(grad * mixed, axis=1, keepdims=True) * rec)
                    high = inner.astype(BF16).astype(F32)
                    low = inner - high
                    tail = jnp.where(rows8 == 0, high, jnp.where(rows8 == 1, low, 0.0))
                    full = jnp.concatenate([grad * rec, tail], axis=1)
                    do_ref[j, at * 128 : (at + 1) * 128, :] = (
                        full.reshape(4 * PAD_DIM, slots).astype(BF16)
                    )

    @pl.when(step == steps - 1)
    def _():
        owners = gown_ref.shape[0]
        some = half // owners
        for h, g_ref in enumerate((gown_ref, gpeer_ref)):
            rows = slice(h * half, (h + 1) * half)
            gdown = dot_nt(act_s[rows, :], cot_s[...])
            gout = dot_nt(mix_s[rows, :], ga_s[...])
            for o in range(owners):
                both = jnp.concatenate(
                    [gdown[o * some : (o + 1) * some], gout[o * some : (o + 1) * some]], axis=0
                )
                g_ref[o, :, 0:width] = both.astype(g_ref.dtype)
            gup = dot_nt(nbt_s[...], gp_s[rows, :])
            g_ref[:, :, width:] = gup.reshape(owners, 2 * some, half).astype(g_ref.dtype)


def middle_kernel(na_ref, q_ref, k_ref, v_ref, do_ref, e_ref, dx_ref, g_ref):
    attention_back(q_ref, k_ref, v_ref, do_ref, e_ref, dx_ref)
    half = dx_ref.shape[0] // 3

    @pl.when(pl.program_id(0) == pl.num_programs(0) - 1)
    def _():
        for c in range(3):
            cut = slice(c * half, (c + 1) * half)
            grad = dot_nt(na_ref[...], dx_ref[cut, :])
            g_ref[:, :, cut] = grad.reshape(g_ref.shape[0:2] + (half,)).astype(BF16)


def middle_own_kernel(
    plane_ref, na_ref, q_ref, k_ref, v_ref, do_ref, e_ref, got_ref, dx_ref, g0, g1, g2, g3, total
):
    attention_back(q_ref, k_ref, v_ref, do_ref, e_ref, dx_ref)
    half = dx_ref.shape[0] // 3

    @pl.when(pl.program_id(0) == pl.num_programs(0) - 1)
    def _():
        for c in range(3):
            cut = slice(c * half, (c + 1) * half)
            grad = dot_nt(na_ref[...], dx_ref[cut, :]).reshape(total.shape[0:2] + (half,))
            total[:, :, cut] = (grad + got_ref[:, :, cut].astype(F32)).astype(BF16)
        plane = plane_ref[0]
        for k, g_ref in enumerate((g0, g1, g2, g3)):
            for line in range(4):
                g_ref[line] = total[line * 4 + (plane ^ k)]


def attention_back(q_ref, k_ref, v_ref, do_ref, e_ref, dx_ref):
    step = pl.program_id(0)
    slots = q_ref.shape[2]
    half = dx_ref.shape[0] // 3
    base = pl.multiple_of(step * PAIR * slots, PAIR * slots)
    groups = half // (4 * HEAD_DIM)

    def rows_of(g):
        return pl.ds(pl.multiple_of(g * 4 * PAD_DIM, 4 * PAD_DIM), 4 * PAD_DIM)

    def score(j, g):
        return dot_nn(v_ref[j, rows_of(g), :].T, block_columns(do_ref[j, rows_of(g), :]))

    def weigh(j, g, back):
        grads = []
        for a in range(4):
            ex = e_ref[j, g * 4 + a].astype(F32)
            grads.append((ex * back[:, a * slots : (a + 1) * slots]).astype(BF16))
        return grads

    def products(j, g, grads):
        dos = do_ref[j, rows_of(g), :]
        qs = q_ref[j, rows_of(g), :]
        ks = k_ref[j, rows_of(g), :]
        dq, dk, dv = [], [], []
        for a in range(0, 4, 2):
            cut = slice(a * PAD_DIM, (a + 2) * PAD_DIM)
            both = jnp.concatenate(grads[a : a + 2], axis=1)
            exps = jnp.concatenate([e_ref[j, g * 4 + a + b].T for b in range(2)], axis=1)
            two = dot_nn(ks[cut], both)
            dq.append(two[0:HEAD_DIM, 0:slots])
            dq.append(two[PAD_DIM : PAD_DIM + HEAD_DIM, slots:])
            two = dot_nt(block_pair(qs[cut]), both)
            dk.append(two[0:HEAD_DIM])
            dk.append(two[PAD_DIM : PAD_DIM + HEAD_DIM])
            two = dot_nn(dos[cut], exps)
            dv.append(two[0:HEAD_DIM, 0:slots])
            dv.append(two[PAD_DIM : PAD_DIM + HEAD_DIM, slots:])
        cols = pl.ds(pl.multiple_of(base + j * slots, slots), slots)
        for c, (parts, scale) in enumerate(((dq, SCORE_SCALE), (dk, LN2), (dv, None))):
            at = pl.ds(pl.multiple_of(c * half + g * 96, 32), 96)
            whole = jnp.concatenate(parts, axis=0)
            if scale is not None:
                whole = whole * scale
            dx_ref[at, cols] = whole.astype(BF16)

    def attend(i, carry):
        at = [i * MIDDLE_UNROLL + u for u in range(MIDDLE_UNROLL)]
        at = [(lax.div(n, groups), lax.rem(n, groups)) for n in at]
        staged(at, score, weigh, products)
        return carry

    lax.fori_loop(0, PAIR * groups // MIDDLE_UNROLL, attend, 0)


def output_kernel(h1_ref, act_ref, down_o, down_p, output_ref, downt):
    slots = output_ref.shape[1]
    half = down_o.shape[0]

    @pl.when(pl.program_id(0) == 0)
    def _():
        for h, down in enumerate((down_o, down_p)):
            downt[:, h * half : (h + 1) * half] = down[...].T

    ffn = [dot_nn(downt[h * half : (h + 1) * half, :], act_ref[...]) for h in range(2)]
    ffn = jnp.concatenate(ffn, axis=0)
    for j in range(PAIR):
        lanes = slice(j * slots, (j + 1) * slots)
        output_ref[j] = (h1_ref[:, lanes] + ffn[:, lanes]).astype(BF16).T


def back_kernel(
    dxo_ref,
    dxp_ref,
    qkv_o,
    qkv_p,
    h0_ref,
    gh1_ref,
    fs_ref,
    gain_ref,
    lnb_ref,
    ig_ref,
    small_ref,
    nb,
    lnacc,
    ge,
    qkvw,
):
    step = pl.program_id(0)
    slots = ig_ref.shape[1]
    width = ig_ref.shape[2]
    half = width // 2
    inv = 1.0 / width

    @pl.when(step == 0)
    def _():
        lnacc[...] = jnp.zeros_like(lnacc)
        ge[...] = jnp.zeros_like(ge)
        nb[...] = lane_columns(gain_ref[0:1, :], slots)
        for h, qkv in enumerate((qkv_o, qkv_p)):
            for c in range(3):
                at = (3 * h + c) * half
                qkvw[:, at : at + half] = qkv[c]

    units = []
    for j in range(PAIR):
        centred, rec = norm_parts(h0_ref[:, j * slots : (j + 1) * slots])
        units.append((centred * rec, rec))
    dxs = jnp.concatenate([dxo_ref[...], dxp_ref[...]], axis=0)
    total = jnp.concatenate([dot_nn(qkvw[0:half, :], dxs), dot_nn(qkvw[half:, :], dxs)], axis=0)
    highs, lows = [], []
    for j in range(PAIR):
        lanes = slice(j * slots, (j + 1) * slots)
        ga = total[:, lanes]
        unit, rec = units[j]
        lnacc[0] += ga * unit
        lnacc[1] += ga
        f = ga * nb[...]
        f_mean = jnp.sum(f, axis=0, keepdims=True) * inv
        fn_mean = jnp.sum(f * unit, axis=0, keepdims=True) * inv
        ig = gh1_ref[:, lanes] + rec * (f - f_mean - unit * fn_mean)
        ig_ref[j] = ig.T
        high = ig.astype(BF16)
        highs.append(high)
        lows.append((ig - high.astype(F32)).astype(BF16))
    fs = fs_ref[...]
    ge[...] += dot_nt(jnp.concatenate(highs, axis=1), fs) + dot_nt(
        jnp.concatenate(lows, axis=1), fs
    )

    @pl.when(step == pl.num_programs(0) - 1)
    def _():
        lane = lax.broadcasted_iota(jnp.int32, (width, slots), 1)
        rows = ge[:, 0:slots] + ge[:, slots:]
        sums = (lnacc[0], lnacc[1], lnb_ref[0], lnb_ref[1])
        for at, part in enumerate(sums):
            rows = jnp.where(lane == IDENT_USED + at, jnp.sum(part, axis=1, keepdims=True), rows)
        rows = jnp.where(lane < IDENT_ROWS, rows, 0.0)
        if small_ref.shape[0] == width:
            small_ref[...] = rows
        else:
            cut = rows.reshape(small_ref.shape[0], 3, 8, slots)
            flat = (small_ref.shape[0] * 8, slots)
            packed = cut[:, 0].reshape(flat)
            packed = packed + pltpu.roll(cut[:, 1].reshape(flat), IDENT_ROWS, 1)
            packed = packed + pltpu.roll(cut[:, 2].reshape(flat), 2 * IDENT_ROWS, 1)
            small_ref[...] = packed.reshape(small_ref.shape)


def square_sum(value, lanes):
    both = value * value
    folded = both[:, 0:lanes]
    for c in range(1, both.shape[1] // lanes):
        folded = folded + both[:, c * lanes : (c + 1) * lanes]
    return jnp.sum(folded, axis=0, keepdims=True)


def gather_kernel(*refs):
    firsts, seconds, got_ref = refs[0:4], refs[4:8], refs[8]
    red1_ref, red2_ref, small_ref, sq_ref = refs[9:]
    lanes = sq_ref.shape[1]
    rows = None
    for refs4, red_ref in ((firsts, red1_ref), (seconds, red2_ref)):
        red = refs4[0][...].astype(F32)
        for ref in refs4[1:]:
            red = red + ref[...].astype(F32)
        red_ref[...] = red
        part = square_sum(red, lanes)
        rows = part if rows is None else rows + part
    small = got_ref[0]
    for o in range(1, got_ref.shape[0]):
        small = small + got_ref[o]
    small_ref[...] = small
    rows = rows + square_sum(small, lanes)
    sq_ref[...] = jnp.full(sq_ref.shape, jnp.sum(rows), F32)


def adam_kernel(*refs):
    sq_ref, red1_ref, red2_ref, small_ref = refs[0:4]
    ins, clip_ref, outs = refs[4:22], refs[22], refs[23:41]
    total = jnp.sum(sq_ref[...], axis=0, keepdims=True)
    clip = jnp.sqrt(total)
    clip_ref[...] = clip
    scale = jnp.max(jnp.minimum(1.0, CLIP_LIMIT / (clip + 1e-06)))
    half = red2_ref.shape[1] // 3
    some = red1_ref.shape[0] // 2
    lanes = small_ref.shape[1]
    small = small_ref[...]
    table = jnp.concatenate(
        [
            small,
            pltpu.roll(small, lanes - IDENT_ROWS, 1),
            pltpu.roll(small, lanes - 2 * IDENT_ROWS, 1),
        ],
        axis=0,
    )
    norm_grad = table.T[IDENT_USED : IDENT_USED + 4]
    matrix = (MATRIX_RATE, MATRIX_DECAY)
    for c in range(3):
        step = adam_step(
            ins[0][c], ins[1][c], ins[2][c], red2_ref[:, c * half : (c + 1) * half], *matrix, scale
        )
        for out, value in zip(outs[0:3], step):
            out[c] = value
    jobs = (
        (red1_ref[some:, 0 : 2 * half], matrix),
        (red1_ref[:, 2 * half :], matrix),
        (red1_ref[0:some, 0 : 2 * half], matrix),
        (norm_grad, (NORM_RATE, 0.0)),
        (table[:, 0:IDENT_USED], (EMBED_RATE, 0.0)),
    )
    for at, (grad, rates) in enumerate(jobs):
        i = 3 * (at + 1)
        step = adam_step(ins[i][...], ins[i + 1][...], ins[i + 2][...], grad, *rates, scale)
        for out, value in zip(outs[i : i + 3], step):
            out[...] = value


def whole_spec(shape):
    zeros = (0,) * len(shape)
    return pl.BlockSpec(shape, lambda i: zeros, pipeline_mode=pl.Buffered(1))


def lead_spec(*rest):
    return pl.BlockSpec((PAIR,) + rest, lambda i: (i,) + (0,) * len(rest))


def column_spec(rows, slots):
    return pl.BlockSpec((rows, PAIR * slots), lambda i: (0, i))


def costs(flops, moved):
    return pl.CostEstimate(flops=flops, bytes_accessed=moved, transcendentals=0)


def embed(tokens, cotangent, token_types, pairs_t, lap_t, embed_weight, norm_params):
    mols, slots, width = tokens.shape
    toks = mols * slots
    rows = (width, width, 256, width)
    types = (F32, BF16, BF16, BF16)
    return pl.pallas_call(
        embed_kernel,
        grid=(mols // PAIR,),
        out_shape=[jax.ShapeDtypeStruct((r, toks), t) for r, t in zip(rows, types)],
        out_specs=[column_spec(r, slots) for r in rows],
        in_specs=[
            lead_spec(slots, width),
            lead_spec(slots, width),
            lead_spec(1, slots),
            lead_spec(2, slots),
            lead_spec(lap_t.shape[1], lap_t.shape[2]),
            whole_spec(embed_weight.shape),
            whole_spec(norm_params.shape),
        ],
        scratch_shapes=[
            pltpu.VMEM((2, width, slots), F32),
            pltpu.VMEM((IDENT_ROWS, width), F32),
            pltpu.VMEM((width, 256), BF16),
        ],
        compiler_params=pltpu.CompilerParams(vmem_limit_bytes=VMEM_BYTES),
        cost_estimate=costs(8_000_000_000, 10_000_000),
        name="embed",
    )(tokens, cotangent, token_types.reshape(mols, 1, slots), pairs_t, lap_t, embed_weight, norm_params)


def front(lengths, h0, na, cot, norm_params, own, peer, mols):
    width, toks = h0.shape
    slots = toks // mols
    half = width // 2
    heads = width // HEAD_DIM
    owners = 16
    col = column_spec(width, slots)
    weights = []
    for pair in zip(own, peer):
        weights += list(pair)
    gshape = (owners, 2 * half // owners, 3 * half)
    padded = jax.ShapeDtypeStruct((mols, heads * PAD_DIM, slots), BF16)
    outs = [
        (jax.ShapeDtypeStruct((width, toks), F32), col),
        (jax.ShapeDtypeStruct((width, toks), F32), col),
        (jax.ShapeDtypeStruct((width, toks), BF16), whole_spec((width, toks))),
        (padded, lead_spec(heads * PAD_DIM, slots)),
        (padded, lead_spec(heads * PAD_DIM, slots)),
        (padded, lead_spec(heads * PAD_DIM, slots)),
        (padded, lead_spec(heads * PAD_DIM, slots)),
        (jax.ShapeDtypeStruct((mols, heads, slots, slots), BF16), lead_spec(heads, slots, slots)),
        (jax.ShapeDtypeStruct(gshape, BF16), whole_spec(gshape)),
        (jax.ShapeDtypeStruct(gshape, BF16), whole_spec(gshape)),
        (jax.ShapeDtypeStruct((2, width, slots), F32), whole_spec((2, width, slots))),
    ]
    return pl.pallas_call(
        front_kernel,
        grid=(mols // PAIR,),
        out_shape=[o[0] for o in outs],
        out_specs=[o[1] for o in outs],
        in_specs=[
            pl.BlockSpec(memory_space=pltpu.SMEM),
            col,
            col,
            whole_spec(cot.shape),
            whole_spec(norm_params.shape),
        ]
        + [whole_spec(w.shape) for w in weights],
        scratch_shapes=[
            pltpu.VMEM((6 * half, width), BF16),
        ]
        + [pltpu.VMEM((width, width), BF16)] * 5
        + [pltpu.VMEM((2, width, slots), F32)]
        + [pltpu.VMEM((width, toks), BF16)] * 4
        + [pltpu.VMEM((PAIR, width, slots), F32), pltpu.VMEM((width, PAIR * slots), F32)]
        + [pltpu.VMEM((PAIR, heads // 4 + 1, 8, slots), F32)],
        compiler_params=pltpu.CompilerParams(vmem_limit_bytes=VMEM_BYTES),
        cost_estimate=costs(60_000_000_000, 50_000_000),
        name="front",
    )(lengths, h0, na, cot, norm_params, *weights)


def middle(which, na, q, k, v, do, e, got=None, plane=None):
    mols, heads, slots, _ = e.shape
    width, toks = na.shape
    half = width // 2
    rows = heads // 2 * PAD_DIM
    part = pl.BlockSpec((PAIR, rows, slots), lambda i: (i, which, 0))
    gshape = (16, width // 16, 3 * half)
    dx = jax.ShapeDtypeStruct((3 * half, toks), BF16)
    specs = [
        whole_spec(na.shape),
        part,
        part,
        part,
        part,
        pl.BlockSpec((PAIR, heads // 2, slots, slots), lambda i: (i, which, 0, 0)),
    ]
    common = dict(
        grid=(mols // PAIR,),
        compiler_params=pltpu.CompilerParams(vmem_limit_bytes=VMEM_BYTES),
        cost_estimate=costs(200_000_000, 120_000),
    )
    if got is None:
        return pl.pallas_call(
            middle_kernel,
            out_shape=[dx, jax.ShapeDtypeStruct(gshape, BF16)],
            in_specs=specs,
            out_specs=[whole_spec(dx.shape), whole_spec(gshape)],
            name="middle_peer",
            **common,
        )(na, q, k, v, do, e)
    piece = (4,) + gshape[1:]
    return pl.pallas_call(
        middle_own_kernel,
        out_shape=[dx] + [jax.ShapeDtypeStruct(piece, BF16)] * 4,
        in_specs=[pl.BlockSpec(memory_space=pltpu.SMEM)] + specs + [whole_spec(gshape)],
        out_specs=[whole_spec(dx.shape)] + [whole_spec(piece)] * 4,
        scratch_shapes=[pltpu.VMEM(gshape, BF16)],
        name="middle_own",
        **common,
    )(plane, na, q, k, v, do, e, got)


def finish_output(h1, act, down_o, down_p, mols):
    width, toks = h1.shape
    slots = toks // mols
    col = column_spec(width, slots)
    return pl.pallas_call(
        output_kernel,
        grid=(mols // PAIR,),
        out_shape=jax.ShapeDtypeStruct((mols, slots, width), BF16),
        in_specs=[col, col, whole_spec(down_o.shape), whole_spec(down_p.shape)],
        out_specs=lead_spec(slots, width),
        scratch_shapes=[pltpu.VMEM((width, width), BF16)],
        compiler_params=pltpu.CompilerParams(vmem_limit_bytes=VMEM_BYTES),
        cost_estimate=costs(60_000_000, 70_000),
        name="finish_output",
    )(h1, act, down_o, down_p)


def back(dxo, dxp, qkv_o, qkv_p, h0, gh1, fs, gain, lnb, mols, packed):
    width, toks = h0.shape
    slots = toks // mols
    col = column_spec(width, slots)
    dxs = column_spec(dxo.shape[0], slots)
    small = (width // 24, 8, slots) if packed else (width, slots)
    return pl.pallas_call(
        back_kernel,
        grid=(mols // PAIR,),
        out_shape=[
            jax.ShapeDtypeStruct((mols, slots, width), F32),
            jax.ShapeDtypeStruct(small, F32),
        ],
        in_specs=[
            dxs,
            dxs,
            whole_spec(qkv_o.shape),
            whole_spec(qkv_p.shape),
            col,
            col,
            column_spec(fs.shape[0], slots),
            whole_spec(gain.shape),
            whole_spec(lnb.shape),
        ],
        out_specs=[lead_spec(slots, width), whole_spec(small)],
        scratch_shapes=[
            pltpu.VMEM((width, slots), F32),
            pltpu.VMEM((2, width, slots), F32),
            pltpu.VMEM((width, fs.shape[0]), F32),
            pltpu.VMEM((width, 3 * width), BF16),
        ],
        compiler_params=pltpu.CompilerParams(vmem_limit_bytes=VMEM_BYTES),
        cost_estimate=costs(18_000_000_000, 15_000_000),
        name="back",
    )(dxo, dxp, qkv_o, qkv_p, h0, gh1, fs, gain, lnb)


def gather(firsts, seconds, got):
    rows, columns = firsts[0].shape
    lanes = got.shape[2]
    return pl.pallas_call(
        gather_kernel,
        out_shape=[
            jax.ShapeDtypeStruct((rows, columns), F32),
            jax.ShapeDtypeStruct((rows, columns), F32),
            jax.ShapeDtypeStruct(got.shape[1:], F32),
            jax.ShapeDtypeStruct((got.shape[0], lanes), F32),
        ],
        compiler_params=pltpu.CompilerParams(vmem_limit_bytes=VMEM_BYTES),
        name="gather",
    )(*firsts, *seconds, got)


def adam_all(squares, red1, red2, small, state):
    return pl.pallas_call(
        adam_kernel,
        out_shape=[jax.ShapeDtypeStruct((1, squares.shape[1]), F32)]
        + [jax.ShapeDtypeStruct(a.shape, F32) for a in state],
        compiler_params=pltpu.CompilerParams(vmem_limit_bytes=VMEM_BYTES),
        name="adam",
    )(squares, red1, red2, small, *state)


def swap(value):
    return lax.ppermute(value, "mp", [(0, 1), (1, 0)])


def hop(value, flip):
    size = lax.axis_size("dp")
    return lax.ppermute(value, "dp", [(i, i ^ flip) for i in range(size)])


def take(value, index, axis=0):
    return lax.dynamic_index_in_dim(value, index, axis, keepdims=False)


def line_pieces(own, near, line):
    total = own.astype(F32)
    for piece in near:
        total = total + piece.astype(F32)
    total = total.astype(BF16)
    return take(total, line), [take(total, line ^ k) for k in (1, 2, 3)]


def adam_step(master, mean_old, square_old, gradient, rate, decay, clip_scale):
    clipped = gradient * clip_scale
    mean_new = BETA_FIRST * mean_old + (1.0 - BETA_FIRST) * clipped
    square_new = BETA_SECOND * square_old + (1.0 - BETA_SECOND) * clipped * clipped
    mean_hat = mean_new / (1.0 - BETA_FIRST**STEP)
    square_hat = square_new / (1.0 - BETA_SECOND**STEP)
    updated = master - rate * (mean_hat / (jnp.sqrt(square_hat) + ADAM_EPS) + decay * master)
    return (updated, mean_new, square_new)


def on_device(
    tokens,
    cotangent,
    lengths,
    token_types,
    node_pairs,
    laplacian,
    qkv_weight,
    out_weight,
    up_weight,
    down_weight,
    qkv_master,
    qkv_mean,
    qkv_square,
    out_master,
    out_mean,
    out_square,
    up_master,
    up_mean,
    up_square,
    down_master,
    down_mean,
    down_square,
    norm_params,
    norm_mean,
    norm_square,
    embed_weight,
    embed_mean,
    embed_square,
):
    mols, slots, width = tokens.shape
    half = width // 2
    dp_size = lax.axis_size("dp")
    mp_size = lax.axis_size("mp")
    idents = embed_weight.shape[0]

    own = (qkv_weight.transpose(1, 0, 2), out_weight, up_weight, down_weight)
    peer = tuple(swap(w) for w in own)

    world = dp_size * mp_size
    shard_width = width // world
    fits = dp_size == 16 and shard_width == 24

    h0, na, fs, cot = embed(
        tokens,
        cotangent,
        token_types,
        node_pairs.transpose(0, 2, 1),
        laplacian.transpose(0, 2, 1),
        embed_weight,
        norm_params,
    )
    (gh1, h1, act, q, k, v, do, e, gown1, gpeer1, lnb) = front(
        lengths, h0, na, cot, norm_params, own, peer, mols
    )
    index = lax.axis_index("dp")
    plane, line = (index & 3, index >> 2) if fits else (jnp.int32(0), None)
    got1 = swap(gpeer1)
    dxp, gpeer2 = middle(1, na, q, k, v, do, e)
    got1, dxp = lax.optimization_barrier((got1, dxp))
    sum1 = (gown1.astype(F32) + got1.astype(F32)).astype(BF16)
    got2 = swap(gpeer2)
    if fits:
        grid = sum1.reshape((4, 4) + sum1.shape[1:]).swapaxes(0, 1)
        pieces1 = [take(grid, plane ^ k) for k in range(4)]
        pieces1, do = lax.optimization_barrier((pieces1, do))
        near1 = [hop(piece, k) for piece, k in zip(pieces1[1:], (1, 2, 3))]
    dxo, *pieces = middle(0, na, q, k, v, do, e, got2, plane.reshape(1))
    if fits:
        h1, pieces = lax.optimization_barrier((h1, pieces))
        near = [hop(piece, k) for piece, k in zip(pieces[1:], (1, 2, 3))]
    output = finish_output(h1, act, own[3], peer[3], mols)
    if fits:
        near1, output = lax.optimization_barrier((near1, output))
        own1, sends1 = line_pieces(pieces1[0], near1, line)
        sends1, dxo = lax.optimization_barrier((sends1, dxo))
        far1 = [hop(piece, 4 * k) for piece, k in zip(sends1, (1, 2, 3))]
    input_grad, small = back(
        dxo,
        dxp,
        own[0],
        peer[0],
        h0,
        gh1,
        fs,
        norm_params,
        lnb,
        mols,
        fits,
    )

    shard_index = index * mp_size + lax.axis_index("mp")
    norm_own = lax.dynamic_slice_in_dim(norm_params, shard_index * shard_width, shard_width, 1)
    embed_own = lax.dynamic_slice_in_dim(embed_weight, shard_index * shard_width, shard_width, 1)
    flip = lambda a: a.transpose(1, 0, 2)
    if fits:
        small, far1[1:] = lax.optimization_barrier((small, far1[1:]))
        got = lax.all_to_all(small, ("dp", "mp"), 0, 0, tiled=True)
        own2, sends2 = line_pieces(pieces[0], near, line)
        far2 = [hop(piece, 4 * k) for piece, k in zip(sends2, (1, 2, 3))]
        red1, red2, small_own, squares = gather([own1, *far1], [own2, *far2], got)
        lanes = squares.shape[1]
        squares = lax.all_to_all(squares.reshape(world, 1, lanes), ("dp", "mp"), 0, 0, tiled=True)
        state = (
            (flip(qkv_master), flip(qkv_mean), flip(qkv_square))
            + (out_master, out_mean, out_square)
            + (up_master, up_mean, up_square)
            + (down_master, down_mean, down_square)
            + (norm_own, norm_mean, norm_square)
            + (embed_own.T, embed_mean.T, embed_square.T)
        )
        clip, *new = adam_all(squares.reshape(world, lanes), red1, red2, small_own, state)
        new = [flip(a) for a in new[0:3]] + list(new[3:15]) + [a.T for a in new[15:18]]
        return (output, input_grad, clip[0, 0]) + tuple(new)

    some = half // 16
    scatter = partial(lax.psum_scatter, axis_name="dp", scatter_dimension=0, tiled=True)
    sum1 = sum1.astype(F32)
    sum2 = jnp.stack(pieces, axis=1).astype(F32)
    reduced_down = scatter(sum1[:, 0:some, 0:width].reshape(half, width))
    reduced_out = scatter(sum1[:, some:, 0:width].reshape(half, width))
    reduced_up = scatter(sum1[:, :, width:].reshape(width, half))
    reduced_qkv = scatter(sum2.reshape(width, 3, half))
    small = small[:, : idents + 4].reshape(world, shard_width, idents + 4)
    small_own = jnp.sum(lax.all_to_all(small, ("dp", "mp"), 0, 0, tiled=True), axis=0).T
    reduced = (reduced_qkv, reduced_out, reduced_up, reduced_down, small_own[idents:], small_own[:idents])
    own_square = sum(jnp.sum(piece * piece) for piece in reduced)
    clip_norm = jnp.sqrt(lax.psum(own_square, ("dp", "mp")))
    clip_scale = jnp.minimum(1.0, CLIP_LIMIT / (clip_norm + 1e-06))
    state = (
        (qkv_master, qkv_mean, qkv_square, MATRIX_RATE, MATRIX_DECAY),
        (out_master, out_mean, out_square, MATRIX_RATE, MATRIX_DECAY),
        (up_master, up_mean, up_square, MATRIX_RATE, MATRIX_DECAY),
        (down_master, down_mean, down_square, MATRIX_RATE, MATRIX_DECAY),
        (norm_own, norm_mean, norm_square, NORM_RATE, 0.0),
        (embed_own, embed_mean, embed_square, EMBED_RATE, 0.0),
    )
    new = ()
    for (master, mean, square, rate, decay), grad in zip(state, reduced):
        new += adam_step(master, mean, square, grad, rate, decay, clip_scale)
    return (output, input_grad, clip_norm) + new


def solution(mesh):
    tokens = P(("dp", "mp"), None, None)
    qkv = P("dp", None, "mp")
    rows = P(("mp", "dp"), None)
    both = P("dp", "mp")
    small = P(None, ("dp", "mp"))
    return jax.shard_map(
        on_device,
        mesh=mesh,
        in_specs=(
            tokens,
            tokens,
            P(("dp", "mp")),
            P(("dp", "mp"), None),
            tokens,
            tokens,
            P(None, None, "mp"),
            P("mp", None),
            P(None, "mp"),
            P("mp", None),
        )
        + (qkv,) * 3
        + (rows,) * 3
        + (both,) * 3
        + (rows,) * 3
        + (P(), small, small) * 2,
        out_specs=(tokens, tokens, P())
        + (qkv,) * 3
        + (rows,) * 3
        + (both,) * 3
        + (rows,) * 3
        + (small,) * 6,
        check_vma=False,
    )
```

```python
from functools import partial
import math

import jax
import jax.numpy as jnp
from jax import lax
from jax.experimental import pallas as pl
from jax.experimental.pallas import tpu as pltpu
from jax.sharding import PartitionSpec as P

HEAD_DIM = 24
PAD_DIM = 32
STEP = 10
NORM_EPS = 1e-05
BETA_FIRST = 0.9
BETA_SECOND = 0.95
ADAM_EPS = 1e-08
MATRIX_RATE = 0.03
NORM_RATE = 0.5
EMBED_RATE = 0.05
MATRIX_DECAY = 0.1
CLIP_LIMIT = 1.0
MASK_VALUE = -1e30
SCORE_SCALE = 1.0 / math.sqrt(HEAD_DIM)
LOG2E = 1.4426950408889634
LN2 = 0.6931471805599453
IDENT_ROWS = 40
IDENT_USED = 34
PAIR = 2
MEGA = 1024 * 1024
FRONT_UNROLL = 8
MIDDLE_UNROLL = 8

F32 = jnp.float32
BF16 = jnp.bfloat16


def dot_nn(lhs, rhs):
    return lax.dot_general(lhs, rhs, (((1,), (0,)), ((), ())), preferred_element_type=F32)


def dot_nt(lhs, rhs):
    return lax.dot_general(lhs, rhs, (((1,), (1,)), ((), ())), preferred_element_type=F32)


def norm_parts(values):
    scale = 1.0 / values.shape[0]
    centred = values - jnp.sum(values, axis=0, keepdims=True) * scale
    spread = jnp.sum(centred * centred, axis=0, keepdims=True) * scale
    return centred, lax.rsqrt(spread + NORM_EPS)


ROWS = 96


def fold(values):
    return jnp.sum(values.reshape(-1, 8, values.shape[1]), axis=0)


def row_chunks(width):
    return [slice(r, r + ROWS) for r in range(0, width, ROWS)]


def norm_forward(ref, lanes):
    width = ref.shape[0]
    total = None
    for r in row_chunks(width):
        part = fold(ref[r, lanes])
        total = part if total is None else total + part
    mean = jnp.sum(total, axis=0, keepdims=True) * (1.0 / width)
    total = None
    for r in row_chunks(width):
        centred = ref[r, lanes] - mean
        part = fold(centred * centred)
        total = part if total is None else total + part
    spread = jnp.sum(total, axis=0, keepdims=True) * (1.0 / width)
    return mean, lax.rsqrt(spread + NORM_EPS)


def norm_sums(grad_ref, unit_ref, gain_ref, acc_ref, lanes):
    width = grad_ref.shape[0]
    first = second = None
    for r in row_chunks(width):
        grad = grad_ref[r, lanes]
        both = grad * unit_ref[r, lanes]
        acc_ref[0, r, :] += both
        acc_ref[1, r, :] += grad
        gain = gain_ref[r, :]
        one, two = fold(grad * gain), fold(both * gain)
        first = one if first is None else first + one
        second = two if second is None else second + two
    return tuple(jnp.sum(v, axis=0, keepdims=True) * (1.0 / width) for v in (first, second))


def gelu_parts(x):
    size = jnp.abs(x)
    bell = jnp.exp2((-0.5 * LOG2E) * (x * x))
    t = 1.0 / (1.0 + (0.3275911 / math.sqrt(2.0)) * size)
    poly = t * (
        0.5 * 0.254829592
        + t
        * (
            0.5 * -0.284496736
            + t * (0.5 * 1.421413741 + t * (0.5 * -1.453152027 + t * (0.5 * 1.061405429)))
        )
    )
    tail = poly * bell
    share = jnp.where(x < 0.0, tail, 1.0 - tail)
    return x * share, share + x * bell * (1.0 / math.sqrt(2.0 * math.pi))


def head_rows(values, tail):
    heads = values.shape[0] // HEAD_DIM
    cut = values.reshape(heads, HEAD_DIM, values.shape[1])
    tails = jnp.broadcast_to(tail[None], (heads,) + tail.shape)
    return jnp.concatenate([cut, tails], axis=1).reshape(heads * PAD_DIM, values.shape[1])


def block_columns(rows):
    zero = jnp.zeros((PAD_DIM, rows.shape[1]), rows.dtype)
    columns = []
    for head in range(4):
        pieces = [zero] * 4
        pieces[head] = rows[head * PAD_DIM : (head + 1) * PAD_DIM]
        columns.append(jnp.concatenate(pieces, axis=0))
    return jnp.concatenate(columns, axis=1)


def lane_columns(row, slots):
    return jnp.broadcast_to(row, (slots, row.shape[1])).T


def embed_kernel(
    tok_ref,
    cot_ref,
    typ_ref,
    pair_ref,
    lap_ref,
    embed_ref,
    norm_ref,
    h0_ref,
    na_ref,
    fs_ref,
    ct_ref,
    nb,
    rows,
    est,
):
    slots = tok_ref.shape[1]
    width = tok_ref.shape[2]

    @pl.when(pl.program_id(0) == 0)
    def _():
        for row in range(2):
            nb[row] = lane_columns(norm_ref[row : row + 1, :], slots)
        rows[...] = jnp.zeros_like(rows)
        rows[0 : embed_ref.shape[0], :] = embed_ref[...]
        whole = rows[...]
        e1 = whole.astype(BF16).astype(F32)
        e2 = (whole - e1).astype(BF16).astype(F32)
        e3 = whole - e1 - e2
        blank = jnp.zeros((8, width), F32)
        stacked = jnp.concatenate([e1, e2, e3, blank, e1, e2, e1, blank], axis=0)
        est[...] = stacked.T.astype(BF16)

    node_iota = lax.broadcasted_iota(jnp.int32, (lap_ref.shape[2], slots), 0)
    row_iota = lax.broadcasted_iota(jnp.int32, (8, slots), 0)
    for j in range(PAIR):
        lanes = slice(j * slots, (j + 1) * slots)
        lap = lap_ref[j]
        lap1 = lap.astype(BF16)
        rest = lap - lap1.astype(F32)
        lap2 = rest.astype(BF16)
        lap3 = (rest - lap2.astype(F32)).astype(BF16)
        laps = jnp.concatenate([lap1.astype(F32), lap2.astype(F32), lap3.astype(F32)], axis=0)
        laps = laps.astype(BF16)
        left = jnp.where(node_iota == pair_ref[j, 0:1, :], 1.0, 0.0).astype(BF16)
        right = jnp.where(node_iota == pair_ref[j, 1:2, :], 1.0, 0.0).astype(BF16)
        lf = dot_nn(laps, left)
        rf = dot_nn(laps, right)
        types = typ_ref[j]
        kinds = jnp.where((row_iota < 2) & (row_iota == types), 1.0, 0.0)
        none = jnp.zeros((8, slots), F32)
        ident = lap.shape[0]
        f1 = jnp.concatenate([lf[0:ident], rf[0:ident], kinds], axis=0)
        f2 = jnp.concatenate([lf[ident : 2 * ident], rf[ident : 2 * ident], none], axis=0)
        f3 = jnp.concatenate([lf[2 * ident :], rf[2 * ident :], none], axis=0)
        stack = jnp.concatenate([f1, f1, f1, none, f2, f2, f3, none], axis=0).astype(BF16)
        fs_ref[:, lanes] = stack
        h0_ref[:, lanes] = tok_ref[j].T.astype(F32) + dot_nn(est[...], stack)
        mean, rec = norm_forward(h0_ref, lanes)
        for r in row_chunks(width):
            unit = (h0_ref[r, lanes] - mean) * rec
            na_ref[r, lanes] = (unit * nb[0, r, :] + nb[1, r, :]).astype(BF16)
        ct_ref[:, lanes] = cot_ref[j].T


def block_pair(rows):
    zero = jnp.zeros((PAD_DIM, rows.shape[1]), rows.dtype)
    left = jnp.concatenate([rows[0:PAD_DIM], zero], axis=0)
    right = jnp.concatenate([zero, rows[PAD_DIM:]], axis=0)
    return jnp.concatenate([left, right], axis=1)


def staged(at, first, second, third):
    one, two = {}, {}
    count = len(at)
    for n in range(count + 2):
        if n < count:
            one[n] = first(*at[n])
        if 0 <= n - 1 < count:
            two[n - 1] = second(*at[n - 1], one.pop(n - 1))
        if 0 <= n - 2 < count:
            third(*at[n - 2], two.pop(n - 2))


def front_kernel(
    len_ref,
    h0_ref,
    na_ref,
    cot_s,
    norm_ref,
    qkv_o,
    qkv_p,
    out_o,
    out_p,
    up_o,
    up_p,
    down_o,
    down_p,
    gh1_ref,
    h1_s,
    act_ref,
    q_ref,
    k_ref,
    v_ref,
    do_ref,
    e_ref,
    gown_ref,
    gpeer_ref,
    lnacc_ref,
    qkvt,
    outt,
    upt,
    outw,
    upw,
    downw,
    nb,
    act_s,
    nbt_s,
    gp_s,
    mix_s,
    ga_s,
    mixf,
    nrm_s,
    gb_s,
    rec_s,
):
    step = pl.program_id(0)
    steps = pl.num_programs(0)
    slots = e_ref.shape[2]
    width = h0_ref.shape[0]
    half = width // 2
    halves = ((qkv_o, out_o, up_o, down_o), (qkv_p, out_p, up_p, down_p))

    @pl.when(step == 0)
    def _():
        for h, (qkv, out, up, down) in enumerate(halves):
            part = slice(h * half, (h + 1) * half)
            for c in range(3):
                at = (3 * h + c) * half
                qkvt[at : at + half, :] = qkv[c].T
            outt[:, part] = out[...].T
            upt[part, :] = up[...].T
            outw[part, :] = out[...]
            upw[:, part] = up[...]
            downw[part, :] = down[...]
        for row in range(2):
            nb[row] = lane_columns(norm_ref[row + 2 : row + 3, :], slots)
        lnacc_ref[...] = jnp.zeros_like(lnacc_ref)

    base = pl.multiple_of(step * PAIR * slots, PAIR * slots)
    span = pl.ds(base, PAIR * slots)

    phase = pl.when(step >= 0)
    groups = width // (4 * HEAD_DIM)
    parts = tuple(slice(h * half, (h + 1) * half) for h in range(2))
    sides = tuple(slice(j * slots, (j + 1) * slots) for j in range(PAIR))
    columns = tuple(
        pl.ds(pl.multiple_of(base + j * slots, slots), slots) for j in range(PAIR)
    )

    @phase
    def _():
        row_iota = lax.broadcasted_iota(jnp.int32, (8, slots), 0)
        lane_iota = lax.broadcasted_iota(jnp.int32, (1, slots), 1)
        one_row = jnp.where(row_iota == 0, 1.0, 0.0)
        two_rows = jnp.where(row_iota < 2, 1.0, 0.0)
        padded = half // HEAD_DIM * PAD_DIM
        for h in range(2):
            rows = slice(h * padded, (h + 1) * padded)
            for c, ref in enumerate((q_ref, k_ref, v_ref)):
                at = (3 * h + c) * half
                proj = dot_nn(qkvt[at : at + half, :], na_ref[...])
                for j in range(PAIR):
                    own = proj[:, sides[j]]
                    if c == 0:
                        own, tail = own * (SCORE_SCALE * LOG2E), one_row
                    elif c == 1:
                        length = len_ref[step * PAIR + j]
                        bias = jnp.where(lane_iota < length, 0.0, MASK_VALUE)
                        tail = jnp.where(row_iota == 0, bias, 0.0)
                    else:
                        tail = two_rows
                    ref[j, rows, :] = head_rows(own, tail).astype(BF16)

    def score(j, g):
        rows = pl.ds(pl.multiple_of(g * 4 * PAD_DIM, 4 * PAD_DIM), 4 * PAD_DIM)
        return dot_nn(k_ref[j, rows, :].T, block_columns(q_ref[j, rows, :]))

    def weigh(j, g, scores):
        exps = []
        for a in range(4):
            own = scores[:, a * slots : (a + 1) * slots]
            ex = jnp.exp2(own - jnp.max(own, axis=0, keepdims=True)).astype(BF16)
            e_ref[j, g * 4 + a] = ex
            exps.append(ex)
        return exps

    def mix_values(j, g, exps):
        rows = pl.ds(pl.multiple_of(g * 4 * PAD_DIM, 4 * PAD_DIM), 4 * PAD_DIM)
        vals = v_ref[j, rows, :]
        mixes = []
        for a in range(0, 4, 2):
            two = dot_nn(
                vals[a * PAD_DIM : (a + 2) * PAD_DIM], jnp.concatenate(exps[a : a + 2], axis=1)
            )
            for b in range(2):
                got = two[b * PAD_DIM : (b + 1) * PAD_DIM, b * slots : (b + 1) * slots]
                rec = 1.0 / got[HEAD_DIM : HEAD_DIM + 1]
                rec_s[j, g, a + b : a + b + 1, :] = rec
                mixes.append(got[0:HEAD_DIM] * rec)
        out_rows = pl.ds(pl.multiple_of(g * 4 * HEAD_DIM, 4 * HEAD_DIM), 4 * HEAD_DIM)
        mixf[j, out_rows, :] = jnp.concatenate(mixes, axis=0)

    def attend(i, carry):
        at = [i * FRONT_UNROLL + u for u in range(FRONT_UNROLL)]
        at = [(lax.div(n, groups), lax.rem(n, groups)) for n in at]
        staged(at, score, weigh, mix_values)
        return carry

    lax.fori_loop(0, PAIR * groups // FRONT_UNROLL, attend, 0)

    @phase
    def _():
        for j in range(PAIR):
            mix_s[:, columns[j]] = mixf[j].astype(BF16)
        for part in parts:
            h1_s[part, :] = h0_ref[part, :] + dot_nn(outt[part, :], mix_s[:, span])
        for j in range(PAIR):
            mean, rec = norm_forward(h1_s, sides[j])
            rec_s[j, groups, 0:1, :] = rec
            for r in row_chunks(width):
                unit = (h1_s[r, sides[j]] - mean) * rec
                nrm_s[r, sides[j]] = unit
                nbt_s[r, columns[j]] = (unit * nb[0, r, :] + nb[1, r, :]).astype(BF16)

    @phase
    def _():
        for part in parts:
            act, slope = gelu_parts(dot_nn(upt[part, :], nbt_s[:, span]))
            low = act.astype(BF16)
            act_s[part, span] = low
            act_ref[part, :] = low
            back = dot_nn(downw[part, :], cot_s[:, span])
            gp_s[part, span] = (back * slope).astype(BF16)

    @phase
    def _():
        for part in parts:
            gb_s[part, :] = dot_nn(upw[part, :], gp_s[:, span])
        for j in range(PAIR):
            f_mean, fn_mean = norm_sums(gb_s, nrm_s, nb.at[0], lnacc_ref, sides[j])
            rec = rec_s[j, groups, 0:1, :]
            for r in row_chunks(width):
                f = gb_s[r, sides[j]] * nb[0, r, :]
                gh1 = cot_s[r, columns[j]].astype(F32) + rec * (
                    f - f_mean - nrm_s[r, sides[j]] * fn_mean
                )
                gh1_ref[r, sides[j]] = gh1
                ga_s[r, columns[j]] = gh1.astype(BF16)

    @phase
    def _():
        rows8 = lax.broadcasted_iota(jnp.int32, (4, 8, slots), 1)
        for h, part in enumerate(parts):
            gm = dot_nn(outw[part, :], ga_s[:, span])
            for j in range(PAIR):
                for g in range(groups // 2):
                    at = h * (groups // 2) + g
                    grad = gm[g * 96 : (g + 1) * 96, sides[j]].reshape(4, HEAD_DIM, slots)
                    mixed = mixf[j, at * 96 : (at + 1) * 96, :].reshape(4, HEAD_DIM, slots)
                    rec = rec_s[j, at].reshape(8, 1, slots)[0:4]
                    inner = -(jnp.sum(grad * mixed, axis=1, keepdims=True) * rec)
                    high = inner.astype(BF16).astype(F32)
                    low = inner - high
                    tail = jnp.where(rows8 == 0, high, jnp.where(rows8 == 1, low, 0.0))
                    full = jnp.concatenate([grad * rec, tail], axis=1)
                    do_ref[j, at * 128 : (at + 1) * 128, :] = (
                        full.reshape(4 * PAD_DIM, slots).astype(BF16)
                    )

    @pl.when(step == steps - 1)
    def _():
        owners = gown_ref.shape[0]
        some = half // owners
        for h, g_ref in enumerate((gown_ref, gpeer_ref)):
            rows = slice(h * half, (h + 1) * half)
            gdown = dot_nt(act_s[rows, :], cot_s[...])
            gout = dot_nt(mix_s[rows, :], ga_s[...])
            for o in range(owners):
                both = jnp.concatenate(
                    [gdown[o * some : (o + 1) * some], gout[o * some : (o + 1) * some]], axis=0
                )
                g_ref[o, :, 0:width] = both.astype(g_ref.dtype)
            gup = dot_nt(nbt_s[...], gp_s[rows, :])
            g_ref[:, :, width:] = gup.reshape(owners, 2 * some, half).astype(g_ref.dtype)


def middle_kernel(
    na_ref, q_ref, k_ref, v_ref, do_ref, e_ref, dx_ref, g_ref, na_s, dx_s
):
    attention_back(na_ref, q_ref, k_ref, v_ref, do_ref, e_ref, dx_ref, na_s, dx_s)
    half = dx_ref.shape[0] // 3

    @pl.when(pl.program_id(0) == pl.num_programs(0) - 1)
    def _():
        for c in range(3):
            cut = slice(c * half, (c + 1) * half)
            grad = dot_nt(na_s[...], dx_s[cut, :])
            g_ref[:, :, cut] = grad.reshape(g_ref.shape[0:2] + (half,)).astype(BF16)


def middle_own_kernel(
    plane_ref,
    na_ref,
    q_ref,
    k_ref,
    v_ref,
    do_ref,
    e_ref,
    got_ref,
    dx_ref,
    g0,
    g1,
    g2,
    g3,
    na_s,
    dx_s,
    total,
):
    attention_back(na_ref, q_ref, k_ref, v_ref, do_ref, e_ref, dx_ref, na_s, dx_s)
    half = dx_ref.shape[0] // 3

    @pl.when(pl.program_id(0) == pl.num_programs(0) - 1)
    def _():
        for c in range(3):
            cut = slice(c * half, (c + 1) * half)
            grad = dot_nt(na_s[...], dx_s[cut, :]).reshape(total.shape[0:2] + (half,))
            total[:, :, cut] = (grad + got_ref[:, :, cut].astype(F32)).astype(BF16)
        plane = plane_ref[0]
        for k, g_ref in enumerate((g0, g1, g2, g3)):
            for line in range(4):
                g_ref[line] = total[line * 4 + (plane ^ k)]


def attention_back(na_ref, q_ref, k_ref, v_ref, do_ref, e_ref, dx_ref, na_s, dx_s):
    step = pl.program_id(0)
    slots = q_ref.shape[2]
    half = dx_ref.shape[0] // 3
    base = pl.multiple_of(step * PAIR * slots, PAIR * slots)
    groups = half // (4 * HEAD_DIM)

    na_s[:, pl.ds(base, PAIR * slots)] = na_ref[...]

    def rows_of(g):
        return pl.ds(pl.multiple_of(g * 4 * PAD_DIM, 4 * PAD_DIM), 4 * PAD_DIM)

    def score(j, g):
        return dot_nn(v_ref[j, rows_of(g), :].T, block_columns(do_ref[j, rows_of(g), :]))

    def weigh(j, g, back):
        grads = []
        for a in range(4):
            ex = e_ref[j, g * 4 + a].astype(F32)
            grads.append((ex * back[:, a * slots : (a + 1) * slots]).astype(BF16))
        return grads

    def products(j, g, grads):
        dos = do_ref[j, rows_of(g), :]
        qs = q_ref[j, rows_of(g), :]
        ks = k_ref[j, rows_of(g), :]
        dq, dk, dv = [], [], []
        for a in range(0, 4, 2):
            cut = slice(a * PAD_DIM, (a + 2) * PAD_DIM)
            both = jnp.concatenate(grads[a : a + 2], axis=1)
            exps = jnp.concatenate([e_ref[j, g * 4 + a + b].T for b in range(2)], axis=1)
            two = dot_nn(ks[cut], both)
            dq.append(two[0:HEAD_DIM, 0:slots])
            dq.append(two[PAD_DIM : PAD_DIM + HEAD_DIM, slots:])
            two = dot_nt(block_pair(qs[cut]), both)
            dk.append(two[0:HEAD_DIM])
            dk.append(two[PAD_DIM : PAD_DIM + HEAD_DIM])
            two = dot_nn(dos[cut], exps)
            dv.append(two[0:HEAD_DIM, 0:slots])
            dv.append(two[PAD_DIM : PAD_DIM + HEAD_DIM, slots:])
        cols = pl.ds(pl.multiple_of(base + j * slots, slots), slots)
        for c, (parts, scale) in enumerate(((dq, SCORE_SCALE), (dk, LN2), (dv, None))):
            at = pl.ds(pl.multiple_of(c * half + g * 96, 32), 96)
            whole = jnp.concatenate(parts, axis=0)
            if scale is not None:
                whole = whole * scale
            low = whole.astype(BF16)
            dx_s[at, cols] = low
            dx_ref[at, pl.ds(pl.multiple_of(j * slots, slots), slots)] = low

    def attend(i, carry):
        at = [i * MIDDLE_UNROLL + u for u in range(MIDDLE_UNROLL)]
        at = [(lax.div(n, groups), lax.rem(n, groups)) for n in at]
        staged(at, score, weigh, products)
        return carry

    lax.fori_loop(0, PAIR * groups // MIDDLE_UNROLL, attend, 0)


def output_kernel(h1_ref, act_ref, down_o, down_p, output_ref, downt):
    slots = output_ref.shape[1]
    half = down_o.shape[0]

    @pl.when(pl.program_id(0) == 0)
    def _():
        for h, down in enumerate((down_o, down_p)):
            downt[:, h * half : (h + 1) * half] = down[...].T

    ffn = [dot_nn(downt[h * half : (h + 1) * half, :], act_ref[...]) for h in range(2)]
    ffn = jnp.concatenate(ffn, axis=0)
    for j in range(PAIR):
        lanes = slice(j * slots, (j + 1) * slots)
        output_ref[j] = (h1_ref[:, lanes] + ffn[:, lanes]).astype(BF16).T


def back_kernel(
    dxo_ref,
    dxp_ref,
    qkv_o,
    qkv_p,
    h0_ref,
    gh1_ref,
    fs_ref,
    gain_ref,
    lnb_ref,
    ig_ref,
    small_ref,
    nb,
    lnacc,
    ge,
    qkvw,
):
    step = pl.program_id(0)
    slots = ig_ref.shape[1]
    width = ig_ref.shape[2]
    half = width // 2
    inv = 1.0 / width

    @pl.when(step == 0)
    def _():
        lnacc[...] = jnp.zeros_like(lnacc)
        ge[...] = jnp.zeros_like(ge)
        nb[...] = lane_columns(gain_ref[0:1, :], slots)
        for h, qkv in enumerate((qkv_o, qkv_p)):
            for c in range(3):
                at = (3 * h + c) * half
                qkvw[:, at : at + half] = qkv[c]

    units = []
    for j in range(PAIR):
        centred, rec = norm_parts(h0_ref[:, j * slots : (j + 1) * slots])
        units.append((centred * rec, rec))
    dxs = jnp.concatenate([dxo_ref[...], dxp_ref[...]], axis=0)
    total = jnp.concatenate([dot_nn(qkvw[0:half, :], dxs), dot_nn(qkvw[half:, :], dxs)], axis=0)
    highs, lows = [], []
    for j in range(PAIR):
        lanes = slice(j * slots, (j + 1) * slots)
        ga = total[:, lanes]
        unit, rec = units[j]
        lnacc[0] += ga * unit
        lnacc[1] += ga
        f = ga * nb[...]
        f_mean = jnp.sum(f, axis=0, keepdims=True) * inv
        fn_mean = jnp.sum(f * unit, axis=0, keepdims=True) * inv
        ig = gh1_ref[:, lanes] + rec * (f - f_mean - unit * fn_mean)
        ig_ref[j] = ig.T
        high = ig.astype(BF16)
        highs.append(high)
        lows.append((ig - high.astype(F32)).astype(BF16))
    fs = fs_ref[...]
    ge[...] += dot_nt(jnp.concatenate(highs, axis=1), fs) + dot_nt(
        jnp.concatenate(lows, axis=1), fs
    )

    @pl.when(step == pl.num_programs(0) - 1)
    def _():
        lane = lax.broadcasted_iota(jnp.int32, (width, slots), 1)
        rows = ge[:, 0:slots] + ge[:, slots:]
        sums = (lnacc[0], lnacc[1], lnb_ref[0], lnb_ref[1])
        for at, part in enumerate(sums):
            rows = jnp.where(lane == IDENT_USED + at, jnp.sum(part, axis=1, keepdims=True), rows)
        rows = jnp.where(lane < IDENT_ROWS, rows, 0.0)
        if small_ref.shape[0] == width:
            small_ref[...] = rows
        else:
            cut = rows.reshape(small_ref.shape[0], 3, 8, slots)
            flat = (small_ref.shape[0] * 8, slots)
            packed = cut[:, 0].reshape(flat)
            packed = packed + pltpu.roll(cut[:, 1].reshape(flat), IDENT_ROWS, 1)
            packed = packed + pltpu.roll(cut[:, 2].reshape(flat), 2 * IDENT_ROWS, 1)
            small_ref[...] = packed.reshape(small_ref.shape)


def square_sum(value, lanes):
    both = value * value
    folded = both[:, 0:lanes]
    for c in range(1, both.shape[1] // lanes):
        folded = folded + both[:, c * lanes : (c + 1) * lanes]
    return jnp.sum(folded, axis=0, keepdims=True)


def gather_kernel(*refs):
    firsts, seconds, got_ref = refs[0:4], refs[4:8], refs[8]
    red1_ref, red2_ref, small_ref, sq_ref = refs[9:]
    lanes = sq_ref.shape[1]
    rows = None
    for refs4, red_ref in ((firsts, red1_ref), (seconds, red2_ref)):
        red = refs4[0][...].astype(F32)
        for ref in refs4[1:]:
            red = red + ref[...].astype(F32)
        red_ref[...] = red
        part = square_sum(red, lanes)
        rows = part if rows is None else rows + part
    small = got_ref[0]
    for o in range(1, got_ref.shape[0]):
        small = small + got_ref[o]
    small_ref[...] = small
    rows = rows + square_sum(small, lanes)
    sq_ref[...] = jnp.full(sq_ref.shape, jnp.sum(rows), F32)


def adam_kernel(*refs):
    sq_ref, red1_ref, red2_ref, small_ref = refs[0:4]
    ins, clip_ref, outs = refs[4:22], refs[22], refs[23:41]
    total = jnp.sum(sq_ref[...], axis=0, keepdims=True)
    clip = jnp.sqrt(total)
    clip_ref[...] = clip
    scale = jnp.max(jnp.minimum(1.0, CLIP_LIMIT / (clip + 1e-06)))
    half = red2_ref.shape[1] // 3
    some = red1_ref.shape[0] // 2
    lanes = small_ref.shape[1]
    small = small_ref[...]
    table = jnp.concatenate(
        [
            small,
            pltpu.roll(small, lanes - IDENT_ROWS, 1),
            pltpu.roll(small, lanes - 2 * IDENT_ROWS, 1),
        ],
        axis=0,
    )
    norm_grad = table.T[IDENT_USED : IDENT_USED + 4]
    matrix = (MATRIX_RATE, MATRIX_DECAY)
    for c in range(3):
        step = adam_step(
            ins[0][c], ins[1][c], ins[2][c], red2_ref[:, c * half : (c + 1) * half], *matrix, scale
        )
        for out, value in zip(outs[0:3], step):
            out[c] = value
    jobs = (
        (red1_ref[some:, 0 : 2 * half], matrix),
        (red1_ref[:, 2 * half :], matrix),
        (red1_ref[0:some, 0 : 2 * half], matrix),
        (norm_grad, (NORM_RATE, 0.0)),
        (table[:, 0:IDENT_USED], (EMBED_RATE, 0.0)),
    )
    for at, (grad, rates) in enumerate(jobs):
        i = 3 * (at + 1)
        step = adam_step(ins[i][...], ins[i + 1][...], ins[i + 2][...], grad, *rates, scale)
        for out, value in zip(outs[i : i + 3], step):
            out[...] = value


def whole_spec(shape):
    zeros = (0,) * len(shape)
    return pl.BlockSpec(shape, lambda i: zeros, pipeline_mode=pl.Buffered(1))


def lead_spec(*rest):
    return pl.BlockSpec((PAIR,) + rest, lambda i: (i,) + (0,) * len(rest))


def column_spec(rows, slots):
    return pl.BlockSpec((rows, PAIR * slots), lambda i: (0, i))


def costs(flops, moved):
    return pl.CostEstimate(flops=flops, bytes_accessed=moved, transcendentals=0)


def embed(tokens, cotangent, token_types, pairs_t, lap_t, embed_weight, norm_params):
    mols, slots, width = tokens.shape
    toks = mols * slots
    rows = (width, width, 256, width)
    types = (F32, BF16, BF16, BF16)
    return pl.pallas_call(
        embed_kernel,
        grid=(mols // PAIR,),
        out_shape=[jax.ShapeDtypeStruct((r, toks), t) for r, t in zip(rows, types)],
        out_specs=[column_spec(r, slots) for r in rows],
        in_specs=[
            lead_spec(slots, width),
            lead_spec(slots, width),
            lead_spec(1, slots),
            lead_spec(2, slots),
            lead_spec(lap_t.shape[1], lap_t.shape[2]),
            whole_spec(embed_weight.shape),
            whole_spec(norm_params.shape),
        ],
        scratch_shapes=[
            pltpu.VMEM((2, width, slots), F32),
            pltpu.VMEM((IDENT_ROWS, width), F32),
            pltpu.VMEM((width, 256), BF16),
        ],
        compiler_params=pltpu.CompilerParams(vmem_limit_bytes=60 * MEGA),
        cost_estimate=costs(8_000_000_000, 10_000_000),
        name="embed",
    )(tokens, cotangent, token_types.reshape(mols, 1, slots), pairs_t, lap_t, embed_weight, norm_params)


def front(lengths, h0, na, cot, norm_params, own, peer, mols):
    width, toks = h0.shape
    slots = toks // mols
    half = width // 2
    heads = width // HEAD_DIM
    owners = 16
    col = column_spec(width, slots)
    weights = []
    for pair in zip(own, peer):
        weights += list(pair)
    gshape = (owners, 2 * half // owners, 3 * half)
    padded = jax.ShapeDtypeStruct((mols, heads * PAD_DIM, slots), BF16)
    outs = [
        (jax.ShapeDtypeStruct((width, toks), F32), col),
        (jax.ShapeDtypeStruct((width, toks), F32), col),
        (jax.ShapeDtypeStruct((width, toks), BF16), col),
        (padded, lead_spec(heads * PAD_DIM, slots)),
        (padded, lead_spec(heads * PAD_DIM, slots)),
        (padded, lead_spec(heads * PAD_DIM, slots)),
        (padded, lead_spec(heads * PAD_DIM, slots)),
        (jax.ShapeDtypeStruct((mols, heads, slots, slots), BF16), lead_spec(heads, slots, slots)),
        (jax.ShapeDtypeStruct(gshape, BF16), whole_spec(gshape)),
        (jax.ShapeDtypeStruct(gshape, BF16), whole_spec(gshape)),
        (jax.ShapeDtypeStruct((2, width, slots), F32), whole_spec((2, width, slots))),
    ]
    return pl.pallas_call(
        front_kernel,
        grid=(mols // PAIR,),
        out_shape=[o[0] for o in outs],
        out_specs=[o[1] for o in outs],
        in_specs=[
            pl.BlockSpec(memory_space=pltpu.SMEM),
            col,
            col,
            whole_spec(cot.shape),
            whole_spec(norm_params.shape),
        ]
        + [whole_spec(w.shape) for w in weights],
        scratch_shapes=[
            pltpu.VMEM((6 * half, width), BF16),
        ]
        + [pltpu.VMEM((width, width), BF16)] * 5
        + [pltpu.VMEM((2, width, slots), F32)]
        + [pltpu.VMEM((width, toks), BF16)] * 5
        + [pltpu.VMEM((PAIR, width, slots), F32)]
        + [pltpu.VMEM((width, PAIR * slots), F32)] * 2
        + [pltpu.VMEM((PAIR, heads // 4 + 1, 8, slots), F32)],
        compiler_params=pltpu.CompilerParams(vmem_limit_bytes=52 * MEGA),
        cost_estimate=costs(60_000_000_000, 50_000_000),
        name="front",
    )(lengths, h0, na, cot, norm_params, *weights)


def middle(which, na, q, k, v, do, e, got=None, plane=None):
    mols, heads, slots, _ = e.shape
    width, toks = na.shape
    half = width // 2
    rows = heads // 2 * PAD_DIM
    part = pl.BlockSpec((PAIR, rows, slots), lambda i: (i, which, 0))
    gshape = (16, width // 16, 3 * half)
    dx = jax.ShapeDtypeStruct((3 * half, toks), BF16)
    specs = [
        column_spec(width, slots),
        part,
        part,
        part,
        part,
        pl.BlockSpec((PAIR, heads // 2, slots, slots), lambda i: (i, which, 0, 0)),
    ]
    scratch = [pltpu.VMEM(na.shape, BF16), pltpu.VMEM(dx.shape, BF16)]
    common = dict(
        grid=(mols // PAIR,),
        compiler_params=pltpu.CompilerParams(vmem_limit_bytes=52 * MEGA),
        cost_estimate=costs(200_000_000, 120_000),
    )
    if got is None:
        return pl.pallas_call(
            middle_kernel,
            out_shape=[dx, jax.ShapeDtypeStruct(gshape, BF16)],
            in_specs=specs,
            out_specs=[column_spec(3 * half, slots), whole_spec(gshape)],
            scratch_shapes=scratch,
            name="middle_peer",
            **common,
        )(na, q, k, v, do, e)
    piece = (4,) + gshape[1:]
    return pl.pallas_call(
        middle_own_kernel,
        out_shape=[dx] + [jax.ShapeDtypeStruct(piece, BF16)] * 4,
        in_specs=[pl.BlockSpec(memory_space=pltpu.SMEM)] + specs + [whole_spec(gshape)],
        out_specs=[column_spec(3 * half, slots)] + [whole_spec(piece)] * 4,
        scratch_shapes=scratch + [pltpu.VMEM(gshape, BF16)],
        name="middle_own",
        **common,
    )(plane, na, q, k, v, do, e, got)


def finish_output(h1, act, down_o, down_p, mols):
    width, toks = h1.shape
    slots = toks // mols
    col = column_spec(width, slots)
    return pl.pallas_call(
        output_kernel,
        grid=(mols // PAIR,),
        out_shape=jax.ShapeDtypeStruct((mols, slots, width), BF16),
        in_specs=[col, col, whole_spec(down_o.shape), whole_spec(down_p.shape)],
        out_specs=lead_spec(slots, width),
        scratch_shapes=[pltpu.VMEM((width, width), BF16)],
        compiler_params=pltpu.CompilerParams(vmem_limit_bytes=48 * MEGA),
        cost_estimate=costs(60_000_000, 70_000),
        name="finish_output",
    )(h1, act, down_o, down_p)


def back(dxo, dxp, qkv_o, qkv_p, h0, gh1, fs, gain, lnb, mols, packed):
    width, toks = h0.shape
    slots = toks // mols
    col = column_spec(width, slots)
    dxs = column_spec(dxo.shape[0], slots)
    small = (width // 24, 8, slots) if packed else (width, slots)
    return pl.pallas_call(
        back_kernel,
        grid=(mols // PAIR,),
        out_shape=[
            jax.ShapeDtypeStruct((mols, slots, width), F32),
            jax.ShapeDtypeStruct(small, F32),
        ],
        in_specs=[
            dxs,
            dxs,
            whole_spec(qkv_o.shape),
            whole_spec(qkv_p.shape),
            col,
            col,
            column_spec(fs.shape[0], slots),
            whole_spec(gain.shape),
            whole_spec(lnb.shape),
        ],
        out_specs=[lead_spec(slots, width), whole_spec(small)],
        scratch_shapes=[
            pltpu.VMEM((width, slots), F32),
            pltpu.VMEM((2, width, slots), F32),
            pltpu.VMEM((width, fs.shape[0]), F32),
            pltpu.VMEM((width, 3 * width), BF16),
        ],
        compiler_params=pltpu.CompilerParams(vmem_limit_bytes=46 * MEGA),
        cost_estimate=costs(18_000_000_000, 15_000_000),
        name="back",
    )(dxo, dxp, qkv_o, qkv_p, h0, gh1, fs, gain, lnb)


def gather(firsts, seconds, got):
    rows, columns = firsts[0].shape
    lanes = got.shape[2]
    return pl.pallas_call(
        gather_kernel,
        out_shape=[
            jax.ShapeDtypeStruct((rows, columns), F32),
            jax.ShapeDtypeStruct((rows, columns), F32),
            jax.ShapeDtypeStruct(got.shape[1:], F32),
            jax.ShapeDtypeStruct((got.shape[0], lanes), F32),
        ],
        compiler_params=pltpu.CompilerParams(vmem_limit_bytes=40 * MEGA),
        name="gather",
    )(*firsts, *seconds, got)


def adam_all(squares, red1, red2, small, state):
    return pl.pallas_call(
        adam_kernel,
        out_shape=[jax.ShapeDtypeStruct((1, squares.shape[1]), F32)]
        + [jax.ShapeDtypeStruct(a.shape, F32) for a in state],
        compiler_params=pltpu.CompilerParams(vmem_limit_bytes=40 * MEGA),
        name="adam",
    )(squares, red1, red2, small, *state)


def swap(value):
    return lax.ppermute(value, "mp", [(0, 1), (1, 0)])


def hop(value, flip):
    size = lax.axis_size("dp")
    return lax.ppermute(value, "dp", [(i, i ^ flip) for i in range(size)])


def take(value, index, axis=0):
    return lax.dynamic_index_in_dim(value, index, axis, keepdims=False)


def line_pieces(own, near, line):
    total = own.astype(F32)
    for piece in near:
        total = total + piece.astype(F32)
    total = total.astype(BF16)
    return take(total, line), [take(total, line ^ k) for k in (1, 2, 3)]


def adam_step(master, mean_old, square_old, gradient, rate, decay, clip_scale):
    clipped = gradient * clip_scale
    mean_new = BETA_FIRST * mean_old + (1.0 - BETA_FIRST) * clipped
    square_new = BETA_SECOND * square_old + (1.0 - BETA_SECOND) * clipped * clipped
    mean_hat = mean_new / (1.0 - BETA_FIRST**STEP)
    square_hat = square_new / (1.0 - BETA_SECOND**STEP)
    updated = master - rate * (mean_hat / (jnp.sqrt(square_hat) + ADAM_EPS) + decay * master)
    return (updated, mean_new, square_new)


def on_device(
    tokens,
    cotangent,
    lengths,
    token_types,
    node_pairs,
    laplacian,
    qkv_weight,
    out_weight,
    up_weight,
    down_weight,
    qkv_master,
    qkv_mean,
    qkv_square,
    out_master,
    out_mean,
    out_square,
    up_master,
    up_mean,
    up_square,
    down_master,
    down_mean,
    down_square,
    norm_params,
    norm_mean,
    norm_square,
    embed_weight,
    embed_mean,
    embed_square,
):
    mols, slots, width = tokens.shape
    half = width // 2
    dp_size = lax.axis_size("dp")
    mp_size = lax.axis_size("mp")
    idents = embed_weight.shape[0]

    own = (qkv_weight.transpose(1, 0, 2), out_weight, up_weight, down_weight)
    peer = tuple(swap(w) for w in own)

    world = dp_size * mp_size
    shard_width = width // world
    fits = dp_size == 16 and shard_width == 24

    h0, na, fs, cot = embed(
        tokens,
        cotangent,
        token_types,
        node_pairs.transpose(0, 2, 1),
        laplacian.transpose(0, 2, 1),
        embed_weight,
        norm_params,
    )
    (gh1, h1, act, q, k, v, do, e, gown1, gpeer1, lnb) = front(
        lengths, h0, na, cot, norm_params, own, peer, mols
    )
    index = lax.axis_index("dp")
    plane, line = (index & 3, index >> 2) if fits else (jnp.int32(0), None)
    got1 = swap(gpeer1)
    dxp, gpeer2 = middle(1, na, q, k, v, do, e)
    got1, dxp = lax.optimization_barrier((got1, dxp))
    sum1 = (gown1.astype(F32) + got1.astype(F32)).astype(BF16)
    got2 = swap(gpeer2)
    if fits:
        grid = sum1.reshape((4, 4) + sum1.shape[1:]).swapaxes(0, 1)
        pieces1 = [take(grid, plane ^ k) for k in range(4)]
        pieces1, do = lax.optimization_barrier((pieces1, do))
        near1 = [hop(piece, k) for piece, k in zip(pieces1[1:], (1, 2, 3))]
    dxo, *pieces = middle(0, na, q, k, v, do, e, got2, plane.reshape(1))
    if fits:
        h1, pieces = lax.optimization_barrier((h1, pieces))
        near = [hop(piece, k) for piece, k in zip(pieces[1:], (1, 2, 3))]
    output = finish_output(h1, act, own[3], peer[3], mols)
    if fits:
        near1, output = lax.optimization_barrier((near1, output))
        own1, sends1 = line_pieces(pieces1[0], near1, line)
        sends1, dxo = lax.optimization_barrier((sends1, dxo))
        far1 = [hop(piece, 4 * k) for piece, k in zip(sends1, (1, 2, 3))]
    input_grad, small = back(
        dxo,
        dxp,
        own[0],
        peer[0],
        h0,
        gh1,
        fs,
        norm_params,
        lnb,
        mols,
        fits,
    )

    shard_index = index * mp_size + lax.axis_index("mp")
    norm_own = lax.dynamic_slice_in_dim(norm_params, shard_index * shard_width, shard_width, 1)
    embed_own = lax.dynamic_slice_in_dim(embed_weight, shard_index * shard_width, shard_width, 1)
    flip = lambda a: a.transpose(1, 0, 2)
    if fits:
        small, far1[1:] = lax.optimization_barrier((small, far1[1:]))
        got = lax.all_to_all(small, ("dp", "mp"), 0, 0, tiled=True)
        own2, sends2 = line_pieces(pieces[0], near, line)
        far2 = [hop(piece, 4 * k) for piece, k in zip(sends2, (1, 2, 3))]
        red1, red2, small_own, squares = gather([own1, *far1], [own2, *far2], got)
        lanes = squares.shape[1]
        squares = lax.all_to_all(squares.reshape(world, 1, lanes), ("dp", "mp"), 0, 0, tiled=True)
        state = (
            (flip(qkv_master), flip(qkv_mean), flip(qkv_square))
            + (out_master, out_mean, out_square)
            + (up_master, up_mean, up_square)
            + (down_master, down_mean, down_square)
            + (norm_own, norm_mean, norm_square)
            + (embed_own.T, embed_mean.T, embed_square.T)
        )
        clip, *new = adam_all(squares.reshape(world, lanes), red1, red2, small_own, state)
        new = [flip(a) for a in new[0:3]] + list(new[3:15]) + [a.T for a in new[15:18]]
        return (output, input_grad, clip[0, 0]) + tuple(new)

    some = half // 16
    scatter = partial(lax.psum_scatter, axis_name="dp", scatter_dimension=0, tiled=True)
    sum1 = sum1.astype(F32)
    sum2 = jnp.stack(pieces, axis=1).astype(F32)
    reduced_down = scatter(sum1[:, 0:some, 0:width].reshape(half, width))
    reduced_out = scatter(sum1[:, some:, 0:width].reshape(half, width))
    reduced_up = scatter(sum1[:, :, width:].reshape(width, half))
    reduced_qkv = scatter(sum2.reshape(width, 3, half))
    small = small[:, : idents + 4].reshape(world, shard_width, idents + 4)
    small_own = jnp.sum(lax.all_to_all(small, ("dp", "mp"), 0, 0, tiled=True), axis=0).T
    reduced = (reduced_qkv, reduced_out, reduced_up, reduced_down, small_own[idents:], small_own[:idents])
    own_square = sum(jnp.sum(piece * piece) for piece in reduced)
    clip_norm = jnp.sqrt(lax.psum(own_square, ("dp", "mp")))
    clip_scale = jnp.minimum(1.0, CLIP_LIMIT / (clip_norm + 1e-06))
    state = (
        (qkv_master, qkv_mean, qkv_square, MATRIX_RATE, MATRIX_DECAY),
        (out_master, out_mean, out_square, MATRIX_RATE, MATRIX_DECAY),
        (up_master, up_mean, up_square, MATRIX_RATE, MATRIX_DECAY),
        (down_master, down_mean, down_square, MATRIX_RATE, MATRIX_DECAY),
        (norm_own, norm_mean, norm_square, NORM_RATE, 0.0),
        (embed_own, embed_mean, embed_square, EMBED_RATE, 0.0),
    )
    new = ()
    for (master, mean, square, rate, decay), grad in zip(state, reduced):
        new += adam_step(master, mean, square, grad, rate, decay, clip_scale)
    return (output, input_grad, clip_norm) + new


def solution(mesh):
    tokens = P(("dp", "mp"), None, None)
    qkv = P("dp", None, "mp")
    rows = P(("mp", "dp"), None)
    both = P("dp", "mp")
    small = P(None, ("dp", "mp"))
    return jax.shard_map(
        on_device,
        mesh=mesh,
        in_specs=(
            tokens,
            tokens,
            P(("dp", "mp")),
            P(("dp", "mp"), None),
            tokens,
            tokens,
            P(None, None, "mp"),
            P("mp", None),
            P(None, "mp"),
            P("mp", None),
        )
        + (qkv,) * 3
        + (rows,) * 3
        + (both,) * 3
        + (rows,) * 3
        + (P(), small, small) * 2,
        out_specs=(tokens, tokens, P())
        + (qkv,) * 3
        + (rows,) * 3
        + (both,) * 3
        + (rows,) * 3
        + (small,) * 6,
        check_vma=False,
    )
```

```python
from functools import partial
import math

import jax
import jax.numpy as jnp
from jax import lax
from jax.experimental import pallas as pl
from jax.experimental.pallas import tpu as pltpu
from jax.sharding import PartitionSpec as P

HEAD_DIM = 24
PAD_DIM = 32
STEP = 10
NORM_EPS = 1e-05
BETA_FIRST = 0.9
BETA_SECOND = 0.95
ADAM_EPS = 1e-08
MATRIX_RATE = 0.03
NORM_RATE = 0.5
EMBED_RATE = 0.05
MATRIX_DECAY = 0.1
CLIP_LIMIT = 1.0
MASK_VALUE = -1e30
SCORE_SCALE = 1.0 / math.sqrt(HEAD_DIM)
LOG2E = 1.4426950408889634
LN2 = 0.6931471805599453
IDENT_ROWS = 40
IDENT_USED = 34
PAIR = 2
MEGA = 1024 * 1024
GATHER_COST = 3000000000
FRONT_UNROLL = 8
MIDDLE_UNROLL = 8

F32 = jnp.float32
BF16 = jnp.bfloat16


def dot_nn(lhs, rhs):
    return lax.dot_general(lhs, rhs, (((1,), (0,)), ((), ())), preferred_element_type=F32)


def dot_nt(lhs, rhs):
    return lax.dot_general(lhs, rhs, (((1,), (1,)), ((), ())), preferred_element_type=F32)


def norm_parts(values):
    scale = 1.0 / values.shape[0]
    centred = values - jnp.sum(values, axis=0, keepdims=True) * scale
    spread = jnp.sum(centred * centred, axis=0, keepdims=True) * scale
    return centred, lax.rsqrt(spread + NORM_EPS)


ROWS = 96


def fold(values):
    return jnp.sum(values.reshape(-1, 8, values.shape[1]), axis=0)


def row_chunks(width):
    return [slice(r, r + ROWS) for r in range(0, width, ROWS)]


def norm_forward(ref, lanes):
    width = ref.shape[0]
    total = None
    for r in row_chunks(width):
        part = fold(ref[r, lanes])
        total = part if total is None else total + part
    mean = jnp.sum(total, axis=0, keepdims=True) * (1.0 / width)
    total = None
    for r in row_chunks(width):
        centred = ref[r, lanes] - mean
        part = fold(centred * centred)
        total = part if total is None else total + part
    spread = jnp.sum(total, axis=0, keepdims=True) * (1.0 / width)
    return mean, lax.rsqrt(spread + NORM_EPS)


def norm_sums(grad_ref, unit_ref, gain_ref, acc_ref, lanes):
    width = grad_ref.shape[0]
    first = second = None
    for r in row_chunks(width):
        grad = grad_ref[r, lanes]
        both = grad * unit_ref[r, lanes]
        acc_ref[0, r, :] += both
        acc_ref[1, r, :] += grad
        gain = gain_ref[r, :]
        one, two = fold(grad * gain), fold(both * gain)
        first = one if first is None else first + one
        second = two if second is None else second + two
    return tuple(jnp.sum(v, axis=0, keepdims=True) * (1.0 / width) for v in (first, second))


def gelu_parts(x):
    size = jnp.abs(x)
    bell = jnp.exp2((-0.5 * LOG2E) * (x * x))
    t = 1.0 / (1.0 + (0.3275911 / math.sqrt(2.0)) * size)
    poly = t * (
        0.5 * 0.254829592
        + t
        * (
            0.5 * -0.284496736
            + t * (0.5 * 1.421413741 + t * (0.5 * -1.453152027 + t * (0.5 * 1.061405429)))
        )
    )
    tail = poly * bell
    share = jnp.where(x < 0.0, tail, 1.0 - tail)
    return x * share, share + x * bell * (1.0 / math.sqrt(2.0 * math.pi))


def head_rows(values, tail):
    heads = values.shape[0] // HEAD_DIM
    cut = values.reshape(heads, HEAD_DIM, values.shape[1])
    tails = jnp.broadcast_to(tail[None], (heads,) + tail.shape)
    return jnp.concatenate([cut, tails], axis=1).reshape(heads * PAD_DIM, values.shape[1])


def block_columns(rows):
    zero = jnp.zeros((PAD_DIM, rows.shape[1]), rows.dtype)
    columns = []
    for head in range(4):
        pieces = [zero] * 4
        pieces[head] = rows[head * PAD_DIM : (head + 1) * PAD_DIM]
        columns.append(jnp.concatenate(pieces, axis=0))
    return jnp.concatenate(columns, axis=1)


def lane_columns(row, slots):
    return jnp.broadcast_to(row, (slots, row.shape[1])).T


def embed_kernel(
    tok_ref,
    cot_ref,
    typ_ref,
    pair_ref,
    lap_ref,
    embed_ref,
    norm_ref,
    h0_ref,
    na_ref,
    fs_ref,
    ct_ref,
    nb,
    rows,
    est,
):
    slots = tok_ref.shape[1]
    width = tok_ref.shape[2]

    @pl.when(pl.program_id(0) == 0)
    def _():
        for row in range(2):
            nb[row] = lane_columns(norm_ref[row : row + 1, :], slots)
        rows[...] = jnp.zeros_like(rows)
        rows[0 : embed_ref.shape[0], :] = embed_ref[...]
        whole = rows[...]
        e1 = whole.astype(BF16).astype(F32)
        e2 = (whole - e1).astype(BF16).astype(F32)
        e3 = whole - e1 - e2
        blank = jnp.zeros((8, width), F32)
        stacked = jnp.concatenate([e1, e2, e3, blank, e1, e2, e1, blank], axis=0)
        est[...] = stacked.T.astype(BF16)

    node_iota = lax.broadcasted_iota(jnp.int32, (lap_ref.shape[2], slots), 0)
    row_iota = lax.broadcasted_iota(jnp.int32, (8, slots), 0)
    for j in range(PAIR):
        lanes = slice(j * slots, (j + 1) * slots)
        lap = lap_ref[j]
        lap1 = lap.astype(BF16)
        rest = lap - lap1.astype(F32)
        lap2 = rest.astype(BF16)
        lap3 = (rest - lap2.astype(F32)).astype(BF16)
        laps = jnp.concatenate([lap1.astype(F32), lap2.astype(F32), lap3.astype(F32)], axis=0)
        laps = laps.astype(BF16)
        left = jnp.where(node_iota == pair_ref[j, 0:1, :], 1.0, 0.0).astype(BF16)
        right = jnp.where(node_iota == pair_ref[j, 1:2, :], 1.0, 0.0).astype(BF16)
        lf = dot_nn(laps, left)
        rf = dot_nn(laps, right)
        types = typ_ref[j]
        kinds = jnp.where((row_iota < 2) & (row_iota == types), 1.0, 0.0)
        none = jnp.zeros((8, slots), F32)
        ident = lap.shape[0]
        f1 = jnp.concatenate([lf[0:ident], rf[0:ident], kinds], axis=0)
        f2 = jnp.concatenate([lf[ident : 2 * ident], rf[ident : 2 * ident], none], axis=0)
        f3 = jnp.concatenate([lf[2 * ident :], rf[2 * ident :], none], axis=0)
        stack = jnp.concatenate([f1, f1, f1, none, f2, f2, f3, none], axis=0).astype(BF16)
        fs_ref[:, lanes] = stack
        h0_ref[:, lanes] = tok_ref[j].T.astype(F32) + dot_nn(est[...], stack)
        mean, rec = norm_forward(h0_ref, lanes)
        for r in row_chunks(width):
            unit = (h0_ref[r, lanes] - mean) * rec
            na_ref[r, lanes] = (unit * nb[0, r, :] + nb[1, r, :]).astype(BF16)
        ct_ref[:, lanes] = cot_ref[j].T


def block_pair(rows):
    zero = jnp.zeros((PAD_DIM, rows.shape[1]), rows.dtype)
    left = jnp.concatenate([rows[0:PAD_DIM], zero], axis=0)
    right = jnp.concatenate([zero, rows[PAD_DIM:]], axis=0)
    return jnp.concatenate([left, right], axis=1)


def staged(at, first, second, third):
    one, two = {}, {}
    count = len(at)
    for n in range(count + 2):
        if n < count:
            one[n] = first(*at[n])
        if 0 <= n - 1 < count:
            two[n - 1] = second(*at[n - 1], one.pop(n - 1))
        if 0 <= n - 2 < count:
            third(*at[n - 2], two.pop(n - 2))


def front_kernel(
    len_ref,
    h0_ref,
    na_ref,
    cot_s,
    norm_ref,
    qkv_o,
    qkv_p,
    out_o,
    out_p,
    up_o,
    up_p,
    down_o,
    down_p,
    gh1_ref,
    h1_s,
    act_ref,
    q_ref,
    k_ref,
    v_ref,
    do_ref,
    e_ref,
    gown_ref,
    gpeer_ref,
    lnacc_ref,
    qkvt,
    outt,
    upt,
    outw,
    upw,
    downw,
    nb,
    act_s,
    nbt_s,
    gp_s,
    mix_s,
    ga_s,
    mixf,
    nrm_s,
    gb_s,
    rec_s,
):
    step = pl.program_id(0)
    steps = pl.num_programs(0)
    slots = e_ref.shape[2]
    width = h0_ref.shape[0]
    half = width // 2
    halves = ((qkv_o, out_o, up_o, down_o), (qkv_p, out_p, up_p, down_p))

    @pl.when(step == 0)
    def _():
        for h, (qkv, out, up, down) in enumerate(halves):
            part = slice(h * half, (h + 1) * half)
            for c in range(3):
                at = (3 * h + c) * half
                qkvt[at : at + half, :] = qkv[c].T
            outt[:, part] = out[...].T
            upt[part, :] = up[...].T
            outw[part, :] = out[...]
            upw[:, part] = up[...]
            downw[part, :] = down[...]
        for row in range(2):
            nb[row] = lane_columns(norm_ref[row + 2 : row + 3, :], slots)
        lnacc_ref[...] = jnp.zeros_like(lnacc_ref)

    base = pl.multiple_of(step * PAIR * slots, PAIR * slots)
    span = pl.ds(base, PAIR * slots)

    phase = pl.when(step >= 0)
    groups = width // (4 * HEAD_DIM)
    parts = tuple(slice(h * half, (h + 1) * half) for h in range(2))
    sides = tuple(slice(j * slots, (j + 1) * slots) for j in range(PAIR))
    columns = tuple(
        pl.ds(pl.multiple_of(base + j * slots, slots), slots) for j in range(PAIR)
    )

    @phase
    def _():
        row_iota = lax.broadcasted_iota(jnp.int32, (8, slots), 0)
        lane_iota = lax.broadcasted_iota(jnp.int32, (1, slots), 1)
        one_row = jnp.where(row_iota == 0, 1.0, 0.0)
        two_rows = jnp.where(row_iota < 2, 1.0, 0.0)
        padded = half // HEAD_DIM * PAD_DIM
        for h in range(2):
            rows = slice(h * padded, (h + 1) * padded)
            for c, ref in enumerate((q_ref, k_ref, v_ref)):
                at = (3 * h + c) * half
                proj = dot_nn(qkvt[at : at + half, :], na_ref[...])
                for j in range(PAIR):
                    own = proj[:, sides[j]]
                    if c == 0:
                        own, tail = own * (SCORE_SCALE * LOG2E), one_row
                    elif c == 1:
                        length = len_ref[step * PAIR + j]
                        bias = jnp.where(lane_iota < length, 0.0, MASK_VALUE)
                        tail = jnp.where(row_iota == 0, bias, 0.0)
                    else:
                        tail = two_rows
                    ref[j, rows, :] = head_rows(own, tail).astype(BF16)

    def score(j, g):
        rows = pl.ds(pl.multiple_of(g * 4 * PAD_DIM, 4 * PAD_DIM), 4 * PAD_DIM)
        return dot_nn(k_ref[j, rows, :].T, block_columns(q_ref[j, rows, :]))

    def weigh(j, g, scores):
        exps = []
        for a in range(4):
            own = scores[:, a * slots : (a + 1) * slots]
            ex = jnp.exp2(own - jnp.max(own, axis=0, keepdims=True)).astype(BF16)
            e_ref[j, g * 4 + a] = ex
            exps.append(ex)
        return exps

    def mix_values(j, g, exps):
        rows = pl.ds(pl.multiple_of(g * 4 * PAD_DIM, 4 * PAD_DIM), 4 * PAD_DIM)
        vals = v_ref[j, rows, :]
        mixes = []
        for a in range(0, 4, 2):
            two = dot_nn(
                vals[a * PAD_DIM : (a + 2) * PAD_DIM], jnp.concatenate(exps[a : a + 2], axis=1)
            )
            for b in range(2):
                got = two[b * PAD_DIM : (b + 1) * PAD_DIM, b * slots : (b + 1) * slots]
                rec = 1.0 / got[HEAD_DIM : HEAD_DIM + 1]
                rec_s[j, g, a + b : a + b + 1, :] = rec
                mixes.append(got[0:HEAD_DIM] * rec)
        out_rows = pl.ds(pl.multiple_of(g * 4 * HEAD_DIM, 4 * HEAD_DIM), 4 * HEAD_DIM)
        mixf[j, out_rows, :] = jnp.concatenate(mixes, axis=0)

    def attend(i, carry):
        at = [i * FRONT_UNROLL + u for u in range(FRONT_UNROLL)]
        at = [(lax.div(n, groups), lax.rem(n, groups)) for n in at]
        staged(at, score, weigh, mix_values)
        return carry

    lax.fori_loop(0, PAIR * groups // FRONT_UNROLL, attend, 0)

    @phase
    def _():
        for j in range(PAIR):
            mix_s[:, columns[j]] = mixf[j].astype(BF16)
        for part in parts:
            h1_s[part, :] = h0_ref[part, :] + dot_nn(outt[part, :], mix_s[:, span])
        for j in range(PAIR):
            mean, rec = norm_forward(h1_s, sides[j])
            rec_s[j, groups, 0:1, :] = rec
            for r in row_chunks(width):
                unit = (h1_s[r, sides[j]] - mean) * rec
                nrm_s[r, sides[j]] = unit
                nbt_s[r, columns[j]] = (unit * nb[0, r, :] + nb[1, r, :]).astype(BF16)

    @phase
    def _():
        for part in parts:
            act, slope = gelu_parts(dot_nn(upt[part, :], nbt_s[:, span]))
            low = act.astype(BF16)
            act_s[part, span] = low
            act_ref[part, :] = low
            back = dot_nn(downw[part, :], cot_s[:, span])
            gp_s[part, span] = (back * slope).astype(BF16)

    @phase
    def _():
        for part in parts:
            gb_s[part, :] = dot_nn(upw[part, :], gp_s[:, span])
        for j in range(PAIR):
            f_mean, fn_mean = norm_sums(gb_s, nrm_s, nb.at[0], lnacc_ref, sides[j])
            rec = rec_s[j, groups, 0:1, :]
            for r in row_chunks(width):
                f = gb_s[r, sides[j]] * nb[0, r, :]
                gh1 = cot_s[r, columns[j]].astype(F32) + rec * (
                    f - f_mean - nrm_s[r, sides[j]] * fn_mean
                )
                gh1_ref[r, sides[j]] = gh1
                ga_s[r, columns[j]] = gh1.astype(BF16)

    @phase
    def _():
        rows8 = lax.broadcasted_iota(jnp.int32, (4, 8, slots), 1)
        for h, part in enumerate(parts):
            gm = dot_nn(outw[part, :], ga_s[:, span])
            for j in range(PAIR):
                for g in range(groups // 2):
                    at = h * (groups // 2) + g
                    grad = gm[g * 96 : (g + 1) * 96, sides[j]].reshape(4, HEAD_DIM, slots)
                    mixed = mixf[j, at * 96 : (at + 1) * 96, :].reshape(4, HEAD_DIM, slots)
                    rec = rec_s[j, at].reshape(8, 1, slots)[0:4]
                    inner = -(jnp.sum(grad * mixed, axis=1, keepdims=True) * rec)
                    high = inner.astype(BF16).astype(F32)
                    low = inner - high
                    tail = jnp.where(rows8 == 0, high, jnp.where(rows8 == 1, low, 0.0))
                    full = jnp.concatenate([grad * rec, tail], axis=1)
                    do_ref[j, at * 128 : (at + 1) * 128, :] = (
                        full.reshape(4 * PAD_DIM, slots).astype(BF16)
                    )

    @pl.when(step == steps - 1)
    def _():
        owners = gown_ref.shape[0]
        some = half // owners
        for h, g_ref in enumerate((gown_ref, gpeer_ref)):
            rows = slice(h * half, (h + 1) * half)
            gdown = dot_nt(act_s[rows, :], cot_s[...])
            gout = dot_nt(mix_s[rows, :], ga_s[...])
            for o in range(owners):
                both = jnp.concatenate(
                    [gdown[o * some : (o + 1) * some], gout[o * some : (o + 1) * some]], axis=0
                )
                g_ref[o, :, 0:width] = both.astype(g_ref.dtype)
            gup = dot_nt(nbt_s[...], gp_s[rows, :])
            g_ref[:, :, width:] = gup.reshape(owners, 2 * some, half).astype(g_ref.dtype)


def middle_kernel(
    na_ref, q_ref, k_ref, v_ref, do_ref, e_ref, dx_ref, g_ref, na_s, dx_s
):
    attention_back(na_ref, q_ref, k_ref, v_ref, do_ref, e_ref, dx_ref, na_s, dx_s)
    half = dx_ref.shape[0] // 3

    @pl.when(pl.program_id(0) == pl.num_programs(0) - 1)
    def _():
        for c in range(3):
            cut = slice(c * half, (c + 1) * half)
            grad = dot_nt(na_s[...], dx_s[cut, :])
            g_ref[:, :, cut] = grad.reshape(g_ref.shape[0:2] + (half,)).astype(BF16)


def middle_own_kernel(
    plane_ref,
    na_ref,
    q_ref,
    k_ref,
    v_ref,
    do_ref,
    e_ref,
    got_ref,
    dx_ref,
    g0,
    g1,
    g2,
    g3,
    na_s,
    dx_s,
    total,
):
    attention_back(na_ref, q_ref, k_ref, v_ref, do_ref, e_ref, dx_ref, na_s, dx_s)
    half = dx_ref.shape[0] // 3

    @pl.when(pl.program_id(0) == pl.num_programs(0) - 1)
    def _():
        for c in range(3):
            cut = slice(c * half, (c + 1) * half)
            grad = dot_nt(na_s[...], dx_s[cut, :]).reshape(total.shape[0:2] + (half,))
            total[:, :, cut] = (grad + got_ref[:, :, cut].astype(F32)).astype(BF16)
        plane = plane_ref[0]
        for k, g_ref in enumerate((g0, g1, g2, g3)):
            for line in range(4):
                g_ref[line] = total[line * 4 + (plane ^ k)]


def attention_back(na_ref, q_ref, k_ref, v_ref, do_ref, e_ref, dx_ref, na_s, dx_s):
    step = pl.program_id(0)
    slots = q_ref.shape[2]
    half = dx_ref.shape[0] // 3
    base = pl.multiple_of(step * PAIR * slots, PAIR * slots)
    groups = half // (4 * HEAD_DIM)

    na_s[:, pl.ds(base, PAIR * slots)] = na_ref[...]

    def rows_of(g):
        return pl.ds(pl.multiple_of(g * 4 * PAD_DIM, 4 * PAD_DIM), 4 * PAD_DIM)

    def score(j, g):
        return dot_nn(v_ref[j, rows_of(g), :].T, block_columns(do_ref[j, rows_of(g), :]))

    def weigh(j, g, back):
        grads = []
        for a in range(4):
            ex = e_ref[j, g * 4 + a].astype(F32)
            grads.append((ex * back[:, a * slots : (a + 1) * slots]).astype(BF16))
        return grads

    def products(j, g, grads):
        dos = do_ref[j, rows_of(g), :]
        qs = q_ref[j, rows_of(g), :]
        ks = k_ref[j, rows_of(g), :]
        dq, dk, dv = [], [], []
        for a in range(0, 4, 2):
            cut = slice(a * PAD_DIM, (a + 2) * PAD_DIM)
            both = jnp.concatenate(grads[a : a + 2], axis=1)
            exps = jnp.concatenate([e_ref[j, g * 4 + a + b].T for b in range(2)], axis=1)
            two = dot_nn(ks[cut], both)
            dq.append(two[0:HEAD_DIM, 0:slots])
            dq.append(two[PAD_DIM : PAD_DIM + HEAD_DIM, slots:])
            two = dot_nt(block_pair(qs[cut]), both)
            dk.append(two[0:HEAD_DIM])
            dk.append(two[PAD_DIM : PAD_DIM + HEAD_DIM])
            two = dot_nn(dos[cut], exps)
            dv.append(two[0:HEAD_DIM, 0:slots])
            dv.append(two[PAD_DIM : PAD_DIM + HEAD_DIM, slots:])
        cols = pl.ds(pl.multiple_of(base + j * slots, slots), slots)
        for c, (parts, scale) in enumerate(((dq, SCORE_SCALE), (dk, LN2), (dv, None))):
            at = pl.ds(pl.multiple_of(c * half + g * 96, 32), 96)
            whole = jnp.concatenate(parts, axis=0)
            if scale is not None:
                whole = whole * scale
            low = whole.astype(BF16)
            dx_s[at, cols] = low
            dx_ref[at, pl.ds(pl.multiple_of(j * slots, slots), slots)] = low

    def attend(i, carry):
        at = [i * MIDDLE_UNROLL + u for u in range(MIDDLE_UNROLL)]
        at = [(lax.div(n, groups), lax.rem(n, groups)) for n in at]
        staged(at, score, weigh, products)
        return carry

    lax.fori_loop(0, PAIR * groups // MIDDLE_UNROLL, attend, 0)


def output_kernel(h1_ref, act_ref, down_o, down_p, output_ref, downt):
    slots = output_ref.shape[1]
    half = down_o.shape[0]

    @pl.when(pl.program_id(0) == 0)
    def _():
        for h, down in enumerate((down_o, down_p)):
            downt[:, h * half : (h + 1) * half] = down[...].T

    ffn = [dot_nn(downt[h * half : (h + 1) * half, :], act_ref[...]) for h in range(2)]
    ffn = jnp.concatenate(ffn, axis=0)
    for j in range(PAIR):
        lanes = slice(j * slots, (j + 1) * slots)
        output_ref[j] = (h1_ref[:, lanes] + ffn[:, lanes]).astype(BF16).T


def back_kernel(
    dxo_ref,
    dxp_ref,
    qkv_o,
    qkv_p,
    h0_ref,
    gh1_ref,
    fs_ref,
    gain_ref,
    lnb_ref,
    ig_ref,
    small_ref,
    nb,
    lnacc,
    ge,
    qkvw,
):
    step = pl.program_id(0)
    slots = ig_ref.shape[1]
    width = ig_ref.shape[2]
    half = width // 2
    inv = 1.0 / width

    @pl.when(step == 0)
    def _():
        lnacc[...] = jnp.zeros_like(lnacc)
        ge[...] = jnp.zeros_like(ge)
        nb[...] = lane_columns(gain_ref[0:1, :], slots)
        for h, qkv in enumerate((qkv_o, qkv_p)):
            for c in range(3):
                at = (3 * h + c) * half
                qkvw[:, at : at + half] = qkv[c]

    units = []
    for j in range(PAIR):
        centred, rec = norm_parts(h0_ref[:, j * slots : (j + 1) * slots])
        units.append((centred * rec, rec))
    dxs = jnp.concatenate([dxo_ref[...], dxp_ref[...]], axis=0)
    total = jnp.concatenate([dot_nn(qkvw[0:half, :], dxs), dot_nn(qkvw[half:, :], dxs)], axis=0)
    highs, lows = [], []
    for j in range(PAIR):
        lanes = slice(j * slots, (j + 1) * slots)
        ga = total[:, lanes]
        unit, rec = units[j]
        lnacc[0] += ga * unit
        lnacc[1] += ga
        f = ga * nb[...]
        f_mean = jnp.sum(f, axis=0, keepdims=True) * inv
        fn_mean = jnp.sum(f * unit, axis=0, keepdims=True) * inv
        ig = gh1_ref[:, lanes] + rec * (f - f_mean - unit * fn_mean)
        ig_ref[j] = ig.T
        high = ig.astype(BF16)
        highs.append(high)
        lows.append((ig - high.astype(F32)).astype(BF16))
    fs = fs_ref[...]
    ge[...] += dot_nt(jnp.concatenate(highs, axis=1), fs) + dot_nt(
        jnp.concatenate(lows, axis=1), fs
    )

    @pl.when(step == pl.num_programs(0) - 1)
    def _():
        lane = lax.broadcasted_iota(jnp.int32, (width, slots), 1)
        rows = ge[:, 0:slots] + ge[:, slots:]
        sums = (lnacc[0], lnacc[1], lnb_ref[0], lnb_ref[1])
        for at, part in enumerate(sums):
            rows = jnp.where(lane == IDENT_USED + at, jnp.sum(part, axis=1, keepdims=True), rows)
        rows = jnp.where(lane < IDENT_ROWS, rows, 0.0)
        if small_ref.shape[0] == width:
            small_ref[...] = rows
        else:
            cut = rows.reshape(small_ref.shape[0], 3, 8, slots)
            flat = (small_ref.shape[0] * 8, slots)
            packed = cut[:, 0].reshape(flat)
            packed = packed + pltpu.roll(cut[:, 1].reshape(flat), IDENT_ROWS, 1)
            packed = packed + pltpu.roll(cut[:, 2].reshape(flat), 2 * IDENT_ROWS, 1)
            small_ref[...] = packed.reshape(small_ref.shape)


def square_sum(value, lanes):
    both = value * value
    folded = both[:, 0:lanes]
    for c in range(1, both.shape[1] // lanes):
        folded = folded + both[:, c * lanes : (c + 1) * lanes]
    return jnp.sum(folded, axis=0, keepdims=True)


def gather_kernel(*refs):
    firsts, seconds = refs[0:4], refs[4:8]
    red1_ref, red2_ref, sq_ref = refs[8:]
    rows = None
    for refs4, red_ref in ((firsts, red1_ref), (seconds, red2_ref)):
        red = refs4[0][...].astype(F32)
        for ref in refs4[1:]:
            red = red + ref[...].astype(F32)
        red_ref[...] = red
        part = square_sum(red, sq_ref.shape[1])
        rows = part if rows is None else rows + part
    sq_ref[...] = rows


def small_kernel(got_ref, rows_ref, small_ref, sq_ref):
    small = got_ref[0]
    for o in range(1, got_ref.shape[0]):
        small = small + got_ref[o]
    small_ref[...] = small
    rows = rows_ref[...] + square_sum(small, sq_ref.shape[1])
    sq_ref[...] = jnp.full(sq_ref.shape, jnp.sum(rows), F32)


def adam_kernel(*refs):
    sq_ref, red1_ref, red2_ref, small_ref = refs[0:4]
    ins, clip_ref, outs = refs[4:22], refs[22], refs[23:41]
    total = jnp.sum(sq_ref[...], axis=0, keepdims=True)
    clip = jnp.sqrt(total)
    clip_ref[...] = clip
    scale = jnp.max(jnp.minimum(1.0, CLIP_LIMIT / (clip + 1e-06)))
    half = red2_ref.shape[1] // 3
    some = red1_ref.shape[0] // 2
    lanes = small_ref.shape[1]
    small = small_ref[...]
    table = jnp.concatenate(
        [
            small,
            pltpu.roll(small, lanes - IDENT_ROWS, 1),
            pltpu.roll(small, lanes - 2 * IDENT_ROWS, 1),
        ],
        axis=0,
    )
    norm_grad = table.T[IDENT_USED : IDENT_USED + 4]
    matrix = (MATRIX_RATE, MATRIX_DECAY)
    for c in range(3):
        step = adam_step(
            ins[0][c], ins[1][c], ins[2][c], red2_ref[:, c * half : (c + 1) * half], *matrix, scale
        )
        for out, value in zip(outs[0:3], step):
            out[c] = value
    jobs = (
        (red1_ref[some:, 0 : 2 * half], matrix),
        (red1_ref[:, 2 * half :], matrix),
        (red1_ref[0:some, 0 : 2 * half], matrix),
        (norm_grad, (NORM_RATE, 0.0)),
        (table[:, 0:IDENT_USED], (EMBED_RATE, 0.0)),
    )
    for at, (grad, rates) in enumerate(jobs):
        i = 3 * (at + 1)
        step = adam_step(ins[i][...], ins[i + 1][...], ins[i + 2][...], grad, *rates, scale)
        for out, value in zip(outs[i : i + 3], step):
            out[...] = value


def whole_spec(shape):
    zeros = (0,) * len(shape)
    return pl.BlockSpec(shape, lambda i: zeros, pipeline_mode=pl.Buffered(1))


def lead_spec(*rest):
    return pl.BlockSpec((PAIR,) + rest, lambda i: (i,) + (0,) * len(rest))


def column_spec(rows, slots):
    return pl.BlockSpec((rows, PAIR * slots), lambda i: (0, i))


def costs(flops, moved):
    return pl.CostEstimate(flops=flops, bytes_accessed=moved, transcendentals=0)


def embed(tokens, cotangent, token_types, pairs_t, lap_t, embed_weight, norm_params):
    mols, slots, width = tokens.shape
    toks = mols * slots
    rows = (width, width, 256, width)
    types = (F32, BF16, BF16, BF16)
    return pl.pallas_call(
        embed_kernel,
        grid=(mols // PAIR,),
        out_shape=[jax.ShapeDtypeStruct((r, toks), t) for r, t in zip(rows, types)],
        out_specs=[column_spec(r, slots) for r in rows],
        in_specs=[
            lead_spec(slots, width),
            lead_spec(slots, width),
            lead_spec(1, slots),
            lead_spec(2, slots),
            lead_spec(lap_t.shape[1], lap_t.shape[2]),
            whole_spec(embed_weight.shape),
            whole_spec(norm_params.shape),
        ],
        scratch_shapes=[
            pltpu.VMEM((2, width, slots), F32),
            pltpu.VMEM((IDENT_ROWS, width), F32),
            pltpu.VMEM((width, 256), BF16),
        ],
        compiler_params=pltpu.CompilerParams(vmem_limit_bytes=60 * MEGA),
        cost_estimate=costs(8_000_000_000, 10_000_000),
        name="embed",
    )(tokens, cotangent, token_types.reshape(mols, 1, slots), pairs_t, lap_t, embed_weight, norm_params)


def front(lengths, h0, na, cot, norm_params, own, peer, mols):
    width, toks = h0.shape
    slots = toks // mols
    half = width // 2
    heads = width // HEAD_DIM
    owners = 16
    col = column_spec(width, slots)
    weights = []
    for pair in zip(own, peer):
        weights += list(pair)
    gshape = (owners, 2 * half // owners, 3 * half)
    padded = jax.ShapeDtypeStruct((mols, heads * PAD_DIM, slots), BF16)
    outs = [
        (jax.ShapeDtypeStruct((width, toks), F32), col),
        (jax.ShapeDtypeStruct((width, toks), F32), col),
        (jax.ShapeDtypeStruct((width, toks), BF16), col),
        (padded, lead_spec(heads * PAD_DIM, slots)),
        (padded, lead_spec(heads * PAD_DIM, slots)),
        (padded, lead_spec(heads * PAD_DIM, slots)),
        (padded, lead_spec(heads * PAD_DIM, slots)),
        (jax.ShapeDtypeStruct((mols, heads, slots, slots), BF16), lead_spec(heads, slots, slots)),
        (jax.ShapeDtypeStruct(gshape, BF16), whole_spec(gshape)),
        (jax.ShapeDtypeStruct(gshape, BF16), whole_spec(gshape)),
        (jax.ShapeDtypeStruct((2, width, slots), F32), whole_spec((2, width, slots))),
    ]
    return pl.pallas_call(
        front_kernel,
        grid=(mols // PAIR,),
        out_shape=[o[0] for o in outs],
        out_specs=[o[1] for o in outs],
        in_specs=[
            pl.BlockSpec(memory_space=pltpu.SMEM),
            col,
            col,
            whole_spec(cot.shape),
            whole_spec(norm_params.shape),
        ]
        + [whole_spec(w.shape) for w in weights],
        scratch_shapes=[
            pltpu.VMEM((6 * half, width), BF16),
        ]
        + [pltpu.VMEM((width, width), BF16)] * 5
        + [pltpu.VMEM((2, width, slots), F32)]
        + [pltpu.VMEM((width, toks), BF16)] * 5
        + [pltpu.VMEM((PAIR, width, slots), F32)]
        + [pltpu.VMEM((width, PAIR * slots), F32)] * 2
        + [pltpu.VMEM((PAIR, heads // 4 + 1, 8, slots), F32)],
        compiler_params=pltpu.CompilerParams(vmem_limit_bytes=52 * MEGA),
        cost_estimate=costs(60_000_000_000, 50_000_000),
        name="front",
    )(lengths, h0, na, cot, norm_params, *weights)


def middle(which, na, q, k, v, do, e, got=None, plane=None):
    mols, heads, slots, _ = e.shape
    width, toks = na.shape
    half = width // 2
    rows = heads // 2 * PAD_DIM
    part = pl.BlockSpec((PAIR, rows, slots), lambda i: (i, which, 0))
    gshape = (16, width // 16, 3 * half)
    dx = jax.ShapeDtypeStruct((3 * half, toks), BF16)
    specs = [
        column_spec(width, slots),
        part,
        part,
        part,
        part,
        pl.BlockSpec((PAIR, heads // 2, slots, slots), lambda i: (i, which, 0, 0)),
    ]
    scratch = [pltpu.VMEM(na.shape, BF16), pltpu.VMEM(dx.shape, BF16)]
    common = dict(
        grid=(mols // PAIR,),
        compiler_params=pltpu.CompilerParams(vmem_limit_bytes=52 * MEGA),
        cost_estimate=costs(200_000_000, 120_000),
    )
    if got is None:
        return pl.pallas_call(
            middle_kernel,
            out_shape=[dx, jax.ShapeDtypeStruct(gshape, BF16)],
            in_specs=specs,
            out_specs=[column_spec(3 * half, slots), whole_spec(gshape)],
            scratch_shapes=scratch,
            name="middle_peer",
            **common,
        )(na, q, k, v, do, e)
    piece = (4,) + gshape[1:]
    return pl.pallas_call(
        middle_own_kernel,
        out_shape=[dx] + [jax.ShapeDtypeStruct(piece, BF16)] * 4,
        in_specs=[pl.BlockSpec(memory_space=pltpu.SMEM)] + specs + [whole_spec(gshape)],
        out_specs=[column_spec(3 * half, slots)] + [whole_spec(piece)] * 4,
        scratch_shapes=scratch + [pltpu.VMEM(gshape, BF16)],
        name="middle_own",
        **common,
    )(plane, na, q, k, v, do, e, got)


def finish_output(h1, act, down_o, down_p, mols):
    width, toks = h1.shape
    slots = toks // mols
    col = column_spec(width, slots)
    return pl.pallas_call(
        output_kernel,
        grid=(mols // PAIR,),
        out_shape=jax.ShapeDtypeStruct((mols, slots, width), BF16),
        in_specs=[col, col, whole_spec(down_o.shape), whole_spec(down_p.shape)],
        out_specs=lead_spec(slots, width),
        scratch_shapes=[pltpu.VMEM((width, width), BF16)],
        compiler_params=pltpu.CompilerParams(vmem_limit_bytes=48 * MEGA),
        cost_estimate=costs(60_000_000, 70_000),
        name="finish_output",
    )(h1, act, down_o, down_p)


def back(dxo, dxp, qkv_o, qkv_p, h0, gh1, fs, gain, lnb, mols, packed):
    width, toks = h0.shape
    slots = toks // mols
    col = column_spec(width, slots)
    dxs = column_spec(dxo.shape[0], slots)
    small = (width // 24, 8, slots) if packed else (width, slots)
    return pl.pallas_call(
        back_kernel,
        grid=(mols // PAIR,),
        out_shape=[
            jax.ShapeDtypeStruct((mols, slots, width), F32),
            jax.ShapeDtypeStruct(small, F32),
        ],
        in_specs=[
            dxs,
            dxs,
            whole_spec(qkv_o.shape),
            whole_spec(qkv_p.shape),
            col,
            col,
            column_spec(fs.shape[0], slots),
            whole_spec(gain.shape),
            whole_spec(lnb.shape),
        ],
        out_specs=[lead_spec(slots, width), whole_spec(small)],
        scratch_shapes=[
            pltpu.VMEM((width, slots), F32),
            pltpu.VMEM((2, width, slots), F32),
            pltpu.VMEM((width, fs.shape[0]), F32),
            pltpu.VMEM((width, 3 * width), BF16),
        ],
        compiler_params=pltpu.CompilerParams(vmem_limit_bytes=46 * MEGA),
        cost_estimate=costs(18_000_000_000, 15_000_000),
        name="back",
    )(dxo, dxp, qkv_o, qkv_p, h0, gh1, fs, gain, lnb)


def gather(firsts, seconds):
    rows, columns = firsts[0].shape
    return pl.pallas_call(
        gather_kernel,
        out_shape=[
            jax.ShapeDtypeStruct((rows, columns), F32),
            jax.ShapeDtypeStruct((rows, columns), F32),
            jax.ShapeDtypeStruct((1, 128), F32),
        ],
        compiler_params=pltpu.CompilerParams(vmem_limit_bytes=40 * MEGA),
        cost_estimate=costs(GATHER_COST, GATHER_COST // 1000),
        name="gather",
    )(*firsts, *seconds)


def gather_small(got, rows):
    return pl.pallas_call(
        small_kernel,
        out_shape=[
            jax.ShapeDtypeStruct(got.shape[1:], F32),
            jax.ShapeDtypeStruct((got.shape[0], got.shape[2]), F32),
        ],
        compiler_params=pltpu.CompilerParams(vmem_limit_bytes=40 * MEGA),
        name="gather_small",
    )(got, rows)


def adam_all(squares, red1, red2, small, state):
    return pl.pallas_call(
        adam_kernel,
        out_shape=[jax.ShapeDtypeStruct((1, squares.shape[1]), F32)]
        + [jax.ShapeDtypeStruct(a.shape, F32) for a in state],
        compiler_params=pltpu.CompilerParams(vmem_limit_bytes=40 * MEGA),
        name="adam",
    )(squares, red1, red2, small, *state)


def swap(value):
    return lax.ppermute(value, "mp", [(0, 1), (1, 0)])


def hop(value, flip):
    size = lax.axis_size("dp")
    return lax.ppermute(value, "dp", [(i, i ^ flip) for i in range(size)])


def take(value, index, axis=0):
    return lax.dynamic_index_in_dim(value, index, axis, keepdims=False)


def line_pieces(own, near, line):
    total = own.astype(F32)
    for piece in near:
        total = total + piece.astype(F32)
    total = total.astype(BF16)
    return take(total, line), [take(total, line ^ k) for k in (1, 2, 3)]


def adam_step(master, mean_old, square_old, gradient, rate, decay, clip_scale):
    clipped = gradient * clip_scale
    mean_new = BETA_FIRST * mean_old + (1.0 - BETA_FIRST) * clipped
    square_new = BETA_SECOND * square_old + (1.0 - BETA_SECOND) * clipped * clipped
    mean_hat = mean_new / (1.0 - BETA_FIRST**STEP)
    square_hat = square_new / (1.0 - BETA_SECOND**STEP)
    updated = master - rate * (mean_hat / (jnp.sqrt(square_hat) + ADAM_EPS) + decay * master)
    return (updated, mean_new, square_new)


def on_device(
    tokens,
    cotangent,
    lengths,
    token_types,
    node_pairs,
    laplacian,
    qkv_weight,
    out_weight,
    up_weight,
    down_weight,
    qkv_master,
    qkv_mean,
    qkv_square,
    out_master,
    out_mean,
    out_square,
    up_master,
    up_mean,
    up_square,
    down_master,
    down_mean,
    down_square,
    norm_params,
    norm_mean,
    norm_square,
    embed_weight,
    embed_mean,
    embed_square,
):
    mols, slots, width = tokens.shape
    half = width // 2
    dp_size = lax.axis_size("dp")
    mp_size = lax.axis_size("mp")
    idents = embed_weight.shape[0]

    own = (qkv_weight.transpose(1, 0, 2), out_weight, up_weight, down_weight)
    peer = tuple(swap(w) for w in own)

    world = dp_size * mp_size
    shard_width = width // world
    fits = dp_size == 16 and shard_width == 24

    h0, na, fs, cot = embed(
        tokens,
        cotangent,
        token_types,
        node_pairs.transpose(0, 2, 1),
        laplacian.transpose(0, 2, 1),
        embed_weight,
        norm_params,
    )
    (gh1, h1, act, q, k, v, do, e, gown1, gpeer1, lnb) = front(
        lengths, h0, na, cot, norm_params, own, peer, mols
    )
    index = lax.axis_index("dp")
    plane, line = (index & 3, index >> 2) if fits else (jnp.int32(0), None)
    got1 = swap(gpeer1)
    dxp, gpeer2 = middle(1, na, q, k, v, do, e)
    got1, dxp = lax.optimization_barrier((got1, dxp))
    sum1 = (gown1.astype(F32) + got1.astype(F32)).astype(BF16)
    got2 = swap(gpeer2)
    if fits:
        grid = sum1.reshape((4, 4) + sum1.shape[1:]).swapaxes(0, 1)
        pieces1 = [take(grid, plane ^ k) for k in range(4)]
        pieces1, do = lax.optimization_barrier((pieces1, do))
        near1 = [hop(piece, k) for piece, k in zip(pieces1[1:], (1, 2, 3))]
    dxo, *pieces = middle(0, na, q, k, v, do, e, got2, plane.reshape(1))
    if fits:
        h1, pieces = lax.optimization_barrier((h1, pieces))
        near = [hop(piece, k) for piece, k in zip(pieces[1:], (1, 2, 3))]
    output = finish_output(h1, act, own[3], peer[3], mols)
    if fits:
        near1, output = lax.optimization_barrier((near1, output))
        own1, sends1 = line_pieces(pieces1[0], near1, line)
        sends1, dxo = lax.optimization_barrier((sends1, dxo))
        far1 = [hop(piece, 4 * k) for piece, k in zip(sends1, (1, 2, 3))]
    input_grad, small = back(
        dxo,
        dxp,
        own[0],
        peer[0],
        h0,
        gh1,
        fs,
        norm_params,
        lnb,
        mols,
        fits,
    )

    shard_index = index * mp_size + lax.axis_index("mp")
    norm_own = lax.dynamic_slice_in_dim(norm_params, shard_index * shard_width, shard_width, 1)
    embed_own = lax.dynamic_slice_in_dim(embed_weight, shard_index * shard_width, shard_width, 1)
    flip = lambda a: a.transpose(1, 0, 2)
    if fits:
        small, far1[1:] = lax.optimization_barrier((small, far1[1:]))
        small, near = lax.optimization_barrier((small, near))
        got = lax.all_to_all(small, ("dp", "mp"), 0, 0, tiled=True)
        own2, sends2 = line_pieces(pieces[0], near, line)
        far2 = [hop(piece, 4 * k) for piece, k in zip(sends2, (1, 2, 3))]
        red1, red2, rows = gather([own1, *far1], [own2, *far2])
        small_own, squares = gather_small(got, rows)
        lanes = squares.shape[1]
        squares = lax.all_to_all(squares.reshape(world, 1, lanes), ("dp", "mp"), 0, 0, tiled=True)
        state = (
            (flip(qkv_master), flip(qkv_mean), flip(qkv_square))
            + (out_master, out_mean, out_square)
            + (up_master, up_mean, up_square)
            + (down_master, down_mean, down_square)
            + (norm_own, norm_mean, norm_square)
            + (embed_own.T, embed_mean.T, embed_square.T)
        )
        clip, *new = adam_all(squares.reshape(world, lanes), red1, red2, small_own, state)
        new = [flip(a) for a in new[0:3]] + list(new[3:15]) + [a.T for a in new[15:18]]
        return (output, input_grad, clip[0, 0]) + tuple(new)

    some = half // 16
    scatter = partial(lax.psum_scatter, axis_name="dp", scatter_dimension=0, tiled=True)
    sum1 = sum1.astype(F32)
    sum2 = jnp.stack(pieces, axis=1).astype(F32)
    reduced_down = scatter(sum1[:, 0:some, 0:width].reshape(half, width))
    reduced_out = scatter(sum1[:, some:, 0:width].reshape(half, width))
    reduced_up = scatter(sum1[:, :, width:].reshape(width, half))
    reduced_qkv = scatter(sum2.reshape(width, 3, half))
    small = small[:, : idents + 4].reshape(world, shard_width, idents + 4)
    small_own = jnp.sum(lax.all_to_all(small, ("dp", "mp"), 0, 0, tiled=True), axis=0).T
    reduced = (reduced_qkv, reduced_out, reduced_up, reduced_down, small_own[idents:], small_own[:idents])
    own_square = sum(jnp.sum(piece * piece) for piece in reduced)
    clip_norm = jnp.sqrt(lax.psum(own_square, ("dp", "mp")))
    clip_scale = jnp.minimum(1.0, CLIP_LIMIT / (clip_norm + 1e-06))
    state = (
        (qkv_master, qkv_mean, qkv_square, MATRIX_RATE, MATRIX_DECAY),
        (out_master, out_mean, out_square, MATRIX_RATE, MATRIX_DECAY),
        (up_master, up_mean, up_square, MATRIX_RATE, MATRIX_DECAY),
        (down_master, down_mean, down_square, MATRIX_RATE, MATRIX_DECAY),
        (norm_own, norm_mean, norm_square, NORM_RATE, 0.0),
        (embed_own, embed_mean, embed_square, EMBED_RATE, 0.0),
    )
    new = ()
    for (master, mean, square, rate, decay), grad in zip(state, reduced):
        new += adam_step(master, mean, square, grad, rate, decay, clip_scale)
    return (output, input_grad, clip_norm) + new


def solution(mesh):
    tokens = P(("dp", "mp"), None, None)
    qkv = P("dp", None, "mp")
    rows = P(("mp", "dp"), None)
    both = P("dp", "mp")
    small = P(None, ("dp", "mp"))
    return jax.shard_map(
        on_device,
        mesh=mesh,
        in_specs=(
            tokens,
            tokens,
            P(("dp", "mp")),
            P(("dp", "mp"), None),
            tokens,
            tokens,
            P(None, None, "mp"),
            P("mp", None),
            P(None, "mp"),
            P("mp", None),
        )
        + (qkv,) * 3
        + (rows,) * 3
        + (both,) * 3
        + (rows,) * 3
        + (P(), small, small) * 2,
        out_specs=(tokens, tokens, P())
        + (qkv,) * 3
        + (rows,) * 3
        + (both,) * 3
        + (rows,) * 3
        + (small,) * 6,
        check_vma=False,
    )
```

```python
from functools import partial
import math

import jax
import jax.numpy as jnp
from jax import lax
from jax.experimental import pallas as pl
from jax.experimental.pallas import tpu as pltpu
from jax.sharding import PartitionSpec as P

HEAD_DIM = 24
PAD_DIM = 32
STEP = 10
NORM_EPS = 1e-05
BETA_FIRST = 0.9
BETA_SECOND = 0.95
ADAM_EPS = 1e-08
MATRIX_RATE = 0.03
NORM_RATE = 0.5
EMBED_RATE = 0.05
MATRIX_DECAY = 0.1
CLIP_LIMIT = 1.0
MASK_VALUE = -1e30
SCORE_SCALE = 1.0 / math.sqrt(HEAD_DIM)
LOG2E = 1.4426950408889634
LN2 = 0.6931471805599453
IDENT_ROWS = 40
IDENT_USED = 34
PAIR = 2
MEGA = 1024 * 1024
GATHER_COST = 3000000000
FRONT_UNROLL = 16
MIDDLE_UNROLL = 8

F32 = jnp.float32
BF16 = jnp.bfloat16


def dot_nn(lhs, rhs):
    return lax.dot_general(lhs, rhs, (((1,), (0,)), ((), ())), preferred_element_type=F32)


def dot_nt(lhs, rhs):
    return lax.dot_general(lhs, rhs, (((1,), (1,)), ((), ())), preferred_element_type=F32)


def norm_parts(values):
    scale = 1.0 / values.shape[0]
    centred = values - jnp.sum(values, axis=0, keepdims=True) * scale
    spread = jnp.sum(centred * centred, axis=0, keepdims=True) * scale
    return centred, lax.rsqrt(spread + NORM_EPS)


ROWS = 96


def fold(values):
    return jnp.sum(values.reshape(-1, 8, values.shape[1]), axis=0)


def row_chunks(width):
    return [slice(r, r + ROWS) for r in range(0, width, ROWS)]


def norm_forward(ref, lanes):
    width = ref.shape[0]
    total = None
    for r in row_chunks(width):
        part = fold(ref[r, lanes])
        total = part if total is None else total + part
    mean = jnp.sum(total, axis=0, keepdims=True) * (1.0 / width)
    total = None
    for r in row_chunks(width):
        centred = ref[r, lanes] - mean
        part = fold(centred * centred)
        total = part if total is None else total + part
    spread = jnp.sum(total, axis=0, keepdims=True) * (1.0 / width)
    return mean, lax.rsqrt(spread + NORM_EPS)


def norm_sums(grad_ref, unit_ref, gain_ref, acc_ref, lanes):
    width = grad_ref.shape[0]
    first = second = None
    for r in row_chunks(width):
        grad = grad_ref[r, lanes]
        both = grad * unit_ref[r, lanes]
        acc_ref[0, r, :] += both
        acc_ref[1, r, :] += grad
        gain = gain_ref[r, :]
        one, two = fold(grad * gain), fold(both * gain)
        first = one if first is None else first + one
        second = two if second is None else second + two
    return tuple(jnp.sum(v, axis=0, keepdims=True) * (1.0 / width) for v in (first, second))


def gelu_parts(x):
    size = jnp.abs(x)
    bell = jnp.exp2((-0.5 * LOG2E) * (x * x))
    t = 1.0 / (1.0 + (0.3275911 / math.sqrt(2.0)) * size)
    poly = t * (
        0.5 * 0.254829592
        + t
        * (
            0.5 * -0.284496736
            + t * (0.5 * 1.421413741 + t * (0.5 * -1.453152027 + t * (0.5 * 1.061405429)))
        )
    )
    tail = poly * bell
    share = jnp.where(x < 0.0, tail, 1.0 - tail)
    return x * share, share + x * bell * (1.0 / math.sqrt(2.0 * math.pi))


def head_rows(values, tail):
    heads = values.shape[0] // HEAD_DIM
    cut = values.reshape(heads, HEAD_DIM, values.shape[1])
    tails = jnp.broadcast_to(tail[None], (heads,) + tail.shape)
    return jnp.concatenate([cut, tails], axis=1).reshape(heads * PAD_DIM, values.shape[1])


def block_columns(rows):
    zero = jnp.zeros((PAD_DIM, rows.shape[1]), rows.dtype)
    columns = []
    for head in range(4):
        pieces = [zero] * 4
        pieces[head] = rows[head * PAD_DIM : (head + 1) * PAD_DIM]
        columns.append(jnp.concatenate(pieces, axis=0))
    return jnp.concatenate(columns, axis=1)


def lane_columns(row, slots):
    return jnp.broadcast_to(row, (slots, row.shape[1])).T


def embed_kernel(
    tok_ref,
    cot_ref,
    typ_ref,
    pair_ref,
    lap_ref,
    embed_ref,
    norm_ref,
    h0_ref,
    na_ref,
    fs_ref,
    ct_ref,
    nb,
    rows,
    est,
):
    slots = tok_ref.shape[1]
    width = tok_ref.shape[2]

    @pl.when(pl.program_id(0) == 0)
    def _():
        for row in range(2):
            nb[row] = lane_columns(norm_ref[row : row + 1, :], slots)
        rows[...] = jnp.zeros_like(rows)
        rows[0 : embed_ref.shape[0], :] = embed_ref[...]
        whole = rows[...]
        e1 = whole.astype(BF16).astype(F32)
        e2 = (whole - e1).astype(BF16).astype(F32)
        e3 = whole - e1 - e2
        blank = jnp.zeros((8, width), F32)
        stacked = jnp.concatenate([e1, e2, e3, blank, e1, e2, e1, blank], axis=0)
        est[...] = stacked.T.astype(BF16)

    node_iota = lax.broadcasted_iota(jnp.int32, (lap_ref.shape[2], slots), 0)
    row_iota = lax.broadcasted_iota(jnp.int32, (8, slots), 0)
    for j in range(PAIR):
        lanes = slice(j * slots, (j + 1) * slots)
        lap = lap_ref[j]
        lap1 = lap.astype(BF16)
        rest = lap - lap1.astype(F32)
        lap2 = rest.astype(BF16)
        lap3 = (rest - lap2.astype(F32)).astype(BF16)
        laps = jnp.concatenate([lap1.astype(F32), lap2.astype(F32), lap3.astype(F32)], axis=0)
        laps = laps.astype(BF16)
        left = jnp.where(node_iota == pair_ref[j, 0:1, :], 1.0, 0.0).astype(BF16)
        right = jnp.where(node_iota == pair_ref[j, 1:2, :], 1.0, 0.0).astype(BF16)
        lf = dot_nn(laps, left)
        rf = dot_nn(laps, right)
        types = typ_ref[j]
        kinds = jnp.where((row_iota < 2) & (row_iota == types), 1.0, 0.0)
        none = jnp.zeros((8, slots), F32)
        ident = lap.shape[0]
        f1 = jnp.concatenate([lf[0:ident], rf[0:ident], kinds], axis=0)
        f2 = jnp.concatenate([lf[ident : 2 * ident], rf[ident : 2 * ident], none], axis=0)
        f3 = jnp.concatenate([lf[2 * ident :], rf[2 * ident :], none], axis=0)
        stack = jnp.concatenate([f1, f1, f1, none, f2, f2, f3, none], axis=0).astype(BF16)
        fs_ref[:, lanes] = stack
        h0_ref[:, lanes] = tok_ref[j].T.astype(F32) + dot_nn(est[...], stack)
        mean, rec = norm_forward(h0_ref, lanes)
        for r in row_chunks(width):
            unit = (h0_ref[r, lanes] - mean) * rec
            na_ref[r, lanes] = (unit * nb[0, r, :] + nb[1, r, :]).astype(BF16)
        ct_ref[:, lanes] = cot_ref[j].T


def block_pair(rows):
    zero = jnp.zeros((PAD_DIM, rows.shape[1]), rows.dtype)
    left = jnp.concatenate([rows[0:PAD_DIM], zero], axis=0)
    right = jnp.concatenate([zero, rows[PAD_DIM:]], axis=0)
    return jnp.concatenate([left, right], axis=1)


def staged(at, first, second, third):
    one, two = {}, {}
    count = len(at)
    for n in range(count + 2):
        if n < count:
            one[n] = first(*at[n])
        if 0 <= n - 1 < count:
            two[n - 1] = second(*at[n - 1], one.pop(n - 1))
        if 0 <= n - 2 < count:
            third(*at[n - 2], two.pop(n - 2))


def front_kernel(
    len_ref,
    h0_ref,
    na_ref,
    cot_s,
    norm_ref,
    qkv_o,
    qkv_p,
    out_o,
    out_p,
    up_o,
    up_p,
    down_o,
    down_p,
    gh1_ref,
    h1_s,
    act_ref,
    q_ref,
    k_ref,
    v_ref,
    do_ref,
    e_ref,
    gown_ref,
    gpeer_ref,
    lnacc_ref,
    qkvt,
    outt,
    upt,
    outw,
    upw,
    downw,
    nb,
    act_s,
    nbt_s,
    gp_s,
    mix_s,
    ga_s,
    mixf,
    nrm_s,
    gb_s,
    rec_s,
):
    step = pl.program_id(0)
    steps = pl.num_programs(0)
    slots = e_ref.shape[2]
    width = h0_ref.shape[0]
    half = width // 2
    halves = ((qkv_o, out_o, up_o, down_o), (qkv_p, out_p, up_p, down_p))

    @pl.when(step == 0)
    def _():
        for h, (qkv, out, up, down) in enumerate(halves):
            part = slice(h * half, (h + 1) * half)
            for c in range(3):
                at = (3 * h + c) * half
                qkvt[at : at + half, :] = qkv[c].T
            outt[:, part] = out[...].T
            upt[part, :] = up[...].T
            outw[part, :] = out[...]
            upw[:, part] = up[...]
            downw[part, :] = down[...]
        for row in range(2):
            nb[row] = lane_columns(norm_ref[row + 2 : row + 3, :], slots)
        lnacc_ref[...] = jnp.zeros_like(lnacc_ref)

    base = pl.multiple_of(step * PAIR * slots, PAIR * slots)
    span = pl.ds(base, PAIR * slots)

    phase = pl.when(step >= 0)
    groups = width // (4 * HEAD_DIM)
    parts = tuple(slice(h * half, (h + 1) * half) for h in range(2))
    sides = tuple(slice(j * slots, (j + 1) * slots) for j in range(PAIR))
    columns = tuple(
        pl.ds(pl.multiple_of(base + j * slots, slots), slots) for j in range(PAIR)
    )

    @phase
    def _():
        row_iota = lax.broadcasted_iota(jnp.int32, (8, slots), 0)
        lane_iota = lax.broadcasted_iota(jnp.int32, (1, slots), 1)
        one_row = jnp.where(row_iota == 0, 1.0, 0.0)
        two_rows = jnp.where(row_iota < 2, 1.0, 0.0)
        padded = half // HEAD_DIM * PAD_DIM
        for h in range(2):
            rows = slice(h * padded, (h + 1) * padded)
            for c, ref in enumerate((q_ref, k_ref, v_ref)):
                at = (3 * h + c) * half
                proj = dot_nn(qkvt[at : at + half, :], na_ref[...])
                for j in range(PAIR):
                    own = proj[:, sides[j]]
                    if c == 0:
                        own, tail = own * (SCORE_SCALE * LOG2E), one_row
                    elif c == 1:
                        length = len_ref[step * PAIR + j]
                        bias = jnp.where(lane_iota < length, 0.0, MASK_VALUE)
                        tail = jnp.where(row_iota == 0, bias, 0.0)
                    else:
                        tail = two_rows
                    ref[j, rows, :] = head_rows(own, tail).astype(BF16)

    def score(j, g):
        rows = pl.ds(pl.multiple_of(g * 4 * PAD_DIM, 4 * PAD_DIM), 4 * PAD_DIM)
        return dot_nn(k_ref[j, rows, :].T, block_columns(q_ref[j, rows, :]))

    def weigh(j, g, scores):
        exps = []
        for a in range(4):
            own = scores[:, a * slots : (a + 1) * slots]
            ex = jnp.exp2(own - jnp.max(own, axis=0, keepdims=True)).astype(BF16)
            e_ref[j, g * 4 + a] = ex
            exps.append(ex)
        return exps

    def mix_values(j, g, exps):
        rows = pl.ds(pl.multiple_of(g * 4 * PAD_DIM, 4 * PAD_DIM), 4 * PAD_DIM)
        vals = v_ref[j, rows, :]
        mixes = []
        for a in range(0, 4, 2):
            two = dot_nn(
                vals[a * PAD_DIM : (a + 2) * PAD_DIM], jnp.concatenate(exps[a : a + 2], axis=1)
            )
            for b in range(2):
                got = two[b * PAD_DIM : (b + 1) * PAD_DIM, b * slots : (b + 1) * slots]
                rec = 1.0 / got[HEAD_DIM : HEAD_DIM + 1]
                rec_s[j, g, a + b : a + b + 1, :] = rec
                mixes.append(got[0:HEAD_DIM] * rec)
        out_rows = pl.ds(pl.multiple_of(g * 4 * HEAD_DIM, 4 * HEAD_DIM), 4 * HEAD_DIM)
        mixf[j, out_rows, :] = jnp.concatenate(mixes, axis=0)

    def attend(i, carry):
        at = [i * FRONT_UNROLL + u for u in range(FRONT_UNROLL)]
        at = [(lax.div(n, groups), lax.rem(n, groups)) for n in at]
        staged(at, score, weigh, mix_values)
        return carry

    lax.fori_loop(0, PAIR * groups // FRONT_UNROLL, attend, 0)

    @phase
    def _():
        for j in range(PAIR):
            mix_s[:, columns[j]] = mixf[j].astype(BF16)
        for part in parts:
            h1_s[part, :] = h0_ref[part, :] + dot_nn(outt[part, :], mix_s[:, span])
        for j in range(PAIR):
            mean, rec = norm_forward(h1_s, sides[j])
            rec_s[j, groups, 0:1, :] = rec
            for r in row_chunks(width):
                unit = (h1_s[r, sides[j]] - mean) * rec
                nrm_s[r, sides[j]] = unit
                nbt_s[r, columns[j]] = (unit * nb[0, r, :] + nb[1, r, :]).astype(BF16)

    @phase
    def _():
        for part in parts:
            act, slope = gelu_parts(dot_nn(upt[part, :], nbt_s[:, span]))
            low = act.astype(BF16)
            act_s[part, span] = low
            act_ref[part, :] = low
            back = dot_nn(downw[part, :], cot_s[:, span])
            gp_s[part, span] = (back * slope).astype(BF16)

    @phase
    def _():
        for part in parts:
            gb_s[part, :] = dot_nn(upw[part, :], gp_s[:, span])
        for j in range(PAIR):
            f_mean, fn_mean = norm_sums(gb_s, nrm_s, nb.at[0], lnacc_ref, sides[j])
            rec = rec_s[j, groups, 0:1, :]
            for r in row_chunks(width):
                f = gb_s[r, sides[j]] * nb[0, r, :]
                gh1 = cot_s[r, columns[j]].astype(F32) + rec * (
                    f - f_mean - nrm_s[r, sides[j]] * fn_mean
                )
                gh1_ref[r, sides[j]] = gh1
                ga_s[r, columns[j]] = gh1.astype(BF16)

    @phase
    def _():
        rows8 = lax.broadcasted_iota(jnp.int32, (4, 8, slots), 1)
        for h, part in enumerate(parts):
            gm = dot_nn(outw[part, :], ga_s[:, span])
            for j in range(PAIR):
                for g in range(groups // 2):
                    at = h * (groups // 2) + g
                    grad = gm[g * 96 : (g + 1) * 96, sides[j]].reshape(4, HEAD_DIM, slots)
                    mixed = mixf[j, at * 96 : (at + 1) * 96, :].reshape(4, HEAD_DIM, slots)
                    rec = rec_s[j, at].reshape(8, 1, slots)[0:4]
                    inner = -(jnp.sum(grad * mixed, axis=1, keepdims=True) * rec)
                    high = inner.astype(BF16).astype(F32)
                    low = inner - high
                    tail = jnp.where(rows8 == 0, high, jnp.where(rows8 == 1, low, 0.0))
                    full = jnp.concatenate([grad * rec, tail], axis=1)
                    do_ref[j, at * 128 : (at + 1) * 128, :] = (
                        full.reshape(4 * PAD_DIM, slots).astype(BF16)
                    )

    @pl.when(step == steps - 1)
    def _():
        owners = gown_ref.shape[0]
        some = half // owners
        for h, g_ref in enumerate((gown_ref, gpeer_ref)):
            rows = slice(h * half, (h + 1) * half)
            gdown = dot_nt(act_s[rows, :], cot_s[...])
            gout = dot_nt(mix_s[rows, :], ga_s[...])
            for o in range(owners):
                both = jnp.concatenate(
                    [gdown[o * some : (o + 1) * some], gout[o * some : (o + 1) * some]], axis=0
                )
                g_ref[o, :, 0:width] = both.astype(g_ref.dtype)
            gup = dot_nt(nbt_s[...], gp_s[rows, :])
            g_ref[:, :, width:] = gup.reshape(owners, 2 * some, half).astype(g_ref.dtype)


def middle_kernel(
    na_ref, q_ref, k_ref, v_ref, do_ref, e_ref, dx_ref, g_ref, na_s, dx_s
):
    attention_back(na_ref, q_ref, k_ref, v_ref, do_ref, e_ref, dx_ref, na_s, dx_s)
    half = dx_ref.shape[0] // 3

    @pl.when(pl.program_id(0) == pl.num_programs(0) - 1)
    def _():
        for c in range(3):
            cut = slice(c * half, (c + 1) * half)
            grad = dot_nt(na_s[...], dx_s[cut, :])
            g_ref[:, :, cut] = grad.reshape(g_ref.shape[0:2] + (half,)).astype(BF16)


def middle_own_kernel(
    plane_ref,
    na_ref,
    q_ref,
    k_ref,
    v_ref,
    do_ref,
    e_ref,
    got_ref,
    dx_ref,
    g0,
    g1,
    g2,
    g3,
    na_s,
    dx_s,
    total,
):
    attention_back(na_ref, q_ref, k_ref, v_ref, do_ref, e_ref, dx_ref, na_s, dx_s)
    half = dx_ref.shape[0] // 3

    @pl.when(pl.program_id(0) == pl.num_programs(0) - 1)
    def _():
        for c in range(3):
            cut = slice(c * half, (c + 1) * half)
            grad = dot_nt(na_s[...], dx_s[cut, :]).reshape(total.shape[0:2] + (half,))
            total[:, :, cut] = (grad + got_ref[:, :, cut].astype(F32)).astype(BF16)
        plane = plane_ref[0]
        for k, g_ref in enumerate((g0, g1, g2, g3)):
            for line in range(4):
                g_ref[line] = total[line * 4 + (plane ^ k)]


def attention_back(na_ref, q_ref, k_ref, v_ref, do_ref, e_ref, dx_ref, na_s, dx_s):
    step = pl.program_id(0)
    slots = q_ref.shape[2]
    half = dx_ref.shape[0] // 3
    base = pl.multiple_of(step * PAIR * slots, PAIR * slots)
    groups = half // (4 * HEAD_DIM)

    na_s[:, pl.ds(base, PAIR * slots)] = na_ref[...]

    def rows_of(g):
        return pl.ds(pl.multiple_of(g * 4 * PAD_DIM, 4 * PAD_DIM), 4 * PAD_DIM)

    def score(j, g):
        return dot_nn(v_ref[j, rows_of(g), :].T, block_columns(do_ref[j, rows_of(g), :]))

    def weigh(j, g, back):
        grads = []
        for a in range(4):
            ex = e_ref[j, g * 4 + a].astype(F32)
            grads.append((ex * back[:, a * slots : (a + 1) * slots]).astype(BF16))
        return grads

    def products(j, g, grads):
        dos = do_ref[j, rows_of(g), :]
        qs = q_ref[j, rows_of(g), :]
        ks = k_ref[j, rows_of(g), :]
        dq, dk, dv = [], [], []
        for a in range(0, 4, 2):
            cut = slice(a * PAD_DIM, (a + 2) * PAD_DIM)
            both = jnp.concatenate(grads[a : a + 2], axis=1)
            exps = jnp.concatenate([e_ref[j, g * 4 + a + b].T for b in range(2)], axis=1)
            two = dot_nn(ks[cut], both)
            dq.append(two[0:HEAD_DIM, 0:slots])
            dq.append(two[PAD_DIM : PAD_DIM + HEAD_DIM, slots:])
            two = dot_nt(block_pair(qs[cut]), both)
            dk.append(two[0:HEAD_DIM])
            dk.append(two[PAD_DIM : PAD_DIM + HEAD_DIM])
            two = dot_nn(dos[cut], exps)
            dv.append(two[0:HEAD_DIM, 0:slots])
            dv.append(two[PAD_DIM : PAD_DIM + HEAD_DIM, slots:])
        cols = pl.ds(pl.multiple_of(base + j * slots, slots), slots)
        for c, (parts, scale) in enumerate(((dq, SCORE_SCALE), (dk, LN2), (dv, None))):
            at = pl.ds(pl.multiple_of(c * half + g * 96, 32), 96)
            whole = jnp.concatenate(parts, axis=0)
            if scale is not None:
                whole = whole * scale
            low = whole.astype(BF16)
            dx_s[at, cols] = low
            dx_ref[at, pl.ds(pl.multiple_of(j * slots, slots), slots)] = low

    def attend(i, carry):
        at = [i * MIDDLE_UNROLL + u for u in range(MIDDLE_UNROLL)]
        at = [(lax.div(n, groups), lax.rem(n, groups)) for n in at]
        staged(at, score, weigh, products)
        return carry

    lax.fori_loop(0, PAIR * groups // MIDDLE_UNROLL, attend, 0)


def output_kernel(h1_ref, act_ref, down_o, down_p, output_ref, downt):
    slots = output_ref.shape[1]
    half = down_o.shape[0]

    @pl.when(pl.program_id(0) == 0)
    def _():
        for h, down in enumerate((down_o, down_p)):
            downt[:, h * half : (h + 1) * half] = down[...].T

    ffn = [dot_nn(downt[h * half : (h + 1) * half, :], act_ref[...]) for h in range(2)]
    ffn = jnp.concatenate(ffn, axis=0)
    for j in range(PAIR):
        lanes = slice(j * slots, (j + 1) * slots)
        output_ref[j] = (h1_ref[:, lanes] + ffn[:, lanes]).astype(BF16).T


def back_kernel(
    dxo_ref,
    dxp_ref,
    qkv_o,
    qkv_p,
    h0_ref,
    gh1_ref,
    fs_ref,
    gain_ref,
    lnb_ref,
    ig_ref,
    small_ref,
    nb,
    lnacc,
    ge,
    qkvw,
):
    step = pl.program_id(0)
    slots = ig_ref.shape[1]
    width = ig_ref.shape[2]
    half = width // 2
    inv = 1.0 / width

    @pl.when(step == 0)
    def _():
        lnacc[...] = jnp.zeros_like(lnacc)
        ge[...] = jnp.zeros_like(ge)
        nb[...] = lane_columns(gain_ref[0:1, :], slots)
        for h, qkv in enumerate((qkv_o, qkv_p)):
            for c in range(3):
                at = (3 * h + c) * half
                qkvw[:, at : at + half] = qkv[c]

    units = []
    for j in range(PAIR):
        centred, rec = norm_parts(h0_ref[:, j * slots : (j + 1) * slots])
        units.append((centred * rec, rec))
    dxs = jnp.concatenate([dxo_ref[...], dxp_ref[...]], axis=0)
    total = jnp.concatenate([dot_nn(qkvw[0:half, :], dxs), dot_nn(qkvw[half:, :], dxs)], axis=0)
    highs, lows = [], []
    for j in range(PAIR):
        lanes = slice(j * slots, (j + 1) * slots)
        ga = total[:, lanes]
        unit, rec = units[j]
        lnacc[0] += ga * unit
        lnacc[1] += ga
        f = ga * nb[...]
        f_mean = jnp.sum(f, axis=0, keepdims=True) * inv
        fn_mean = jnp.sum(f * unit, axis=0, keepdims=True) * inv
        ig = gh1_ref[:, lanes] + rec * (f - f_mean - unit * fn_mean)
        ig_ref[j] = ig.T
        high = ig.astype(BF16)
        highs.append(high)
        lows.append((ig - high.astype(F32)).astype(BF16))
    fs = fs_ref[...]
    ge[...] += dot_nt(jnp.concatenate(highs, axis=1), fs) + dot_nt(
        jnp.concatenate(lows, axis=1), fs
    )

    @pl.when(step == pl.num_programs(0) - 1)
    def _():
        lane = lax.broadcasted_iota(jnp.int32, (width, slots), 1)
        rows = ge[:, 0:slots] + ge[:, slots:]
        sums = (lnacc[0], lnacc[1], lnb_ref[0], lnb_ref[1])
        for at, part in enumerate(sums):
            rows = jnp.where(lane == IDENT_USED + at, jnp.sum(part, axis=1, keepdims=True), rows)
        rows = jnp.where(lane < IDENT_ROWS, rows, 0.0)
        if small_ref.shape[0] == width:
            small_ref[...] = rows
        else:
            cut = rows.reshape(small_ref.shape[0], 3, 8, slots)
            flat = (small_ref.shape[0] * 8, slots)
            packed = cut[:, 0].reshape(flat)
            packed = packed + pltpu.roll(cut[:, 1].reshape(flat), IDENT_ROWS, 1)
            packed = packed + pltpu.roll(cut[:, 2].reshape(flat), 2 * IDENT_ROWS, 1)
            small_ref[...] = packed.reshape(small_ref.shape)


def square_sum(value, lanes):
    both = value * value
    folded = both[:, 0:lanes]
    for c in range(1, both.shape[1] // lanes):
        folded = folded + both[:, c * lanes : (c + 1) * lanes]
    return jnp.sum(folded, axis=0, keepdims=True)


def gather_kernel(*refs):
    firsts, seconds = refs[0:4], refs[4:8]
    red1_ref, red2_ref, sq_ref = refs[8:]
    rows = None
    for refs4, red_ref in ((firsts, red1_ref), (seconds, red2_ref)):
        red = refs4[0][...].astype(F32)
        for ref in refs4[1:]:
            red = red + ref[...].astype(F32)
        red_ref[...] = red
        part = square_sum(red, sq_ref.shape[1])
        rows = part if rows is None else rows + part
    sq_ref[...] = rows


def small_kernel(got_ref, rows_ref, small_ref, sq_ref):
    small = got_ref[0]
    for o in range(1, got_ref.shape[0]):
        small = small + got_ref[o]
    small_ref[...] = small
    rows = rows_ref[...] + square_sum(small, sq_ref.shape[1])
    sq_ref[...] = jnp.full(sq_ref.shape, jnp.sum(rows), F32)


def adam_kernel(*refs):
    sq_ref, red1_ref, red2_ref, small_ref = refs[0:4]
    ins, clip_ref, outs = refs[4:22], refs[22], refs[23:41]
    total = jnp.sum(sq_ref[...], axis=0, keepdims=True)
    clip = jnp.sqrt(total)
    clip_ref[...] = clip
    scale = jnp.max(jnp.minimum(1.0, CLIP_LIMIT / (clip + 1e-06)))
    half = red2_ref.shape[1] // 3
    some = red1_ref.shape[0] // 2
    lanes = small_ref.shape[1]
    small = small_ref[...]
    table = jnp.concatenate(
        [
            small,
            pltpu.roll(small, lanes - IDENT_ROWS, 1),
            pltpu.roll(small, lanes - 2 * IDENT_ROWS, 1),
        ],
        axis=0,
    )
    norm_grad = table.T[IDENT_USED : IDENT_USED + 4]
    matrix = (MATRIX_RATE, MATRIX_DECAY)
    for c in range(3):
        step = adam_step(
            ins[0][c], ins[1][c], ins[2][c], red2_ref[:, c * half : (c + 1) * half], *matrix, scale
        )
        for out, value in zip(outs[0:3], step):
            out[c] = value
    jobs = (
        (red1_ref[some:, 0 : 2 * half], matrix),
        (red1_ref[:, 2 * half :], matrix),
        (red1_ref[0:some, 0 : 2 * half], matrix),
        (norm_grad, (NORM_RATE, 0.0)),
        (table[:, 0:IDENT_USED], (EMBED_RATE, 0.0)),
    )
    for at, (grad, rates) in enumerate(jobs):
        i = 3 * (at + 1)
        step = adam_step(ins[i][...], ins[i + 1][...], ins[i + 2][...], grad, *rates, scale)
        for out, value in zip(outs[i : i + 3], step):
            out[...] = value


def whole_spec(shape):
    zeros = (0,) * len(shape)
    return pl.BlockSpec(shape, lambda i: zeros, pipeline_mode=pl.Buffered(1))


def lead_spec(*rest):
    return pl.BlockSpec((PAIR,) + rest, lambda i: (i,) + (0,) * len(rest))


def column_spec(rows, slots):
    return pl.BlockSpec((rows, PAIR * slots), lambda i: (0, i))


def costs(flops, moved):
    return pl.CostEstimate(flops=flops, bytes_accessed=moved, transcendentals=0)


def embed(tokens, cotangent, token_types, pairs_t, lap_t, embed_weight, norm_params):
    mols, slots, width = tokens.shape
    toks = mols * slots
    rows = (width, width, 256, width)
    types = (F32, BF16, BF16, BF16)
    return pl.pallas_call(
        embed_kernel,
        grid=(mols // PAIR,),
        out_shape=[jax.ShapeDtypeStruct((r, toks), t) for r, t in zip(rows, types)],
        out_specs=[column_spec(r, slots) for r in rows],
        in_specs=[
            lead_spec(slots, width),
            lead_spec(slots, width),
            lead_spec(1, slots),
            lead_spec(2, slots),
            lead_spec(lap_t.shape[1], lap_t.shape[2]),
            whole_spec(embed_weight.shape),
            whole_spec(norm_params.shape),
        ],
        scratch_shapes=[
            pltpu.VMEM((2, width, slots), F32),
            pltpu.VMEM((IDENT_ROWS, width), F32),
            pltpu.VMEM((width, 256), BF16),
        ],
        compiler_params=pltpu.CompilerParams(vmem_limit_bytes=60 * MEGA),
        cost_estimate=costs(8_000_000_000, 10_000_000),
        name="embed",
    )(tokens, cotangent, token_types.reshape(mols, 1, slots), pairs_t, lap_t, embed_weight, norm_params)


def front(lengths, h0, na, cot, norm_params, own, peer, mols):
    width, toks = h0.shape
    slots = toks // mols
    half = width // 2
    heads = width // HEAD_DIM
    owners = 16
    col = column_spec(width, slots)
    weights = []
    for pair in zip(own, peer):
        weights += list(pair)
    gshape = (owners, 2 * half // owners, 3 * half)
    padded = jax.ShapeDtypeStruct((mols, heads * PAD_DIM, slots), BF16)
    outs = [
        (jax.ShapeDtypeStruct((width, toks), F32), col),
        (jax.ShapeDtypeStruct((width, toks), F32), col),
        (jax.ShapeDtypeStruct((width, toks), BF16), col),
        (padded, lead_spec(heads * PAD_DIM, slots)),
        (padded, lead_spec(heads * PAD_DIM, slots)),
        (padded, lead_spec(heads * PAD_DIM, slots)),
        (padded, lead_spec(heads * PAD_DIM, slots)),
        (jax.ShapeDtypeStruct((mols, heads, slots, slots), BF16), lead_spec(heads, slots, slots)),
        (jax.ShapeDtypeStruct(gshape, BF16), whole_spec(gshape)),
        (jax.ShapeDtypeStruct(gshape, BF16), whole_spec(gshape)),
        (jax.ShapeDtypeStruct((2, width, slots), F32), whole_spec((2, width, slots))),
    ]
    return pl.pallas_call(
        front_kernel,
        grid=(mols // PAIR,),
        out_shape=[o[0] for o in outs],
        out_specs=[o[1] for o in outs],
        in_specs=[
            pl.BlockSpec(memory_space=pltpu.SMEM),
            col,
            col,
            whole_spec(cot.shape),
            whole_spec(norm_params.shape),
        ]
        + [whole_spec(w.shape) for w in weights],
        scratch_shapes=[
            pltpu.VMEM((6 * half, width), BF16),
        ]
        + [pltpu.VMEM((width, width), BF16)] * 5
        + [pltpu.VMEM((2, width, slots), F32)]
        + [pltpu.VMEM((width, toks), BF16)] * 5
        + [pltpu.VMEM((PAIR, width, slots), F32)]
        + [pltpu.VMEM((width, PAIR * slots), F32)] * 2
        + [pltpu.VMEM((PAIR, heads // 4 + 1, 8, slots), F32)],
        compiler_params=pltpu.CompilerParams(vmem_limit_bytes=52 * MEGA),
        cost_estimate=costs(60_000_000_000, 50_000_000),
        name="front",
    )(lengths, h0, na, cot, norm_params, *weights)


def middle(which, na, q, k, v, do, e, got=None, plane=None):
    mols, heads, slots, _ = e.shape
    width, toks = na.shape
    half = width // 2
    rows = heads // 2 * PAD_DIM
    part = pl.BlockSpec((PAIR, rows, slots), lambda i: (i, which, 0))
    gshape = (16, width // 16, 3 * half)
    dx = jax.ShapeDtypeStruct((3 * half, toks), BF16)
    specs = [
        column_spec(width, slots),
        part,
        part,
        part,
        part,
        pl.BlockSpec((PAIR, heads // 2, slots, slots), lambda i: (i, which, 0, 0)),
    ]
    scratch = [pltpu.VMEM(na.shape, BF16), pltpu.VMEM(dx.shape, BF16)]
    common = dict(
        grid=(mols // PAIR,),
        compiler_params=pltpu.CompilerParams(vmem_limit_bytes=52 * MEGA),
        cost_estimate=costs(200_000_000, 120_000),
    )
    if got is None:
        return pl.pallas_call(
            middle_kernel,
            out_shape=[dx, jax.ShapeDtypeStruct(gshape, BF16)],
            in_specs=specs,
            out_specs=[column_spec(3 * half, slots), whole_spec(gshape)],
            scratch_shapes=scratch,
            name="middle_peer",
            **common,
        )(na, q, k, v, do, e)
    piece = (4,) + gshape[1:]
    return pl.pallas_call(
        middle_own_kernel,
        out_shape=[dx] + [jax.ShapeDtypeStruct(piece, BF16)] * 4,
        in_specs=[pl.BlockSpec(memory_space=pltpu.SMEM)] + specs + [whole_spec(gshape)],
        out_specs=[column_spec(3 * half, slots)] + [whole_spec(piece)] * 4,
        scratch_shapes=scratch + [pltpu.VMEM(gshape, BF16)],
        name="middle_own",
        **common,
    )(plane, na, q, k, v, do, e, got)


def finish_output(h1, act, down_o, down_p, mols):
    width, toks = h1.shape
    slots = toks // mols
    col = column_spec(width, slots)
    return pl.pallas_call(
        output_kernel,
        grid=(mols // PAIR,),
        out_shape=jax.ShapeDtypeStruct((mols, slots, width), BF16),
        in_specs=[col, col, whole_spec(down_o.shape), whole_spec(down_p.shape)],
        out_specs=lead_spec(slots, width),
        scratch_shapes=[pltpu.VMEM((width, width), BF16)],
        compiler_params=pltpu.CompilerParams(vmem_limit_bytes=48 * MEGA),
        cost_estimate=costs(60_000_000, 70_000),
        name="finish_output",
    )(h1, act, down_o, down_p)


def back(dxo, dxp, qkv_o, qkv_p, h0, gh1, fs, gain, lnb, mols, packed):
    width, toks = h0.shape
    slots = toks // mols
    col = column_spec(width, slots)
    dxs = column_spec(dxo.shape[0], slots)
    small = (width // 24, 8, slots) if packed else (width, slots)
    return pl.pallas_call(
        back_kernel,
        grid=(mols // PAIR,),
        out_shape=[
            jax.ShapeDtypeStruct((mols, slots, width), F32),
            jax.ShapeDtypeStruct(small, F32),
        ],
        in_specs=[
            dxs,
            dxs,
            whole_spec(qkv_o.shape),
            whole_spec(qkv_p.shape),
            col,
            col,
            column_spec(fs.shape[0], slots),
            whole_spec(gain.shape),
            whole_spec(lnb.shape),
        ],
        out_specs=[lead_spec(slots, width), whole_spec(small)],
        scratch_shapes=[
            pltpu.VMEM((width, slots), F32),
            pltpu.VMEM((2, width, slots), F32),
            pltpu.VMEM((width, fs.shape[0]), F32),
            pltpu.VMEM((width, 3 * width), BF16),
        ],
        compiler_params=pltpu.CompilerParams(vmem_limit_bytes=46 * MEGA),
        cost_estimate=costs(18_000_000_000, 15_000_000),
        name="back",
    )(dxo, dxp, qkv_o, qkv_p, h0, gh1, fs, gain, lnb)


def gather(firsts, seconds):
    rows, columns = firsts[0].shape
    return pl.pallas_call(
        gather_kernel,
        out_shape=[
            jax.ShapeDtypeStruct((rows, columns), F32),
            jax.ShapeDtypeStruct((rows, columns), F32),
            jax.ShapeDtypeStruct((1, 128), F32),
        ],
        compiler_params=pltpu.CompilerParams(vmem_limit_bytes=40 * MEGA),
        cost_estimate=costs(GATHER_COST, GATHER_COST // 1000),
        name="gather",
    )(*firsts, *seconds)


def gather_small(got, rows):
    return pl.pallas_call(
        small_kernel,
        out_shape=[
            jax.ShapeDtypeStruct(got.shape[1:], F32),
            jax.ShapeDtypeStruct((got.shape[0], got.shape[2]), F32),
        ],
        compiler_params=pltpu.CompilerParams(vmem_limit_bytes=40 * MEGA),
        name="gather_small",
    )(got, rows)


def adam_all(squares, red1, red2, small, state):
    return pl.pallas_call(
        adam_kernel,
        out_shape=[jax.ShapeDtypeStruct((1, squares.shape[1]), F32)]
        + [jax.ShapeDtypeStruct(a.shape, F32) for a in state],
        compiler_params=pltpu.CompilerParams(vmem_limit_bytes=40 * MEGA),
        name="adam",
    )(squares, red1, red2, small, *state)


def swap(value):
    return lax.ppermute(value, "mp", [(0, 1), (1, 0)])


def hop(value, flip):
    size = lax.axis_size("dp")
    return lax.ppermute(value, "dp", [(i, i ^ flip) for i in range(size)])


def take(value, index, axis=0):
    return lax.dynamic_index_in_dim(value, index, axis, keepdims=False)


def line_pieces(own, near, line):
    total = own.astype(F32)
    for piece in near:
        total = total + piece.astype(F32)
    total = total.astype(BF16)
    return take(total, line), [take(total, line ^ k) for k in (1, 2, 3)]


def adam_step(master, mean_old, square_old, gradient, rate, decay, clip_scale):
    clipped = gradient * clip_scale
    mean_new = BETA_FIRST * mean_old + (1.0 - BETA_FIRST) * clipped
    square_new = BETA_SECOND * square_old + (1.0 - BETA_SECOND) * clipped * clipped
    mean_hat = mean_new / (1.0 - BETA_FIRST**STEP)
    square_hat = square_new / (1.0 - BETA_SECOND**STEP)
    updated = master - rate * (mean_hat / (jnp.sqrt(square_hat) + ADAM_EPS) + decay * master)
    return (updated, mean_new, square_new)


def on_device(
    tokens,
    cotangent,
    lengths,
    token_types,
    node_pairs,
    laplacian,
    qkv_weight,
    out_weight,
    up_weight,
    down_weight,
    qkv_master,
    qkv_mean,
    qkv_square,
    out_master,
    out_mean,
    out_square,
    up_master,
    up_mean,
    up_square,
    down_master,
    down_mean,
    down_square,
    norm_params,
    norm_mean,
    norm_square,
    embed_weight,
    embed_mean,
    embed_square,
):
    mols, slots, width = tokens.shape
    half = width // 2
    dp_size = lax.axis_size("dp")
    mp_size = lax.axis_size("mp")
    idents = embed_weight.shape[0]

    own = (qkv_weight.transpose(1, 0, 2), out_weight, up_weight, down_weight)
    peer = tuple(swap(w) for w in own)

    world = dp_size * mp_size
    shard_width = width // world
    fits = dp_size == 16 and shard_width == 24

    h0, na, fs, cot = embed(
        tokens,
        cotangent,
        token_types,
        node_pairs.transpose(0, 2, 1),
        laplacian.transpose(0, 2, 1),
        embed_weight,
        norm_params,
    )
    (gh1, h1, act, q, k, v, do, e, gown1, gpeer1, lnb) = front(
        lengths, h0, na, cot, norm_params, own, peer, mols
    )
    index = lax.axis_index("dp")
    plane, line = (index & 3, index >> 2) if fits else (jnp.int32(0), None)
    got1 = swap(gpeer1)
    dxp, gpeer2 = middle(1, na, q, k, v, do, e)
    got1, dxp = lax.optimization_barrier((got1, dxp))
    sum1 = (gown1.astype(F32) + got1.astype(F32)).astype(BF16)
    got2 = swap(gpeer2)
    if fits:
        grid = sum1.reshape((4, 4) + sum1.shape[1:]).swapaxes(0, 1)
        pieces1 = [take(grid, plane ^ k) for k in range(4)]
        pieces1, do = lax.optimization_barrier((pieces1, do))
        near1 = [hop(piece, k) for piece, k in zip(pieces1[1:], (1, 2, 3))]
    dxo, *pieces = middle(0, na, q, k, v, do, e, got2, plane.reshape(1))
    if fits:
        h1, pieces = lax.optimization_barrier((h1, pieces))
        near = [hop(piece, k) for piece, k in zip(pieces[1:], (1, 2, 3))]
    output = finish_output(h1, act, own[3], peer[3], mols)
    if fits:
        near1, output = lax.optimization_barrier((near1, output))
        own1, sends1 = line_pieces(pieces1[0], near1, line)
        sends1, dxo = lax.optimization_barrier((sends1, dxo))
        far1 = [hop(piece, 4 * k) for piece, k in zip(sends1, (1, 2, 3))]
    input_grad, small = back(
        dxo,
        dxp,
        own[0],
        peer[0],
        h0,
        gh1,
        fs,
        norm_params,
        lnb,
        mols,
        fits,
    )

    shard_index = index * mp_size + lax.axis_index("mp")
    norm_own = lax.dynamic_slice_in_dim(norm_params, shard_index * shard_width, shard_width, 1)
    embed_own = lax.dynamic_slice_in_dim(embed_weight, shard_index * shard_width, shard_width, 1)
    flip = lambda a: a.transpose(1, 0, 2)
    if fits:
        small, far1[1:] = lax.optimization_barrier((small, far1[1:]))
        small, near = lax.optimization_barrier((small, near))
        got = lax.all_to_all(small, ("dp", "mp"), 0, 0, tiled=True)
        own2, sends2 = line_pieces(pieces[0], near, line)
        far2 = [hop(piece, 4 * k) for piece, k in zip(sends2, (1, 2, 3))]
        red1, red2, rows = gather([own1, *far1], [own2, *far2])
        small_own, squares = gather_small(got, rows)
        lanes = squares.shape[1]
        squares = lax.all_to_all(squares.reshape(world, 1, lanes), ("dp", "mp"), 0, 0, tiled=True)
        state = (
            (flip(qkv_master), flip(qkv_mean), flip(qkv_square))
            + (out_master, out_mean, out_square)
            + (up_master, up_mean, up_square)
            + (down_master, down_mean, down_square)
            + (norm_own, norm_mean, norm_square)
            + (embed_own.T, embed_mean.T, embed_square.T)
        )
        clip, *new = adam_all(squares.reshape(world, lanes), red1, red2, small_own, state)
        new = [flip(a) for a in new[0:3]] + list(new[3:15]) + [a.T for a in new[15:18]]
        return (output, input_grad, clip[0, 0]) + tuple(new)

    some = half // 16
    scatter = partial(lax.psum_scatter, axis_name="dp", scatter_dimension=0, tiled=True)
    sum1 = sum1.astype(F32)
    sum2 = jnp.stack(pieces, axis=1).astype(F32)
    reduced_down = scatter(sum1[:, 0:some, 0:width].reshape(half, width))
    reduced_out = scatter(sum1[:, some:, 0:width].reshape(half, width))
    reduced_up = scatter(sum1[:, :, width:].reshape(width, half))
    reduced_qkv = scatter(sum2.reshape(width, 3, half))
    small = small[:, : idents + 4].reshape(world, shard_width, idents + 4)
    small_own = jnp.sum(lax.all_to_all(small, ("dp", "mp"), 0, 0, tiled=True), axis=0).T
    reduced = (reduced_qkv, reduced_out, reduced_up, reduced_down, small_own[idents:], small_own[:idents])
    own_square = sum(jnp.sum(piece * piece) for piece in reduced)
    clip_norm = jnp.sqrt(lax.psum(own_square, ("dp", "mp")))
    clip_scale = jnp.minimum(1.0, CLIP_LIMIT / (clip_norm + 1e-06))
    state = (
        (qkv_master, qkv_mean, qkv_square, MATRIX_RATE, MATRIX_DECAY),
        (out_master, out_mean, out_square, MATRIX_RATE, MATRIX_DECAY),
        (up_master, up_mean, up_square, MATRIX_RATE, MATRIX_DECAY),
        (down_master, down_mean, down_square, MATRIX_RATE, MATRIX_DECAY),
        (norm_own, norm_mean, norm_square, NORM_RATE, 0.0),
        (embed_own, embed_mean, embed_square, EMBED_RATE, 0.0),
    )
    new = ()
    for (master, mean, square, rate, decay), grad in zip(state, reduced):
        new += adam_step(master, mean, square, grad, rate, decay, clip_scale)
    return (output, input_grad, clip_norm) + new


def solution(mesh):
    tokens = P(("dp", "mp"), None, None)
    qkv = P("dp", None, "mp")
    rows = P(("mp", "dp"), None)
    both = P("dp", "mp")
    small = P(None, ("dp", "mp"))
    return jax.shard_map(
        on_device,
        mesh=mesh,
        in_specs=(
            tokens,
            tokens,
            P(("dp", "mp")),
            P(("dp", "mp"), None),
            tokens,
            tokens,
            P(None, None, "mp"),
            P("mp", None),
            P(None, "mp"),
            P("mp", None),
        )
        + (qkv,) * 3
        + (rows,) * 3
        + (both,) * 3
        + (rows,) * 3
        + (P(), small, small) * 2,
        out_specs=(tokens, tokens, P())
        + (qkv,) * 3
        + (rows,) * 3
        + (both,) * 3
        + (rows,) * 3
        + (small,) * 6,
        check_vma=False,
    )
```
